32 devices in a mesh: seq: 16 (over z, y, x), batch: 2 (over core).
Axes of the slice: x: 2, y: 2, z: 4, core: 2. Of those that a mesh axis runs over, the one named last changes fastest.
Arguments:
- tokens: bfloat16 [2, 2048, 1024], P('batch', 'seq'), may hold values from -6 to 6
- out_grad: bfloat16 [2, 2048, 1024], P('batch', 'seq'), may hold values from -6 to 6
- norm1_gain: float32 [1024], replicated, may hold values from 0.5 to 1.5
- norm1_bias: float32 [1024], replicated, may hold values from -1.75 to 1.75
- value_weight: float32 [1024, 2048], P(('seq', 'batch')), may hold values from -0.1875 to 0.1875
- value_bias: float32 [2048], replicated, may hold values from -1.75 to 1.75
- ema_delta: float32 [1024, 16], replicated, may hold values from -11 to -2
- ema_alpha: float32 [1024, 16], replicated, may hold values from -1 to 2
- ema_beta: float32 [1024, 16], replicated, may hold values from -6 to 6
- ema_gamma: float32 [1024, 16], replicated, may hold values from -6 to 6
- ema_omega: float32 [1024], replicated, may hold values from -3 to 3
- base_weight: float32 [1024, 4224], P(('seq', 'batch')), may hold values from -0.1875 to 0.1875
- base_bias: float32 [4224], replicated, may hold values from -1.75 to 1.75
- shared_gamma: float32 [2, 128], replicated, may hold values from -12 to 12
- query_offset: float32 [128], replicated, may hold values from -6 to 6
- position_bias: float32 [128], replicated, may hold values from -6 to 6
- proj_weight: float32 [2048, 1024], P(('seq', 'batch')), may hold values from -0.5 to 0.5
- proj_bias: float32 [1024], replicated, may hold values from -1.75 to 1.75
- norm2_gain: float32 [1024], replicated, may hold values from 0.5 to 1.5
- norm2_bias: float32 [1024], replicated, may hold values from -1.75 to 1.75
- ffn1_weight: float32 [1024, 4096], P(('seq', 'batch')), may hold values from -0.1875 to 0.1875
- ffn1_bias: float32 [4096], replicated, may hold values from -1.75 to 1.75
- ffn2_weight: float32 [4096, 1024], P(('seq', 'batch')), may hold values from -0.09375 to 0.09375
- ffn2_bias: float32 [1024], replicated, may hold values from -1.75 to 1.75
Outputs:
- block_out: bfloat16 [2, 2048, 1024], P('batch', 'seq')
- tokens_grad: bfloat16 [2, 2048, 1024], P('batch', 'seq')
- dnorm1_gain: float32 [1024], replicated
- dnorm1_bias: float32 [1024], replicated
- dvalue_weight: float32 [1024, 2048], P(('seq', 'batch'))
- dvalue_bias: float32 [2048], replicated
- dema_delta: float32 [1024, 16], replicated
- dema_alpha: float32 [1024, 16], replicated
- dema_beta: float32 [1024, 16], replicated
- dema_gamma: float32 [1024, 16], replicated
- dema_omega: float32 [1024], replicated
- dbase_weight: float32 [1024, 4224], P(('seq', 'batch'))
- dbase_bias: float32 [4224], replicated
- dshared_gamma: float32 [2, 128], replicated
- dquery_offset: float32 [128], replicated
- dposition_bias: float32 [128], replicated
- dproj_weight: float32 [2048, 1024], P(('seq', 'batch'))
- dproj_bias: float32 [1024], replicated
- dnorm2_gain: float32 [1024], replicated
- dnorm2_bias: float32 [1024], replicated
- dffn1_weight: float32 [1024, 4096], P(('seq', 'batch'))
- dffn1_bias: float32 [4096], replicated
- dffn2_weight: float32 [4096, 1024], P(('seq', 'batch'))
- dffn2_bias: float32 [1024], replicated
The draws below stay inside these ranges and needn't reach their ends.
All inputs are finite; a program needn't handle non-finite values.
Results may differ from the reference program's by a relative error of at most 0.02.
Values may be sent and summed in bfloat16 or wider, within the bound.
A program may use at most 320 MiB of HBM per device.

```python
import jax
import jax.numpy as jnp
from jax import lax

D = 1024
ZD = 128
VD = 2048
NDIM = 16
FF = 4096
BLOCK = 128
MXW = 4224
LENGTH = 2048
SEQS = 2


def level_of(own_key, shape, cuts, smallest, high):
    def one(axis_at, shards_of):
        steps = jax.random.uniform(jax.random.fold_in(jax.random.fold_in(own_key, 6), axis_at), (shards_of,), jnp.float32, smallest / len(cuts), high / len(cuts))
        return jnp.repeat(jnp.exp(steps), shape[axis_at] // shards_of).reshape((-1,) + (1,) * (len(shape) - axis_at - 1))

    factor_of = one(*cuts[0])
    for cut in cuts[1:]:
        factor_of = factor_of * one(*cut)
    return factor_of


def noise(stream_key, dims, scale, reach, shards=(), kind=jnp.bfloat16):
    level = level_of(stream_key, dims, shards, -0.22, 0.18) if shards else 1.0
    values = jax.random.normal(stream_key, dims, jnp.float32) * scale * level
    return jnp.minimum(jnp.maximum(values, -reach), reach).astype(kind)


def setup_inputs(seed: int = 0) -> dict:
    streams_of = jax.random.split(jax.random.key(seed), 25)
    tokens = noise(streams_of[0], (SEQS, LENGTH, D), 1.0, 6.0, ((0, 2), (1, 16)))
    out_grad = noise(streams_of[1], (SEQS, LENGTH, D), 1.0, 6.0, ((0, 2), (1, 16)))
    norm1_gain = jnp.clip(1.0 + 0.1 * jax.random.normal(streams_of[2], (D,), jnp.float32), 0.5, 1.5)
    norm1_bias = noise(streams_of[3], (D,), 0.3, 1.75, (), jnp.float32)
    value_weight = noise(streams_of[4], (D, VD), D ** -0.5, 0.1875, ((0, 32),), jnp.float32)
    value_bias = noise(streams_of[5], (VD,), 0.3, 1.75, (), jnp.float32)
    ema_delta = jnp.clip(jax.random.uniform(streams_of[6], (D, NDIM), jnp.float32, -11.0, -2.0), -11.0, -2.0)
    ema_alpha = jnp.clip(jax.random.uniform(streams_of[7], (D, NDIM), jnp.float32, -1.0, 2.0), -1.0, 2.0)
    ema_beta = noise(streams_of[8], (D, NDIM), 1.0, 6.0, (), jnp.float32)
    ema_gamma = noise(streams_of[9], (D, NDIM), 1.0, 6.0, (), jnp.float32)
    ema_omega = noise(streams_of[10], (D,), 0.5, 3.0, (), jnp.float32)
    base_weight = noise(streams_of[11], (D, MXW), D ** -0.5, 0.1875, ((0, 32),), jnp.float32)
    base_bias = noise(streams_of[12], (MXW,), 0.3, 1.75, (), jnp.float32)
    shared_gamma = noise(streams_of[13], (2, ZD), 2.0, 12.0, (), jnp.float32)
    query_offset = noise(streams_of[14], (ZD,), 1.0, 6.0, (), jnp.float32)
    position_bias = noise(streams_of[15], (BLOCK,), 1.0, 6.0, (), jnp.float32)
    proj_weight = noise(streams_of[16], (VD, D), (VD // 16) ** -0.5, 0.5, ((0, 32),), jnp.float32)
    proj_bias = noise(streams_of[17], (D,), 0.3, 1.75, (), jnp.float32)
    norm2_gain = jnp.clip(1.0 + 0.1 * jax.random.normal(streams_of[18], (D,), jnp.float32), 0.5, 1.5)
    norm2_bias = noise(streams_of[19], (D,), 0.3, 1.75, (), jnp.float32)
    ffn1_weight = noise(streams_of[20], (D, FF), D ** -0.5, 0.1875, ((0, 32),), jnp.float32)
    ffn1_bias = noise(streams_of[21], (FF,), 0.3, 1.75, (), jnp.float32)
    ffn2_weight = noise(streams_of[22], (FF, D), FF ** -0.5, 0.09375, ((0, 32),), jnp.float32)
    ffn2_bias = noise(streams_of[23], (D,), 0.3, 1.75, (), jnp.float32)
    return {"tokens": tokens, "out_grad": out_grad, "norm1_gain": norm1_gain, "norm1_bias": norm1_bias, "value_weight": value_weight, "value_bias": value_bias, "ema_delta": ema_delta, "ema_alpha": ema_alpha, "ema_beta": ema_beta, "ema_gamma": ema_gamma, "ema_omega": ema_omega, "base_weight": base_weight, "base_bias": base_bias, "shared_gamma": shared_gamma, "query_offset": query_offset, "position_bias": position_bias, "proj_weight": proj_weight, "proj_bias": proj_bias, "norm2_gain": norm2_gain, "norm2_bias": norm2_bias, "ffn1_weight": ffn1_weight, "ffn1_bias": ffn1_bias, "ffn2_weight": ffn2_weight, "ffn2_bias": ffn2_bias}


precise = lax.Precision.HIGHEST

@jax.custom_vjp
def low(v):
    return lax.optimization_barrier(v.astype(jnp.bfloat16)).astype(jnp.float32)

@jax.custom_vjp
def low_back(v):
    return v

def low_keep(v):
    return (low(v), None)

def low_pass(kept, grad):
    return (grad,)

def back_keep(v):
    return (v, None)

def back_low(kept, grad):
    return (low(grad),)
low.defvjp(low_keep, low_pass)
low_back.defvjp(back_keep, back_low)

def layer_norm(values, norm_gain, norm_bias):
    center = values - lax.optimization_barrier(jnp.mean(values, axis=-1, keepdims=True))
    spread = lax.optimization_barrier(jnp.mean(center * center, axis=-1, keepdims=True))
    return center * lax.rsqrt(spread + 1e-05) * norm_gain + norm_bias

def decay_tables(delta, alpha):
    input_rate = jax.nn.sigmoid(delta)
    damping = jax.nn.sigmoid(alpha)
    return (input_rate, jnp.log1p(-input_rate * damping))

def toeplitz_rows(kern_part):
    chans = kern_part.shape[0]
    block_len = kern_part.shape[1]
    wrapped = jnp.concatenate([kern_part[:, :1], jnp.zeros((chans, block_len), kern_part.dtype), kern_part[:, :0:-1]], axis=1)
    tiled = jnp.tile(wrapped, (1, block_len))[:, :block_len * (2 * block_len - 1)]
    return tiled.reshape(chans, block_len, 2 * block_len - 1)[:, :, :block_len]

def local_conv(normed3, kernel):
    block_len = normed3.shape[1]
    blocks = normed3.shape[2] // 128
    kern_blocks = kernel.reshape(blocks, 128, block_len)
    data_blocks = normed3.reshape(normed3.shape[0], block_len, blocks, 128).transpose(2, 0, 1, 3)

    def one_block(block_pair):
        kern_part, data_part = block_pair
        toeplitz = toeplitz_rows(kern_part)
        return jnp.einsum('dts,bsd->btd', toeplitz, data_part, precision=precise)
    result = lax.map(one_block, (kern_blocks, data_blocks))
    return result.transpose(1, 2, 0, 3).reshape(normed3.shape)

def ema_terms(normed3, delta, alpha, beta, gamma, omega, incoming):
    block_len = normed3.shape[1]
    input_rate, log_decay = decay_tables(delta, alpha)
    step_index = jnp.arange(block_len, dtype=jnp.float32)
    ema_scale = NDIM ** (-0.5)
    powers = jnp.exp(log_decay[:, :, None] * step_index)
    kernel = ema_scale * jnp.einsum('dj,djk->dk', gamma * input_rate * beta, powers, precision=precise)
    convolved = local_conv(normed3, kernel)
    carry_table = ema_scale * gamma[:, :, None] * jnp.exp(log_decay[:, :, None] * (step_index + 1.0))
    carried = jnp.einsum('djt,bdj->btd', carry_table, incoming, precision=precise)
    return convolved + carried + omega * normed3

def ema_ends(normed3, delta, alpha, beta):
    block_len = normed3.shape[1]
    input_rate, log_decay = decay_tables(delta, alpha)
    step_index = jnp.arange(block_len, dtype=jnp.float32)
    end_table = (input_rate * beta)[:, :, None] * jnp.exp(log_decay[:, :, None] * (block_len - 1.0 - step_index))
    end_states = jnp.einsum('djs,bsd->bdj', end_table, normed3, precision=precise)
    return (jnp.exp(log_decay * block_len), end_states)

def rel_table(position_bias):
    step_index = jnp.arange(position_bias.shape[0])
    offsets = step_index[:, None] - step_index[None, :]
    return jnp.where(offsets >= 0, position_bias[jnp.maximum(offsets, 0)], 0.0)

def masked_softmax(scores):
    step_index = jnp.arange(scores.shape[-1])
    causal = step_index[:, None] >= step_index[None, :]
    masked = jnp.where(causal, scores, -jnp.inf)
    row_top = lax.optimization_barrier(jnp.max(masked, axis=-1, keepdims=True))
    expo_vals = jnp.exp(masked - row_top)
    return expo_vals / lax.optimization_barrier(jnp.sum(expo_vals, axis=-1, keepdims=True))

def layer(tokens, params):
    norm1_gain, norm1_bias, value_weight, value_bias, ema_delta, ema_alpha, ema_beta, ema_gamma, ema_omega, base_weight, base_bias, shared_gamma, query_offset, position_bias, proj_weight, proj_bias, norm2_gain, norm2_bias, ffn1_weight, ffn1_bias, ffn2_weight, ffn2_bias = params
    length = tokens.shape[0]
    normed = layer_norm(tokens, norm1_gain, norm1_bias)
    normed_low = low(normed)
    value_pre = low_back(jnp.dot(normed_low, low(value_weight), precision=precise) + value_bias)
    value_low = low(jax.nn.silu(value_pre))
    normed3 = normed.reshape(-1, BLOCK, D)
    whole_decay, end_states = ema_ends(normed3, ema_delta, ema_alpha, ema_beta)

    def advance(state, end_state):
        return (whole_decay * state + end_state, state)
    _, incoming = lax.scan(advance, jnp.zeros((D, NDIM), jnp.float32), end_states)
    ema_out = ema_terms(normed3, ema_delta, ema_alpha, ema_beta, ema_gamma, ema_omega, incoming).reshape(length, D)
    mixed_low = low(jax.nn.silu(ema_out))
    base_pre = low_back(jnp.dot(mixed_low, low(base_weight), precision=precise) + base_bias)
    update = jax.nn.sigmoid(base_pre[:, :D])
    shared_reset = jax.nn.silu(base_pre[:, D:D + ZD + VD])
    shared = shared_reset[:, :ZD]
    reset_gate = shared_reset[:, ZD:]
    hidden_x = base_pre[:, D + ZD + VD:]
    queries = low(shared * shared_gamma[0] + query_offset).reshape(-1, BLOCK, ZD)
    key_rows = low(shared * shared_gamma[1]).reshape(-1, BLOCK, ZD)
    scores = low_back(jnp.einsum('bik,bjk->bij', queries, key_rows, precision=precise) * ZD ** (-0.5) + rel_table(position_bias))
    attn = masked_softmax(scores)
    attended = low_back(jnp.einsum('bij,bjv->biv', low(attn), value_low.reshape(-1, BLOCK, VD), precision=precise)).reshape(length, VD)
    gated_low = low(attended * reset_gate)
    proj_pre = low_back(jnp.dot(gated_low, low(proj_weight), precision=precise) + proj_bias)
    hidden = jax.nn.silu(hidden_x + proj_pre)
    first_out = tokens + update * (hidden - tokens)
    normed_two = layer_norm(first_out, norm2_gain, norm2_bias)
    ffn_pre = low_back(jnp.dot(low(normed_two), low(ffn1_weight), precision=precise) + ffn1_bias)
    ffn_out = low_back(jnp.dot(low(jax.nn.silu(ffn_pre)), low(ffn2_weight), precision=precise) + ffn2_bias)
    return first_out + ffn_out

def reference(tokens, out_grad, norm1_gain, norm1_bias, value_weight, value_bias, ema_delta, ema_alpha, ema_beta, ema_gamma, ema_omega, base_weight, base_bias, shared_gamma, query_offset, position_bias, proj_weight, proj_bias, norm2_gain, norm2_bias, ffn1_weight, ffn1_bias, ffn2_weight, ffn2_bias):
    params = (norm1_gain, norm1_bias, value_weight, value_bias, ema_delta, ema_alpha, ema_beta, ema_gamma, ema_omega, base_weight, base_bias, shared_gamma, query_offset, position_bias, proj_weight, proj_bias, norm2_gain, norm2_bias, ffn1_weight, ffn1_bias, ffn2_weight, ffn2_bias)

    def one_sequence(totals, seq_pair):
        seq_tokens, seq_grad = seq_pair
        result, pullback = jax.vjp(layer, seq_tokens.astype(jnp.float32), params)
        token_grad, param_grads = pullback(seq_grad.astype(jnp.float32))
        totals = jax.tree.map(lambda left_val, right_val: left_val + right_val, totals, param_grads)
        return (totals, (result.astype(jnp.bfloat16), token_grad.astype(jnp.bfloat16)))
    zero_grads = jax.tree.map(jnp.zeros_like, params)
    totals, (outputs, token_grads) = lax.scan(one_sequence, zero_grads, (tokens, out_grad))
    return (outputs, token_grads, totals[0], totals[1], totals[2], totals[3], totals[4], totals[5], totals[6], totals[7], totals[8], totals[9], totals[10], totals[11], totals[12], totals[13], totals[14], totals[15], totals[16], totals[17], totals[18], totals[19], totals[20], totals[21])
```

```python
import functools

import jax
import jax.numpy as jnp
from jax import lax
from jax.experimental import pallas as pl
from jax.experimental.pallas import tpu as pltpu
from jax.sharding import PartitionSpec as P

D = 1024
ZD = 128
VD = 2048
NDIM = 16


precise = lax.Precision.HIGHEST


def entering(part, axis, combine, identity):
    place = lax.axis_index(axis)
    gathered = jax.tree.map(lambda a: lax.all_gather(a, axis), part)
    state = jax.tree.map(lambda a, e: jnp.zeros_like(a) + jnp.asarray(e, a.dtype), part, identity)

    def one(step, state):
        return combine(
            state, jax.tree.map(lambda a: lax.dynamic_index_in_dim(a, step, 0, False), gathered)
        )

    return lax.fori_loop(0, place, one, state)


def prefix_2(value, axis, combine, identity):
    size, index = (lax.axis_size(axis), lax.axis_index(axis))
    everything = jax.tree.map(
        lambda part, kind: lax.all_gather(part.astype(kind), axis),
        value,
        jax.tree.map(lambda a: jnp.bfloat16 if a.dtype == jnp.float32 else a.dtype, value),
    )
    start = jax.tree.map(
        lambda part, zero: jnp.broadcast_to(jnp.asarray(zero, part.dtype), part.shape),
        value,
        identity,
    )

    def step(k, before):
        at = size - 1 - k
        reached = at > index
        new = combine(
            before, jax.tree.map(lambda part, own: part[at].astype(own.dtype), everything, value)
        )
        return jax.tree.map(lambda a, b: jnp.where(reached, a, b), new, before)

    return lax.fori_loop(0, size, step, start)


def layer_norm(values, norm_gain, norm_bias):
    center = values - jnp.mean(values, axis=-1, keepdims=True)
    spread = jnp.mean(center * center, axis=-1, keepdims=True)
    return center * lax.rsqrt(spread + 1e-05) * norm_gain + norm_bias


def decay_tables(delta, alpha):
    input_rate = jax.nn.sigmoid(delta)
    damping = jax.nn.sigmoid(alpha)
    return (input_rate, jnp.log1p(-input_rate * damping))


def toeplitz_rows(kern_part):
    chans = kern_part.shape[0]
    block_len = kern_part.shape[1]
    wrapped = jnp.concatenate(
        [kern_part[:, :1], jnp.zeros((chans, block_len), kern_part.dtype), kern_part[:, :0:-1]],
        axis=1,
    )
    tiled = jnp.tile(wrapped, (1, block_len))[:, : block_len * (2 * block_len - 1)]
    return tiled.reshape(chans, block_len, 2 * block_len - 1)[:, :, :block_len]


def local_conv(normed3, kernel):
    block_len = normed3.shape[1]
    blocks = normed3.shape[2] // 128
    kern_blocks = kernel.reshape(blocks, 128, block_len)
    data_blocks = normed3.reshape(normed3.shape[0], block_len, blocks, 128).transpose(2, 0, 1, 3)

    def one_block(block_pair):
        kern_part, data_part = block_pair
        toeplitz = toeplitz_rows(kern_part)
        return jnp.einsum("dts,bsd->btd", toeplitz, data_part, precision=precise)

    result = lax.map(one_block, (kern_blocks, data_blocks))
    return result.transpose(1, 2, 0, 3).reshape(normed3.shape)


def ema_terms(normed3, delta, alpha, beta, gamma, omega, incoming):
    block_len = normed3.shape[1]
    input_rate, log_decay = decay_tables(delta, alpha)
    step_index = jnp.arange(block_len, dtype=jnp.float32)
    ema_scale = NDIM ** (-0.5)
    powers = jnp.exp(log_decay[:, :, None] * step_index)
    kernel = ema_scale * jnp.einsum(
        "dj,djk->dk", gamma * input_rate * beta, powers, precision=precise
    )
    convolved = local_conv(normed3, kernel)
    carry_table = (
        ema_scale * gamma[:, :, None] * jnp.exp(log_decay[:, :, None] * (step_index + 1.0))
    )
    carried = jnp.einsum("djt,bdj->btd", carry_table, incoming, precision=precise)
    return convolved + carried + omega * normed3


def ema_ends(normed3, delta, alpha, beta):
    block_len = normed3.shape[1]
    input_rate, log_decay = decay_tables(delta, alpha)
    step_index = jnp.arange(block_len, dtype=jnp.float32)
    end_table = (input_rate * beta)[:, :, None] * jnp.exp(
        log_decay[:, :, None] * (block_len - 1.0 - step_index)
    )
    end_states = jnp.einsum("djs,bsd->bdj", end_table, normed3, precision=precise)
    return (jnp.exp(log_decay * block_len), end_states)


def rel_table(position_bias):
    step_index = jnp.arange(position_bias.shape[0])
    offsets = step_index[:, None] - step_index[None, :]
    return jnp.where(offsets >= 0, position_bias[jnp.maximum(offsets, 0)], 0.0)


def masked_softmax(scores):
    step_index = jnp.arange(scores.shape[-1])
    causal = step_index[:, None] >= step_index[None, :]
    masked = jnp.where(causal, scores, -jnp.inf)
    row_top = jnp.max(masked, axis=-1, keepdims=True)
    expo_vals = jnp.exp(masked - row_top)
    return expo_vals / jnp.sum(expo_vals, axis=-1, keepdims=True)


def silu_slope(values):
    logistic = jax.nn.sigmoid(values)
    return logistic * (1.0 + values * (1.0 - logistic))


def matmul(left_mat, right_mat):
    return jnp.dot(left_mat, right_mat, preferred_element_type=jnp.float32)


def left_product(left_mat, right_mat):
    return lax.dot_general(
        left_mat, right_mat, (((0,), (0,)), ((), ())), preferred_element_type=jnp.float32
    )


def right_product(left_mat, right_mat):
    return lax.dot_general(
        left_mat, right_mat, (((1,), (1,)), ((), ())), preferred_element_type=jnp.float32
    )


def column_sums(values):
    return jnp.sum(values.astype(jnp.float32), axis=0)


def shards(
    tokens,
    out_grad,
    norm1_gain,
    norm1_bias,
    value_weight,
    value_bias,
    ema_delta,
    ema_alpha,
    ema_beta,
    ema_gamma,
    ema_omega,
    base_weight,
    base_bias,
    shared_gamma,
    query_offset,
    position_bias,
    proj_weight,
    proj_bias,
    norm2_gain,
    norm2_bias,
    ffn1_weight,
    ffn1_bias,
    ffn2_weight,
    ffn2_bias,
):
    seq_local, block_len, _ = tokens.shape
    row_count = seq_local * block_len
    gathered = (
        lax.all_gather(value_weight.astype(jnp.bfloat16), ("seq", "batch"), axis=0, tiled=True),
        lax.all_gather(base_weight.astype(jnp.bfloat16), ("seq", "batch"), axis=0, tiled=True),
        lax.all_gather(proj_weight.astype(jnp.bfloat16), ("seq", "batch"), axis=0, tiled=True),
        lax.all_gather(ffn1_weight.astype(jnp.bfloat16), ("seq", "batch"), axis=0, tiled=True),
        lax.all_gather(ffn2_weight.astype(jnp.bfloat16), ("seq", "batch"), axis=0, tiled=True),
    )
    value_full, base_full, proj_full, ffn1_full, ffn2_full = gathered
    _, log_decay = decay_tables(ema_delta, ema_alpha)
    block_log = log_decay * block_len

    def chain_step(earlier_pair, later_pair):
        carried = earlier_pair[1] * jnp.exp(block_log * later_pair[0][0])
        return (earlier_pair[0] + later_pair[0], carried + later_pair[1])

    one_block = jnp.ones((1,), jnp.float32)
    no_block = jnp.zeros((1,), jnp.float32)
    tokens_flat = tokens.astype(jnp.float32).reshape(row_count, D)
    normed, norm1_back = jax.vjp(layer_norm, tokens_flat, norm1_gain, norm1_bias)
    normed_low = normed.astype(jnp.bfloat16)
    value_pre = matmul(normed_low, value_full) + value_bias
    value_low = jax.nn.silu(value_pre).astype(jnp.bfloat16)
    normed3 = normed.reshape(seq_local, block_len, D)
    (whole_decay, end_states), ends_back = jax.vjp(
        ema_ends, normed3, ema_delta, ema_alpha, ema_beta
    )
    prefix = entering(
        (one_block, end_states), "seq", chain_step, (no_block, jnp.zeros_like(end_states))
    )
    incoming = prefix[1]
    ema_out, ema_back = jax.vjp(
        ema_terms, normed3, ema_delta, ema_alpha, ema_beta, ema_gamma, ema_omega, incoming
    )
    ema_flat = ema_out.reshape(row_count, D)
    mixed_low = jax.nn.silu(ema_flat).astype(jnp.bfloat16)
    base_pre = matmul(mixed_low, base_full) + base_bias
    update = jax.nn.sigmoid(base_pre[:, :D])
    shared_pre = base_pre[:, D : D + ZD + VD]
    shared_reset = jax.nn.silu(shared_pre)
    shared = shared_reset[:, :ZD]
    reset_gate = shared_reset[:, ZD:]
    hidden_x = base_pre[:, D + ZD + VD :]
    queries = (
        (shared * shared_gamma[0] + query_offset)
        .astype(jnp.bfloat16)
        .reshape(seq_local, block_len, ZD)
    )
    key_rows = (shared * shared_gamma[1]).astype(jnp.bfloat16).reshape(seq_local, block_len, ZD)
    position, position_back = jax.vjp(rel_table, position_bias)
    scores = (
        jnp.einsum("bik,bjk->bij", queries, key_rows, preferred_element_type=jnp.float32)
        * ZD ** (-0.5)
        + position
    )
    attn = masked_softmax(scores)
    attn_low = attn.astype(jnp.bfloat16)
    values3 = value_low.reshape(seq_local, block_len, VD)
    attended = jnp.einsum(
        "bij,bjv->biv", attn_low, values3, preferred_element_type=jnp.float32
    ).reshape(row_count, VD)
    gated_low = (attended * reset_gate).astype(jnp.bfloat16)
    proj_pre = matmul(gated_low, proj_full) + proj_bias
    hidden_sum = hidden_x + proj_pre
    hidden = jax.nn.silu(hidden_sum)
    first_out = tokens_flat + update * (hidden - tokens_flat)
    normed_two, norm2_back = jax.vjp(layer_norm, first_out, norm2_gain, norm2_bias)
    normed_two_low = normed_two.astype(jnp.bfloat16)
    ffn_pre = matmul(normed_two_low, ffn1_full) + ffn1_bias
    ffn_low = jax.nn.silu(ffn_pre).astype(jnp.bfloat16)
    ffn_out = matmul(ffn_low, ffn2_full) + ffn2_bias
    block_out = (first_out + ffn_out).astype(jnp.bfloat16).reshape(seq_local, block_len, D)
    grad_ffn2 = out_grad.reshape(row_count, D)
    dffn2_weight = left_product(ffn_low, grad_ffn2)
    dffn2_bias = column_sums(grad_ffn2)
    grad_ffn1 = (right_product(grad_ffn2, ffn2_full) * silu_slope(ffn_pre)).astype(jnp.bfloat16)
    dffn1_weight = left_product(normed_two_low, grad_ffn1)
    dffn1_bias = column_sums(grad_ffn1)
    grad_first_norm, dnorm2_gain, dnorm2_bias = norm2_back(right_product(grad_ffn1, ffn1_full))
    grad_first = grad_ffn2.astype(jnp.float32) + grad_first_norm
    grad_skip = grad_first * (1.0 - update)
    grad_update = grad_first * (hidden - tokens_flat)
    grad_hidden = grad_first * update * silu_slope(hidden_sum)
    grad_proj = grad_hidden.astype(jnp.bfloat16)
    dproj_weight = left_product(gated_low, grad_proj)
    dproj_bias = column_sums(grad_proj)
    grad_gated = right_product(grad_proj, proj_full)
    grad_attended = (grad_gated * reset_gate).astype(jnp.bfloat16).reshape(seq_local, block_len, VD)
    grad_reset = grad_gated * attended
    grad_attn = jnp.einsum(
        "biv,bjv->bij", grad_attended, values3, preferred_element_type=jnp.float32
    )
    grad_values = jnp.einsum(
        "bij,biv->bjv", attn_low, grad_attended, preferred_element_type=jnp.float32
    ).reshape(row_count, VD)
    grad_scores = (attn * (grad_attn - jnp.sum(grad_attn * attn, axis=-1, keepdims=True))).astype(
        jnp.bfloat16
    )
    (dposition_bias,) = position_back(jnp.sum(grad_scores.astype(jnp.float32), axis=0))
    grad_queries = jnp.einsum(
        "bij,bjk->bik", grad_scores, key_rows, preferred_element_type=jnp.float32
    ).reshape(row_count, ZD) * ZD ** (-0.5)
    grad_keys = jnp.einsum(
        "bij,bik->bjk", grad_scores, queries, preferred_element_type=jnp.float32
    ).reshape(row_count, ZD) * ZD ** (-0.5)
    dshared_gamma = jnp.stack(
        [jnp.sum(grad_queries * shared, axis=0), jnp.sum(grad_keys * shared, axis=0)]
    )
    dquery_offset = jnp.sum(grad_queries, axis=0)
    grad_shared = grad_queries * shared_gamma[0] + grad_keys * shared_gamma[1]
    grad_shared_pre = jnp.concatenate([grad_shared, grad_reset], axis=1) * silu_slope(shared_pre)
    grad_update_pre = grad_update * update * (1.0 - update)
    grad_base = jnp.concatenate([grad_update_pre, grad_shared_pre, grad_hidden], axis=1).astype(
        jnp.bfloat16
    )
    dbase_weight = left_product(mixed_low, grad_base)
    dbase_bias = column_sums(grad_base)
    grad_ema = right_product(grad_base, base_full) * silu_slope(ema_flat)
    grad_value_pre = (grad_values * silu_slope(value_pre)).astype(jnp.bfloat16)
    dvalue_weight = left_product(normed_low, grad_value_pre)
    dvalue_bias = column_sums(grad_value_pre)
    grad_normed = right_product(grad_value_pre, value_full)
    grad_normed_ema, delta_part, alpha_part, beta_part, dema_gamma, dema_omega, grad_incoming = (
        ema_back(grad_ema.reshape(seq_local, block_len, D))
    )
    suffix = prefix_2(
        (one_block, grad_incoming), "seq", chain_step, (no_block, jnp.zeros_like(grad_incoming))
    )
    grad_ends = suffix[1]
    grad_whole = jnp.sum(grad_ends * incoming, axis=0)
    grad_normed_ends, delta_rest, alpha_rest, beta_rest = ends_back((grad_whole, grad_ends))
    dema_delta = delta_part + delta_rest
    dema_alpha = alpha_part + alpha_rest
    dema_beta = beta_part + beta_rest
    grad_normed = grad_normed + (grad_normed_ema + grad_normed_ends).reshape(row_count, D)
    grad_tokens_norm, dnorm1_gain, dnorm1_bias = norm1_back(grad_normed)
    tokens_grad = (
        (grad_skip + grad_tokens_norm).astype(jnp.bfloat16).reshape(seq_local, block_len, D)
    )
    small_sums = lax.psum(
        (
            dnorm1_gain,
            dnorm1_bias,
            dvalue_bias,
            dema_delta,
            dema_alpha,
            dema_beta,
            dema_gamma,
            dema_omega,
            dbase_bias,
            dshared_gamma,
            dquery_offset,
            dposition_bias,
            dproj_bias,
            dnorm2_gain,
            dnorm2_bias,
            dffn1_bias,
            dffn2_bias,
        ),
        ("seq", "batch"),
    )
    reduced = (
        lax.psum_scatter(dvalue_weight, ("seq", "batch"), scatter_dimension=0, tiled=True),
        lax.psum_scatter(dbase_weight, ("seq", "batch"), scatter_dimension=0, tiled=True),
        lax.psum_scatter(dproj_weight, ("seq", "batch"), scatter_dimension=0, tiled=True),
        lax.psum_scatter(dffn1_weight, ("seq", "batch"), scatter_dimension=0, tiled=True),
        lax.psum_scatter(dffn2_weight, ("seq", "batch"), scatter_dimension=0, tiled=True),
    )
    return (
        block_out,
        tokens_grad,
        small_sums[0],
        small_sums[1],
        reduced[0],
        small_sums[2],
        small_sums[3],
        small_sums[4],
        small_sums[5],
        small_sums[6],
        small_sums[7],
        reduced[1],
        small_sums[8],
        small_sums[9],
        small_sums[10],
        small_sums[11],
        reduced[2],
        small_sums[12],
        small_sums[13],
        small_sums[14],
        reduced[3],
        small_sums[15],
        reduced[4],
        small_sums[16],
    )


VMEM_LIMIT = 63 * 1024 * 1024
BF = jnp.bfloat16
F32 = jnp.float32
MESH = pl.DeviceIdType.MESH
SCALE = ZD ** (-0.5)
EMA_SCALE = NDIM ** (-0.5)
BLK = 128
VH = 1024
BASE_COLS = 2176
SM_ROWS = 400
ROW_OMEGA, ROW_N1G, ROW_N1B, ROW_N2G, ROW_N2B = 256, 264, 272, 280, 288
ROW_VB, ROW_BB, ROW_PB, ROW_F1B, ROW_F2B = 296, 312, 345, 353, 385
ROW_SG, ROW_QO, ROW_POS = 393, 395, 396
VALUE, BASE, PROJ, FFN1, FFN2 = range(5)
U_V, U_P, U_BA, U_BB, U_1, U_2 = range(6)


def pick(flag, yes, no):
    return lax.select(flag, yes, no)


def sig(v):
    return jax.nn.sigmoid(v)


def silu(v):
    return v * sig(v)


def slope(v):
    s = sig(v)
    return s * (1.0 + v * (1.0 - s))


def dot_nn(a, b):
    return jnp.dot(a, b, preferred_element_type=F32)


def dot_nt(a, b):
    return lax.dot_general(a, b, (((1,), (1,)), ((), ())), preferred_element_type=F32)


def dot_tn(a, b):
    return lax.dot_general(a, b, (((0,), (0,)), ((), ())), preferred_element_type=F32)


def split_pair(first, second, low_lanes):
    lo = jnp.where(low_lanes, first, pltpu.roll(second, 64, 1))
    hi = jnp.where(low_lanes, pltpu.roll(first, 64, 1), second)
    return lo, hi


def fold8(v):
    rows, cols = v.shape
    return jnp.sum(v.reshape(rows // 8, 8, cols), axis=0)


def shear(v, left):
    rows = lax.broadcasted_iota(jnp.int32, (BLK, BLK), 0)
    for bit in range(7):
        step = 1 << bit
        turned = pltpu.roll(v, BLK - step if left else step, 1)
        v = jnp.where((rows & step) != 0, turned, v)
    return v


def layer_kernel(NS, *refs):
    NZ = NS // 4
    names = iter(refs)
    take = lambda n: [next(names) for _ in range(n)]
    (tok, og, n1g, n1b, vb, ema, om, bb, sg, qo, pbr, pbias, n2g, n2b, f1b, f2b) = take(16)
    (vw, bw, pw, f1w, f2w) = take(5)
    (o_block, o_tok, o_dv, o_db, o_dp, o_d1, o_d2, o_sm, o_ema) = take(9)
    (WV, WB, WP, W1, W2) = take(5)
    (G1, G2, GBA, GBB, RXBB) = take(5)
    RY = take(6)
    RZ = take(6)
    (FV, FB, FXV, FXB, FX1) = take(5)
    (SV, SB, NL, ML, NO, VP, VL, UH, UU, HH, SHP, RP, AD, GT, AT, PR, FO, FP, FG) = take(19)
    (AS, AR, AX, AXR, OXR, GH, GUS, GBS, GA, GAT, GATR, GVP, GNVR) = take(13)
    (XP, YP, GEP, GNP, HC, H8, EC, EXX, EXY, EXZ, BXX, BXY, BXZ, DEC, CIN, LAM, PIN) = take(17)
    (SMR, SMX, SMY, SMZ, SMC) = take(5)
    (in_sem, zs, zr, ys, yr, xs, xr, rxs, rxr, rys, ryr, rzs, rzr, es, er) = take(15)

    s = lax.axis_index("seq")
    b = lax.axis_index("batch")
    x = lax.rem(s, 2)
    y = lax.rem(lax.div(s, 2), 2)
    z = lax.div(s, 4)
    p = lax.div(s, 2)
    q = 2 * x + b
    xs_ = s + 1 - 2 * x
    ys_ = s + 2 - 4 * y
    C = (s, 1 - b)
    X = (xs_, b)
    XC = (xs_, 1 - b)
    Y = (ys_, b)
    ahead = lambda k: lax.rem(s + 4 * k, NS)
    behind = lambda k: lax.rem(s - 4 * k + NS * 4, NS)
    first = b == 0
    al = pl.multiple_of
    rows_of = lambda i, n: pl.ds(al(i * n, n), n)

    loads = [
        pltpu.make_async_copy(src, dst, in_sem.at[i])
        for i, (src, dst) in enumerate(
            ((vw, o_dv), (bw, o_db), (pw, o_dp), (f1w, o_d1), (f2w, o_d2))
        )
    ]
    for load in loads:
        load.start()

    barrier = pltpu.get_barrier_semaphore()
    partners = [C, X, XC, Y] + [(ahead(k), b) for k in range(1, NZ)]
    for device in partners:
        pl.semaphore_signal(barrier, inc=1, device_id=device, device_id_type=MESH)
    pl.semaphore_wait(barrier, len(partners))

    def remote(src, dst, send, recv, device):
        return pltpu.make_async_remote_copy(
            src_ref=src, dst_ref=dst, send_sem=send, recv_sem=recv, device_id=device, device_id_type=MESH
        )

    open_sends = []

    def settle(copy):
        open_sends[:] = [other for other in open_sends if other is not copy]

    n_ex = [0]

    def exchange(src, dst, device, landed=None):
        i = n_ex[0]
        n_ex[0] += 1
        copy = remote(src, dst, es.at[i], er.at[i], device)
        copy.start()
        open_sends.append(copy)
        arrival = copy if landed is None else remote(src, landed, es.at[i], er.at[i], device)
        return copy, arrival

    low1 = lambda n: lax.broadcasted_iota(jnp.int32, (n, BLK), 1) < 64

    my_rows = pl.ds(al(64 * s + 32 * b, 32), 32)
    other_rows = pl.ds(al(64 * s + 32 * (1 - b), 32), 32)

    def split_columns(src, src0, blocks, mine_ref, mine_rows, dst0, other_ref):
        low = low1(32)
        for t in range(blocks):
            lo, hi = split_pair(
                src[:, src0 + 256 * t : src0 + 256 * t + 128],
                src[:, src0 + 256 * t + 128 : src0 + 256 * t + 256],
                low,
            )
            cols = slice(dst0 + 128 * t, dst0 + 128 * t + 128)
            mine_ref[mine_rows, cols] = pick(first, lo, hi).astype(BF)
            other_ref[:, cols] = pick(first, hi, lo).astype(BF)

    loads[0].wait()
    split_columns(o_dv, 0, 8, WV, my_rows, 0, SV)
    _, got_wv = exchange(SV, WV.at[my_rows], C, WV.at[other_rows])
    loads[1].wait()
    WB[my_rows, 0:512] = o_db[:, pl.ds(al(512 * b, 512), 512)].astype(BF)
    SB[:, 0:512] = o_db[:, pl.ds(al(512 * (1 - b), 512), 512)].astype(BF)
    WB[my_rows, 512:1024] = o_db[:, pl.ds(al(3200 + 512 * b, 128), 512)].astype(BF)
    SB[:, 512:1024] = o_db[:, pl.ds(al(3200 + 512 * (1 - b), 128), 512)].astype(BF)
    shared_cols = o_db[:, 1024:1152].astype(BF)
    WB[my_rows, 1024:1152] = shared_cols
    SB[:, 1024:1152] = shared_cols
    split_columns(o_db, 1152, 8, WB, my_rows, 1152, SB)
    _, got_wb = exchange(SB, WB.at[my_rows], C, WB.at[other_rows])

    gather = [WV, WB, WP, W1, W2]

    def piece(w, chip):
        if w < FFN1:
            return gather[w].at[rows_of(chip, 64)]
        return gather[w].at[rows_of(lax.div(chip, 2), 128)]

    def send_z(w, k):
        here = piece(w, s)
        return remote(here, here, zs.at[w, k], zr.at[w, k], (ahead(k), b))

    def got_z(w, k):
        there = piece(w, behind(k))
        return remote(there, there, zs.at[w, k], zr.at[w, k], (ahead(k), b))

    def send_y(w, k):
        part = piece(w, behind(k))
        return remote(part, part, ys.at[w, k], yr.at[w, k], Y)

    def got_y(w, k):
        part = piece(w, ys_ + behind(k) - s)
        return remote(part, part, ys.at[w, k], yr.at[w, k], Y)

    def send_x(w, k, far):
        chip = behind(k) if far == 0 else ys_ + behind(k) - s
        part = piece(w, chip)
        return remote(part, part, xs.at[w, far, k], xr.at[w, far, k], X)

    def got_x(w, k, far):
        chip = behind(k) if far == 0 else ys_ + behind(k) - s
        part = piece(w, chip + xs_ - s)
        return remote(part, part, xs.at[w, far, k], xr.at[w, far, k], X)

    def open_gather(w):
        for k in range(1, NZ):
            send_z(w, k).start()
        send_y(w, 0).start()
        if w < FFN1:
            send_x(w, 0, 0).start()

    def relay_z(w):
        def one(k, carry):
            got_z(w, k).wait_recv()
            send_y(w, k).start()
            if w < FFN1:
                send_x(w, k, 0).start()
            return carry

        lax.fori_loop(1, NZ, one, 0)

    def relay_y(w):
        def one(k, carry):
            got_y(w, k).wait_recv()
            if w < FFN1:
                send_x(w, k, 1).start()
            return carry

        lax.fori_loop(0, NZ, one, 0)

    def finish_x(w):
        def one(k, carry):
            got_x(w, k, 0).wait_recv()
            got_x(w, k, 1).wait_recv()
            return carry

        lax.fori_loop(0, NZ, one, 0)

    def close_gather(w):
        def one(k, carry):
            send_y(w, k).wait_send()
            if w < FFN1:
                send_x(w, k, 0).wait_send()
                send_x(w, k, 1).wait_send()
            return carry

        lax.fori_loop(0, NZ, one, 0)

        def plane(k, carry):
            send_z(w, k).wait_send()
            return carry

        lax.fori_loop(1, NZ, plane, 0)

    def norm_rows(v):
        center = v - jnp.mean(v, axis=-1, keepdims=True)
        rstd = lax.rsqrt(jnp.mean(center * center, axis=-1, keepdims=True) + 1e-05)
        return center * rstd, rstd

    own = rows_of(b, BLK)

    def norm_one(i, carry):
        rows = rows_of(i, 32)
        n, _ = norm_rows(tok[rows, :].astype(F32))
        normed = n * n1g[...] + n1b[...]
        for g in range(8):
            XP[pl.ds(al(128 * g + 32 * i, 32), 32), :] = normed[:, 128 * g : 128 * g + 128]
        NL[pl.ds(al(128 * b + 32 * i, 32), 32), :] = normed.astype(BF)
        return carry

    got_wv.wait_recv()
    open_gather(VALUE)
    lax.fori_loop(0, 4, norm_one, 0)
    _, got_nl = exchange(NL.at[own], NL.at[own], C, NL.at[rows_of(1 - b, BLK)])
    got_wb.wait_recv()
    open_gather(BASE)

    NT = NO.at[0:512]
    OG = NO.at[512:1024]
    quad = lambda j: rows_of(j, BLK)

    for j in range(NDIM):
        rate = sig(ema[0, j])
        DEC[j] = 1.0 - rate * sig(ema[1, j])
        CIN[j] = rate * ema[2, j]
        lam = DEC[j]
        for _ in range(7):
            lam = lam * lam
        LAM[j] = lam

    def panel(t):
        return pl.ds(t, 8, stride=BLK)

    def end_scan():
        d = [DEC[j] for j in range(NDIM)]
        c = [CIN[j] for j in range(NDIM)]

        def step(t, h):
            row = XP[panel(t), :]
            return tuple(h[j] * d[j] + c[j] * row for j in range(NDIM))

        h = lax.fori_loop(
            0, BLK, step, tuple(jnp.zeros((8, 128), F32) for _ in range(NDIM)), unroll=4
        )
        for j in range(NDIM):
            EC[0, j] = h[j]

    end_scan()
    _, got_ex = exchange(EC.at[0], EXX, X)

    loads[2].wait()
    WP[rows_of(s, 64), :] = o_dp[...].astype(BF)
    loads[3].wait()
    for j in range(4):
        for t in range(8):
            AS[32 * j : 32 * j + 32, 128 * t : 128 * t + 128] = o_d1[
                :, 128 * (4 * t + j) : 128 * (4 * t + j) + 128
            ].astype(BF)
    f1_rows = lambda j: pl.ds(al(128 * p + 32 * j, 32), 32)
    W1[f1_rows(q), :] = AS[rows_of(q, 32), :]
    q_c = q + 1 - 2 * b
    q_x = lax.rem(q + 2, 4)
    q_xc = lax.rem(q_c + 2, 4)
    f1_pairs = [
        exchange(AS.at[rows_of(j, 32)], W1.at[f1_rows(q)], device, W1.at[f1_rows(j)])
        for j, device in ((q_c, C), (q_x, X), (q_xc, XC))
    ]
    loads[4].wait()
    W2[rows_of(p, 128), :] = o_d2[...].astype(BF)
    OG[quad(q), :] = og[...]
    copy_og_c, got_og_c = exchange(OG.at[quad(q)], OG.at[quad(q)], C, OG.at[quad(q_c)])
    copy_og_x, got_og_x = exchange(OG.at[quad(q)], OG.at[quad(q)], X, OG.at[quad(q_x)])

    open_gather(PROJ)
    relay_z(VALUE)
    relay_y(VALUE)

    def scan_round_x(own_state, arrived, out, incoming, later):
        for j in range(NDIM):
            l, mine, theirs = LAM[j], own_state[j], arrived[j]
            out[j] = pick(later, l * theirs + mine, l * mine + theirs)
            incoming[j] = pick(later, theirs, jnp.zeros_like(theirs))

    def scan_round_y(own_state, arrived, out, incoming, later, inner):
        for j in range(NDIM):
            l = LAM[j]
            l2 = l * l
            mine, theirs = own_state[j], arrived[j]
            out[j] = pick(later, l2 * theirs + mine, l2 * mine + theirs)
            hop = pick(inner == 1, l, jnp.ones_like(l))
            incoming[j] += pick(later, hop * theirs, jnp.zeros_like(l))

    def scan_round_z(arrived, incoming, reach, inner):
        for j in range(NDIM):
            l = LAM[j]
            l2 = l * l
            l4 = l2 * l2
            one = jnp.ones_like(l)
            hop = pick(lax.rem(inner, 2) == 1, l, one) * pick(inner >= 2, l2, one)
            total = incoming[j]
            for k in range(1, NZ):
                total += pick(k <= reach, hop * arrived[k - 1, j], jnp.zeros_like(l))
                hop = hop * l4
            incoming[j] = total

    got_ex.wait_recv()
    scan_round_x(EC.at[0], EXX, EC.at[1], PIN, x == 1)
    _, got_ey = exchange(EC.at[1], EXY, Y)
    for copy, got in f1_pairs:
        copy.wait_send()
        settle(copy)
        got.wait_recv()
    open_gather(FFN1)
    relay_z(BASE)
    got_ey.wait_recv()
    scan_round_y(EC.at[1], EXY, EC.at[2], PIN, y == 1, x)
    got_ez = [exchange(EC.at[2], EXZ.at[k - 1], (ahead(k), b))[1] for k in range(1, NZ)]
    open_gather(FFN2)
    relay_y(BASE)
    got_og_x.wait_recv()
    copy_og_xc, got_og_xc = exchange(OG.at[quad(q_x)], OG.at[quad(q_x)], C, OG.at[quad(q_xc)])
    relay_z(PROJ)
    relay_y(PROJ)
    for got in got_ez:
        got.wait_recv()
    scan_round_z(EXZ, PIN, z, 2 * y + x)

    def forward_scan():
        for half in range(2):
            js = range(8 * half, 8 * half + 8)
            d = [DEC[j] for j in js]
            c = [CIN[j] for j in js]
            g = [EMA_SCALE * ema[3, j] for j in js]

            def group(i, h):
                for n, j in enumerate(js):
                    HC[i, j] = h[n]
                for u in range(8):
                    t = 8 * i + u
                    row = XP[panel(t), :]
                    h = tuple(h[n] * d[n] + c[n] * row for n in range(8))
                    out = g[0] * h[0]
                    for n in range(1, 8):
                        out = out + g[n] * h[n]
                    if half == 0:
                        out = out + om[...] * row
                    else:
                        out = out + YP[panel(t), :]
                    YP[panel(t), :] = out
                return h

            lax.fori_loop(0, 16, group, tuple(PIN[j] for j in js))

    forward_scan()

    def mixed_one(i, carry):
        for g in range(8):
            v = YP[pl.ds(al(128 * g + 32 * i, 32), 32), :]
            ML[pl.ds(al(128 * b + 32 * i, 32), 32), 128 * g : 128 * g + 128] = silu(v).astype(BF)
        return carry

    lax.fori_loop(0, 4, mixed_one, 0)
    _, got_ml = exchange(ML.at[own], ML.at[own], C, ML.at[rows_of(1 - b, BLK)])

    low_row = low1(1)

    def my_half(ref, start):
        parts = []
        for t in range(8):
            lo, hi = split_pair(
                ref[:, start + 256 * t : start + 256 * t + 128],
                ref[:, start + 256 * t + 128 : start + 256 * t + 256],
                low_row,
            )
            parts.append(pick(first, lo, hi))
        return jnp.concatenate(parts, axis=1)

    got_nl.wait_recv()
    finish_x(VALUE)
    vbias = my_half(vb, 0)
    for n in range(2):
        cols = slice(512 * n, 512 * n + 512)
        v = dot_nn(NL[...], WV[:, cols]) + vbias[:, cols]
        VP[:, cols] = v.astype(BF)
        VL[:, cols] = silu(v).astype(BF)

    relay_z(FFN1)

    got_ml.wait_recv()
    finish_x(BASE)
    UH[:, 0:512] = dot_nn(ML[...], WB[:, 0:512]) + bb[:, pl.ds(al(512 * b, 512), 512)]
    UH[:, 512:1024] = dot_nn(ML[...], WB[:, 512:1024]) + bb[:, pl.ds(al(3200 + 512 * b, 128), 512)]
    theirs = rows_of(1 - b, BLK)
    my_cols = pl.ds(al(512 * b, 512), 512)
    their_cols = pl.ds(al(512 * (1 - b), 512), 512)
    copy_u, got_u = exchange(UH.at[theirs, 0:512], UU.at[:, my_cols], C, UU.at[:, their_cols])
    copy_h, got_h = exchange(UH.at[theirs, 512:1024], HH.at[:, my_cols], C, HH.at[:, their_cols])
    UU[:, my_cols] = UH[own, 0:512]
    HH[:, my_cols] = UH[own, 512:1024]
    SHP[...] = dot_nn(ML[...], WB[:, 1024:1152]) + bb[:, 1024:1152]
    rbias = my_half(bb, 1152)
    for n in range(2):
        RP[:, 512 * n : 512 * n + 512] = (
            dot_nn(ML[...], WB[:, 1152 + 512 * n : 1664 + 512 * n]) + rbias[:, 512 * n : 512 * n + 512]
        ).astype(BF)

    shared_of = lambda i: silu(SHP[128 * i : 128 * i + 128, :])

    def queries_keys(i):
        sh = shared_of(i)
        return (sh * sg[0:1, :] + qo[...]).astype(BF), (sh * sg[1:2, :]).astype(BF)

    position = shear(jnp.broadcast_to(pbr[...], (BLK, BLK)), False)
    at_row = lax.broadcasted_iota(jnp.int32, (BLK, BLK), 0)
    at_col = lax.broadcasted_iota(jnp.int32, (BLK, BLK), 1)
    causal = at_row >= at_col
    for i in range(2):
        rows = slice(128 * i, 128 * i + 128)
        qs, ks = queries_keys(i)
        scores = jnp.where(causal, dot_nt(qs, ks) * SCALE + position, -jnp.inf)
        e = jnp.exp(scores - jnp.max(scores, axis=-1, keepdims=True))
        attn = e / jnp.sum(e, axis=-1, keepdims=True)
        AT[rows, :] = attn
        low = attn.astype(BF)
        for n in range(2):
            cols = slice(512 * n, 512 * n + 512)
            att = dot_nn(low, VL[rows, cols])
            AD[rows, cols] = att.astype(BF)
            GT[rows, cols] = (att * silu(RP[rows, cols].astype(F32))).astype(BF)

    relay_z(FFN2)

    finish_x(PROJ)
    copy_u.wait_send()
    copy_h.wait_send()
    settle(copy_u)
    settle(copy_h)
    for n in range(2):
        cols = slice(512 * n, 512 * n + 512)
        UH[:, cols] = dot_nn(GT[...], WP[:, cols])
    copy_p, got_p = exchange(UH.at[theirs], PR, C)
    got_u.wait_recv()
    got_h.wait_recv()
    got_p.wait_recv()

    def residual_one(i, carry):
        rows = rows_of(i, 32)
        mine = pl.ds(al(128 * b + 32 * i, 32), 32)
        total = HH[rows, :] + ((UH[mine, :] + PR[rows, :]) + pbias[...])
        HH[rows, :] = total
        base = tok[rows, :].astype(F32)
        out = base + sig(UU[rows, :]) * (silu(total) - base)
        FO[rows, :] = out
        n, _ = norm_rows(out)
        NT[pl.ds(al(128 * q + 32 * i, 32), 32), :] = (n * n2g[...] + n2b[...]).astype(BF)
        return carry

    lax.fori_loop(0, 4, residual_one, 0)
    copy_nt_x, got_nt_x = exchange(NT.at[quad(q)], NT.at[quad(q)], X, NT.at[quad(q_x)])
    copy_nt_c, got_nt_c = exchange(NT.at[quad(q)], NT.at[quad(q)], C, NT.at[quad(q_c)])

    relay_y(FFN1)
    relay_y(FFN2)
    got_og_c.wait_recv()
    got_og_xc.wait_recv()
    for m in range(2):
        for n in range(2):
            rows = slice(256 * m, 256 * m + 256)
            cols = slice(512 * n, 512 * n + 512)
            FP[rows, cols] = dot_nt(OG[rows, :], W2[cols, :])
    got_nt_x.wait_recv()
    copy_nt_xc, got_nt_xc = exchange(NT.at[quad(q_x)], NT.at[quad(q_x)], C, NT.at[quad(q_xc)])
    got_nt_c.wait_recv()
    got_nt_xc.wait_recv()

    FL = FG.at[0:512]
    GF = FG.at[512:1024]
    fbias = jnp.concatenate(
        [f1b[:, pl.ds(al(512 * t + 128 * q, 128), 128)] for t in range(8)], axis=1
    )
    for m in range(2):
        for n in range(2):
            rows = slice(256 * m, 256 * m + 256)
            cols = slice(512 * n, 512 * n + 512)
            pre = dot_nn(NT[rows, :], W1[:, cols]) + fbias[:, cols]
            FL[rows, cols] = silu(pre).astype(BF)
            GF[rows, cols] = (FP[rows, cols] * slope(pre)).astype(BF)
    for m in range(2):
        for n in range(2):
            rows = slice(256 * m, 256 * m + 256)
            cols = slice(512 * n, 512 * n + 512)
            AS[rows, cols] = dot_nt(GF[rows, :], W1[cols, :]).astype(BF)

    def reduce_pair(staged, landing):
        copies = []
        for c in range(2):
            there = rows_of(2 * c + 1 - b, BLK)
            copies.append(exchange(staged.at[there], landing.at[rows_of(c, BLK)], C))
        return copies

    def reduce_x(staged, landing, arrivals, out, out_landing):
        for _, arrival in arrivals:
            arrival.wait_recv()

        def one(i, carry):
            mine = pl.ds(al(128 * (2 * (1 - x) + b) + 32 * i, 32), 32)
            got = pl.ds(al(128 * (1 - x) + 32 * i, 32), 32)
            out[rows_of(i, 32), :] = (staged[mine, :].astype(F32) + landing[got, :].astype(F32)).astype(BF)
            return carry

        lax.fori_loop(0, 4, one, 0)
        return exchange(out, out_landing, X)

    def reduced(staged, landing, out_landing, i):
        mine = pl.ds(al(128 * q + 32 * i, 32), 32)
        got = pl.ds(al(128 * x + 32 * i, 32), 32)
        return (
            staged[mine, :].astype(F32)
            + landing[got, :].astype(F32)
            + out_landing[rows_of(i, 32), :].astype(F32)
        )

    got_a = reduce_pair(AS, AR)

    def store_row(row, v):
        for g in range(v.shape[1] // 128):
            SM_OUT[row + g : row + g + 1, :] = v[:, 128 * g : 128 * g + 128]

    SM_OUT = o_sm
    SM_OUT[...] = jnp.zeros((SM_ROWS, 128), F32)

    def weight_grad(left, right, out, right0, out0, width):
        tile = 512 if width % 512 == 0 else 384
        for m in range(2):
            for n in range(width // tile):
                out[512 * m : 512 * m + 512, out0 + tile * n : out0 + tile * n + tile] = dot_tn(
                    left[:, 512 * m : 512 * m + 512],
                    right[:, right0 + tile * n : right0 + tile * n + tile],
                ).astype(BF)

    grads = [NO, FG, GBA, GBB, G1, G2]
    RXV = W1.at[0:512]
    RXP = W1.at[512:1024]
    RXBA = W2.at[0:512]
    half = [RXV, RXP, RXBA, RXBB]

    def shard(u, chip):
        if u < U_1:
            return rows_of(chip, 64)
        return rows_of(lax.div(chip, 2), 128)

    def rs_x(u, k, far):
        plane = ahead(k)
        chip = plane if far == 0 else plane + ys_ - s
        src = grads[u].at[shard(u, chip + xs_ - s)]
        slot = half[u].at[pl.ds(al(64 * (2 * k + far), 64), 64)]
        return remote(src, slot, rxs.at[u, k, far], rxr.at[u, k, far], X)

    def rs_y(u, k):
        src = grads[u].at[shard(u, ahead(k) + ys_ - s)]
        return remote(src, RY[u].at[k], rys.at[u, k], ryr.at[u, k], Y)

    def rs_z(u, k):
        src = grads[u].at[shard(u, ahead(k))]
        return remote(src, RZ[u].at[k - 1], rzs.at[u, k], rzr.at[u, k], (ahead(k), b))

    turn = lambda i: lax.rem(i + 1, NZ)

    def rs_open(u):
        def one(i, carry):
            k = turn(i)
            if u < U_1:
                rs_x(u, k, 1).start()
                rs_x(u, k, 0).start()
            else:
                rs_y(u, k).start()
            return carry

        lax.fori_loop(0, NZ, one, 0)

    def rs_pass_x(u):
        def one(i, carry):
            k = turn(i)
            plane = ahead(k)
            for far in (1, 0):
                rs_x(u, k, far).wait_recv()
                chip = plane if far == 0 else plane + ys_ - s
                rows = shard(u, chip)
                got = half[u][pl.ds(al(64 * (2 * k + far), 64), 64), :]
                grads[u][rows, :] = (grads[u][rows, :].astype(F32) + got.astype(F32)).astype(BF)
                if far == 1:
                    rs_y(u, k).start()
            return carry

        lax.fori_loop(0, NZ, one, 0)

    def rs_pass_y(u):
        def one(i, carry):
            k = i + 1
            rs_y(u, k).wait_recv()
            rows = shard(u, ahead(k))
            grads[u][rows, :] = (grads[u][rows, :].astype(F32) + RY[u][k].astype(F32)).astype(BF)
            rs_z(u, k).start()
            return carry

        lax.fori_loop(0, NZ - 1, one, 0)
        rs_y(u, 0).wait_recv()

    def rs_total(u, rows_in):
        rows = shard(u, s)
        size = 64 if u < U_1 else 128
        start = size * (s if u < U_1 else p)
        at = pl.ds(al(start + rows_in[0], 16), rows_in[1])
        in_ = pl.ds(al(rows_in[0], 16), rows_in[1])
        total = grads[u][at, :].astype(F32) + RY[u][0, in_, :].astype(F32)
        for k in range(1, NZ):
            total += RZ[u][k - 1, in_, :].astype(F32)
        return total

    def rs_wait_z(u):
        def one(k, carry):
            rs_z(u, k).wait_recv()
            return carry

        lax.fori_loop(1, NZ, one, 0)

    def column_sum(ref, start, width):
        def one(i, acc):
            return acc + fold8(ref[rows_of(i, 32), start : start + width].astype(F32))

        acc = lax.fori_loop(0, ref.shape[0] // 32, one, jnp.zeros((8, width), F32))
        return jnp.sum(acc, axis=0, keepdims=True)

    weight_grad(FL, OG, G2, 0, 0, 1024)
    rs_open(U_2)
    a_x = reduce_x(AS, AR, got_a, AX, AXR)
    weight_grad(NT, GF, G1, 0, 0, 1024)
    rs_open(U_1)
    f1_sum = column_sum(GF, 0, 1024)
    for t in range(8):
        SM_OUT[pl.ds(ROW_F1B + 4 * t + q, 1), :] = f1_sum[:, 128 * t : 128 * t + 128]

    a_x[1].wait_recv()

    def back_two(i, carry):
        rows = rows_of(i, 32)
        a = reduced(AS, AR, AXR, i)
        n, rstd = norm_rows(FO[rows, :])
        g = a * n2g[...]
        grad = og[rows, :].astype(F32) + (
            g - jnp.mean(g, axis=-1, keepdims=True) - n * jnp.mean(g * n, axis=-1, keepdims=True)
        ) * rstd
        update = sig(UU[rows, :])
        total = HH[rows, :]
        logistic = sig(total)
        base = tok[rows, :].astype(F32)
        gh = (grad * update * (logistic * (1.0 + total * (1.0 - logistic)))).astype(BF)
        GH[pl.ds(al(128 * b + 32 * i, 32), 32), :] = gh
        GUS[rows, :] = (grad * (total * logistic - base) * update * (1.0 - update)).astype(BF)
        PR[rows, :] = grad * (1.0 - update)
        return (
            carry[0] + fold8(a * n),
            carry[1] + fold8(a),
            carry[2] + fold8(gh.astype(F32)),
            carry[3] + fold8(og[rows, :].astype(F32)),
        )

    zero8 = jnp.zeros((8, 1024), F32)
    sums = lax.fori_loop(0, 4, back_two, (zero8, zero8, zero8, zero8))
    _, got_gh = exchange(GH.at[own], GH.at[own], C, GH.at[theirs])
    _, got_gu = exchange(GUS.at[:, their_cols], GBS.at[own, 0:512], C, GBS.at[theirs, 0:512])
    GBS[own, 0:512] = GUS[:, my_cols]
    for row, acc in zip((ROW_N2G, ROW_N2B, ROW_PB, ROW_F2B), sums):
        store_row(row, jnp.sum(acc, axis=0, keepdims=True))

    got_gh.wait_recv()
    for copy, _ in got_a:
        copy.wait_send()
        settle(copy)
    for m in range(2):
        for n in range(2):
            rows = slice(256 * m, 256 * m + 256)
            cols = slice(512 * n, 512 * n + 512)
            AS[rows, cols] = dot_nn(FL[rows, :], W2[:, cols]).astype(BF)
    got_o = reduce_pair(AS, AR)
    close_gather(FFN1)
    close_gather(FFN2)

    for n in range(2):
        cols = slice(512 * n, 512 * n + 512)
        gg = dot_nt(GH[...], WP[cols, :])
        pre = RP[:, cols].astype(F32)
        logistic = sig(pre)
        GA[:, cols] = (gg * (pre * logistic)).astype(BF)
        GBS[:, 1152 + 512 * n : 1664 + 512 * n] = (
            gg * AD[:, cols].astype(F32) * (logistic * (1.0 + pre * (1.0 - logistic)))
        ).astype(BF)
    for i in range(2):
        rows = slice(128 * i, 128 * i + 128)
        GAT[rows, :] = dot_nt(GA[rows, :], VL[rows, :])
    _, got_gat = exchange(GAT, GATR, C)
    a_x[0].wait_send()
    settle(a_x[0])
    o_x = reduce_x(AS, AR, got_o, AX, OXR)
    for i in range(2):
        rows = slice(128 * i, 128 * i + 128)
        low = AT[rows, :].astype(BF)
        for n in range(2):
            cols = slice(512 * n, 512 * n + 512)
            gv = dot_tn(low, GA[rows, cols])
            GVP[rows, cols] = (gv * slope(VP[rows, cols].astype(F32))).astype(BF)
    GBS[:, 512:1024] = GH[:, my_cols]
    o_x[1].wait_recv()
    weight_grad(GT, GH, FG, 0, 0, 1024)
    rs_open(U_P)
    got_gat.wait_recv()
    for i in range(2):
        rows = slice(128 * i, 128 * i + 128)
        attn = AT[rows, :]
        gat = GAT[rows, :] + GATR[rows, :]
        gs = (attn * (gat - jnp.sum(gat * attn, axis=-1, keepdims=True))).astype(BF)
        qs, ks = queries_keys(i)
        gq = dot_nn(gs, ks) * SCALE
        gk = dot_tn(gs, qs) * SCALE
        pre = SHP[rows, :]
        sh = silu(pre)
        GBS[rows, 1024:1152] = ((gq * sg[0:1, :] + gk * sg[1:2, :]) * slope(pre)).astype(BF)
        mine = b == i

        @pl.when(mine)
        def _(gs=gs, gq=gq, gk=gk, sh=sh):
            SM_OUT[ROW_SG : ROW_SG + 1, :] = jnp.sum(gq * sh, axis=0, keepdims=True)
            SM_OUT[ROW_SG + 1 : ROW_SG + 2, :] = jnp.sum(gk * sh, axis=0, keepdims=True)
            SM_OUT[ROW_QO : ROW_QO + 1, :] = jnp.sum(gq, axis=0, keepdims=True)
            SM_OUT[ROW_POS : ROW_POS + 1, :] = jnp.sum(
                shear(gs.astype(F32), True), axis=0, keepdims=True
            )

    got_gu.wait_recv()
    weight_grad(ML, GBS, GBA, 0, 0, 1024)
    rs_open(U_BA)
    weight_grad(ML, GBS, GBB, 1024, 0, 1152)
    rs_open(U_BB)
    base_sum = column_sum(GBS, 0, BASE_COLS)
    for t in range(4):
        cols = slice(128 * t, 128 * t + 128)
        SM_OUT[pl.ds(ROW_BB + 4 * b + t, 1), :] = base_sum[:, cols]
        SM_OUT[pl.ds(ROW_BB + 25 + 4 * b + t, 1), :] = base_sum[:, 512 + 128 * t : 640 + 128 * t]
    SM_OUT[ROW_BB + 8 : ROW_BB + 9, :] = base_sum[:, 1024:1152] * 0.5

    low_float = low_row.astype(F32)
    keep = pick(first, low_float, 1.0 - low_float)

    def store_half(row, v):
        for t in range(8):
            block = v[:, 128 * t : 128 * t + 128]
            turned = pltpu.roll(block, 64, 1)
            SM_OUT[row + 2 * t : row + 2 * t + 1, :] = keep * pick(first, block, turned)
            SM_OUT[row + 2 * t + 1 : row + 2 * t + 2, :] = keep * pick(first, turned, block)

    store_half(ROW_BB + 9, base_sum[:, 1152:2176])
    GBS[:, 1024:1152] = (GBS[:, 1024:1152].astype(F32) * 0.5).astype(BF)
    GM = FP.at[0:256]
    GNV = FP.at[256:512]
    for n in range(2):
        cols = slice(512 * n, 512 * n + 512)
        GM[:, cols] = dot_nt(GBS[...], WB[cols, :])
    _, got_gm = exchange(GM.at[theirs], GNVR.at[0], C)
    for n in range(2):
        cols = slice(512 * n, 512 * n + 512)
        GNV[:, cols] = dot_nt(GVP[...], WV[cols, :])
    _, got_gnv = exchange(GNV.at[theirs], GNVR.at[1], C)
    for copy in (copy_og_c, copy_og_x, copy_og_xc, copy_nt_x, copy_nt_c, copy_nt_xc):
        copy.wait_send()
        settle(copy)
    weight_grad(NL, GVP, NO, 0, 0, 1024)
    rs_open(U_V)
    store_half(ROW_VB, column_sum(GVP, 0, 1024))

    got_gm.wait_recv()

    def grad_ema_one(i, carry):
        for g in range(8):
            cols = slice(128 * g, 128 * g + 128)
            rows = pl.ds(al(128 * g + 32 * i, 32), 32)
            v = GM[pl.ds(al(128 * b + 32 * i, 32), 32), cols] + GNVR[0, rows_of(i, 32), cols]
            GEP[rows, :] = v * slope(YP[rows, :])
        return carry

    lax.fori_loop(0, 4, grad_ema_one, 0)

    def adjoint_end():
        d = [DEC[j] for j in range(NDIM)]

        def step(i, g):
            row = GEP[panel(BLK - 1 - i), :]
            return tuple(g[j] * d[j] + row for j in range(NDIM))

        g = lax.fori_loop(
            0, BLK, step, tuple(jnp.zeros((8, 128), F32) for _ in range(NDIM)), unroll=4
        )
        for j in range(NDIM):
            EC[3, j] = g[j]

    adjoint_end()
    _, got_bx = exchange(EC.at[3], BXX, X)
    rs_pass_y(U_2)
    got_bx.wait_recv()
    scan_round_x(EC.at[3], BXX, EC.at[4], PIN, x == 0)
    _, got_by = exchange(EC.at[4], BXY, Y)
    rs_pass_y(U_1)
    got_by.wait_recv()
    scan_round_y(EC.at[4], BXY, EC.at[5], PIN, y == 0, 1 - x)
    got_bz = [
        exchange(EC.at[5], BXZ.at[k - 1], (ahead(NZ - k), b))[1] for k in range(1, NZ)
    ]
    rs_pass_x(U_P)

    def block_out_one(i, carry):
        rows = rows_of(i, 32)
        o_block[rows, :] = (FO[rows, :] + (reduced(AS, AR, OXR, i) + f2b[...])).astype(BF)
        return carry

    lax.fori_loop(0, 4, block_out_one, 0)
    for got in got_bz:
        got.wait_recv()
    scan_round_z(BXZ, PIN, NZ - 1 - z, 2 * (1 - y) + 1 - x)

    def backward_scan():
        for part in range(2):
            js = range(8 * part, 8 * part + 8)
            d = [DEC[j] for j in js]
            c = [CIN[j] for j in js]
            e = [EMA_SCALE * CIN[j] * ema[3, j] for j in js]

            def group(i, carry):
                at = 15 - i
                h = tuple(HC[at, j] for j in js)
                for u in range(8):
                    for n in range(8):
                        H8[u, n] = h[n]
                    if u < 7:
                        row = XP[panel(8 * at + u), :]
                        h = tuple(h[n] * d[n] + c[n] * row for n in range(8))
                g, s1, m = carry
                for u in range(7, -1, -1):
                    t = 8 * at + u
                    row = XP[panel(t), :]
                    ge = GEP[panel(t), :]
                    g = tuple(g[n] * d[n] + ge for n in range(8))
                    s1 = tuple(s1[n] + row * g[n] for n in range(8))
                    m = tuple(m[n] + g[n] * H8[u, n] for n in range(8))
                    out = e[0] * g[0]
                    for n in range(1, 8):
                        out = out + e[n] * g[n]
                    if part == 0:
                        out = out + om[...] * ge
                    else:
                        out = out + GNP[panel(t), :]
                    GNP[panel(t), :] = out
                return g, s1, m

            zeros = tuple(jnp.zeros((8, 128), F32) for _ in range(8))
            _, s1, m = lax.fori_loop(0, 16, group, (tuple(PIN[j] for j in js), zeros, zeros))
            for n, j in enumerate(js):
                SM_OUT[8 * j : 8 * j + 8, :] = s1[n]
                SM_OUT[128 + 8 * j : 128 + 8 * j + 8, :] = m[n]

    backward_scan()

    for g in range(8):
        rows = slice(128 * g, 128 * g + 128)
        SM_OUT[ROW_OMEGA + g : ROW_OMEGA + g + 1, :] = jnp.sum(
            fold8(XP[rows, :] * GEP[rows, :]), axis=0, keepdims=True
        )

    got_gnv.wait_recv()

    def back_one(i, carry):
        rows = rows_of(i, 32)
        wide = jnp.concatenate(
            [GNP[pl.ds(al(128 * g + 32 * i, 32), 32), :] for g in range(8)], axis=1
        )
        a = (GNV[pl.ds(al(128 * b + 32 * i, 32), 32), :] + GNVR[1, rows, :]) + wide
        n, rstd = norm_rows(tok[rows, :].astype(F32))
        g = a * n1g[...]
        back = (
            g - jnp.mean(g, axis=-1, keepdims=True) - n * jnp.mean(g * n, axis=-1, keepdims=True)
        ) * rstd
        o_tok[rows, :] = (PR[rows, :] + back).astype(BF)
        return carry[0] + fold8(a * n), carry[1] + fold8(a)

    sums = lax.fori_loop(0, 4, back_one, (zero8, zero8))
    for row, acc in zip((ROW_N1G, ROW_N1B), sums):
        store_row(row, jnp.sum(acc, axis=0, keepdims=True))

    half_rows = SM_ROWS // 2
    my_part = rows_of(b, half_rows)
    their_part = rows_of(1 - b, half_rows)
    copy_c, got_c = exchange(SM_OUT.at[their_part], SMR, C)
    rs_pass_x(U_BA)
    got_c.wait_recv()
    SMX[0] = SM_OUT[my_part, :] + SMR[...]
    _, got_sx = exchange(SMX.at[0], SMX.at[1], X)
    rs_pass_y(U_P)
    got_sx.wait_recv()
    SMY[0] = SMX[0] + SMX[1]
    _, got_sy = exchange(SMY.at[0], SMY.at[1], Y)
    rs_pass_y(U_BA)
    got_sy.wait_recv()
    SMZ[0] = SMY[0] + SMY[1]
    got_sz = [exchange(SMZ.at[0], SMZ.at[k], (ahead(k), b))[1] for k in range(1, NZ)]
    rs_pass_x(U_BB)
    rs_pass_x(U_V)
    for got in got_sz:
        got.wait_recv()
    total = SMZ[lax.rem(z, NZ)]
    for k in range(1, NZ):
        total = total + SMZ[lax.rem(z + NZ - k, NZ)]
    SM_OUT[my_part, :] = total
    _, got_cc = exchange(SM_OUT.at[my_part], SMC, C)

    rs_pass_y(U_BB)
    rs_pass_y(U_V)
    rs_wait_z(U_2)
    for i in range(4):
        o_d2[32 * i : 32 * i + 32, :] = rs_total(U_2, (32 * i, 32))
    rs_wait_z(U_1)
    for i in range(4):
        o_d1[:, 1024 * i : 1024 * i + 1024] = rs_total(U_1, (32 * i, 32))
    quarter = lambda j: pl.ds(al(1024 * j, 1024), 1024)
    d1_pairs = [
        exchange(o_d1.at[:, quarter(j)], FX1.at[q], device, FX1.at[j])
        for j, device in ((q_c, C), (q_x, X), (q_xc, XC))
    ]
    rs_wait_z(U_P)
    for i in range(2):
        o_dp[32 * i : 32 * i + 32, :] = rs_total(U_P, (32 * i, 32))
    mine32 = 32 * b
    their32 = 32 * (1 - b)
    h_mine = pl.ds(al(3200 + 512 * b, 128), 512)
    h_their = pl.ds(al(3200 + 512 * (1 - b), 128), 512)
    low = low1(32)

    def merge(out, start, own_half, other_half):
        for t in range(8):
            cols = slice(128 * t, 128 * t + 128)
            m, o = own_half[:, cols], other_half[:, cols]
            lo, hi = pick(first, m, o), pick(first, o, m)
            at = start + 256 * t
            out[:, at : at + 128] = jnp.where(low, lo, pltpu.roll(hi, 64, 1))
            out[:, at + 128 : at + 256] = jnp.where(low, pltpu.roll(lo, 64, 1), hi)

    rs_wait_z(U_BA)
    FB[:, 0:1024] = rs_total(U_BA, (their32, 32))
    _, got_ba = exchange(FB.at[:, 0:1024], FXB.at[:, 0:1024], C)
    part = rs_total(U_BA, (mine32, 32))
    o_db[:, my_cols] = part[:, 0:512]
    o_db[:, h_mine] = part[:, 512:1024]
    rs_wait_z(U_BB)
    FB[:, 1024:2176] = rs_total(U_BB, (their32, 32))
    _, got_bb = exchange(FB.at[:, 1024:2176], FXB.at[:, 1024:2176], C)
    part = rs_total(U_BB, (mine32, 32))
    o_db[:, 1024:1152] = part[:, 0:128]
    rs_wait_z(U_V)
    FV[...] = rs_total(U_V, (their32, 32))
    _, got_v = exchange(FV, FXV, C)
    part_v = rs_total(U_V, (mine32, 32))

    FX1[q] = o_d1[:, quarter(q)]
    for copy, got in d1_pairs:
        copy.wait_send()
        settle(copy)
        got.wait_recv()
    for j in range(4):
        for t in range(8):
            o_d1[:, 128 * (4 * t + j) : 128 * (4 * t + j) + 128] = FX1[j, :, 128 * t : 128 * t + 128]

    copy_c.wait_send()
    settle(copy_c)
    got_cc.wait_recv()
    SM_OUT[their_part, :] = SMC[...]
    for j in range(NDIM):
        rate, damping = sig(ema[0, j]), sig(ema[1, j])
        beta, gamma = ema[2, j], EMA_SCALE * ema[3, j]
        s1 = SM_OUT[8 * j : 8 * j + 8, :]
        m = gamma * SM_OUT[128 + 8 * j : 136 + 8 * j, :]
        o_ema[0, j] = (beta * gamma * s1 - damping * m) * rate * (1.0 - rate)
        o_ema[1, j] = -rate * m * damping * (1.0 - damping)
        o_ema[2, j] = gamma * rate * s1
        o_ema[3, j] = EMA_SCALE * rate * beta * s1

    got_ba.wait_recv()
    o_db[:, their_cols] = FXB[:, 0:512]
    o_db[:, h_their] = FXB[:, 512:1024]
    got_bb.wait_recv()
    merge(o_db, 1152, part[:, 128:1152], FXB[:, 1152:2176])
    got_v.wait_recv()
    merge(o_dv, 0, part_v, FXV[...])

    for copy in open_sends:
        copy.wait_send()
    for w in (VALUE, BASE, PROJ):
        close_gather(w)

    def close_sums(u):
        def one(k, carry):
            rs_y(u, k).wait_send()
            if u < U_1:
                rs_x(u, k, 0).wait_send()
                rs_x(u, k, 1).wait_send()
            return carry

        lax.fori_loop(0, NZ, one, 0)

        def plane(k, carry):
            rs_z(u, k).wait_send()
            return carry

        lax.fori_loop(1, NZ, plane, 0)

    for u in (U_V, U_P, U_BA, U_BB, U_1, U_2):
        close_sums(u)


def fast_shards(
    tokens,
    out_grad,
    norm1_gain,
    norm1_bias,
    value_weight,
    value_bias,
    ema_delta,
    ema_alpha,
    ema_beta,
    ema_gamma,
    ema_omega,
    base_weight,
    base_bias,
    shared_gamma,
    query_offset,
    position_bias,
    proj_weight,
    proj_bias,
    norm2_gain,
    norm2_bias,
    ffn1_weight,
    ffn1_bias,
    ffn2_weight,
    ffn2_bias,
):
    NS = lax.axis_size("seq")
    NZ = NS // 4
    row = lambda v: v.reshape(1, -1)
    ema = (
        jnp.stack([ema_delta, ema_alpha, ema_beta, ema_gamma])
        .transpose(0, 2, 1)
        .reshape(4, NDIM, 8, 128)
    )
    backward_bias = jnp.concatenate([position_bias[:1], position_bias[:0:-1]])
    small = [
        tokens[0], out_grad[0], row(norm1_gain), row(norm1_bias), row(value_bias), ema,
        ema_omega.reshape(8, 128), row(base_bias), shared_gamma, row(query_offset),
        row(backward_bias), row(proj_bias), row(norm2_gain), row(norm2_bias), row(ffn1_bias),
        row(ffn2_bias),
    ]
    large = [value_weight, base_weight, proj_weight, ffn1_weight, ffn2_weight]
    f = lambda *shape: jax.ShapeDtypeStruct(shape, F32)
    h = lambda *shape: jax.ShapeDtypeStruct(shape, BF)
    outs = [
        h(128, 1024), h(128, 1024), f(32, 2048), f(32, 4224), f(64, 1024), f(32, 4096), f(128, 1024),
        f(SM_ROWS, 128), f(4, NDIM, 8, 128),
    ]
    vm = lambda *shape: pltpu.VMEM(shape, BF)
    vf = lambda *shape: pltpu.VMEM(shape, F32)
    dma = lambda *shape: pltpu.SemaphoreType.DMA(shape)
    scratch = [
        vm(1024, 1024), vm(1024, BASE_COLS), vm(1024, 1024), vm(1024, 1024), vm(1024, 1024),
        vm(1024, 1024), vm(1024, 1024), vm(1024, 1024), vm(1024, 1152), vm(512, 1152),
        vm(NZ, 64, 1024), vm(NZ, 64, 1024), vm(NZ, 64, 1024), vm(NZ, 64, 1152),
        vm(NZ, 128, 1024), vm(NZ, 128, 1024),
        vm(NZ - 1, 64, 1024), vm(NZ - 1, 64, 1024), vm(NZ - 1, 64, 1024), vm(NZ - 1, 64, 1152),
        vm(NZ - 1, 128, 1024), vm(NZ - 1, 128, 1024),
        vf(32, 1024), vf(32, BASE_COLS), vf(32, 1024), vf(32, BASE_COLS), vf(4, 32, 1024),
        vm(32, 1024), vm(32, BASE_COLS), vm(256, 1024), vm(256, 1024), vm(1024, 1024),
        vm(256, 1024), vm(256, 1024), vf(256, 1024), vf(128, 1024), vf(128, 1024), vf(256, 128),
        vm(256, 1024), vm(256, 1024), vm(256, 1024), vf(256, 128), vf(128, 1024), vf(128, 1024),
        vf(512, 1024), vm(1024, 1024),
        vm(512, 1024), vm(256, 1024), vm(128, 1024), vm(128, 1024), vm(128, 1024),
        vm(256, 1024), vm(128, 1024), vm(256, BASE_COLS), vm(256, 1024), vf(256, 128), vf(256, 128),
        vm(256, 1024), vf(2, 128, 1024),
        vf(1024, 128), vf(1024, 128), vf(1024, 128), vf(1024, 128), vf(16, NDIM, 8, 128), vf(8, 8, 8, 128),
        vf(6, NDIM, 8, 128), vf(NDIM, 8, 128), vf(NDIM, 8, 128), vf(NZ - 1, NDIM, 8, 128),
        vf(NDIM, 8, 128), vf(NDIM, 8, 128), vf(NZ - 1, NDIM, 8, 128),
        vf(NDIM, 8, 128), vf(NDIM, 8, 128), vf(NDIM, 8, 128), vf(NDIM, 8, 128),
        vf(SM_ROWS // 2, 128), vf(2, SM_ROWS // 2, 128), vf(2, SM_ROWS // 2, 128),
        vf(NZ, SM_ROWS // 2, 128), vf(SM_ROWS // 2, 128),
        dma(5), dma(5, NZ), dma(5, NZ), dma(5, NZ), dma(5, NZ), dma(3, 2, NZ), dma(3, 2, NZ),
        dma(4, NZ, 2), dma(4, NZ, 2), dma(6, NZ), dma(6, NZ), dma(6, NZ), dma(6, NZ), dma(64), dma(64),
    ]
    (block_out, tokens_grad, dvalue, dbase, dproj, dffn1, dffn2, sums, dema) = pl.pallas_call(
        functools.partial(layer_kernel, NS),
        out_shape=outs,
        in_specs=[pl.BlockSpec(memory_space=pltpu.VMEM)] * len(small)
        + [pl.BlockSpec(memory_space=pl.ANY)] * len(large),
        out_specs=[pl.BlockSpec(memory_space=pltpu.VMEM)] * len(outs),
        scratch_shapes=scratch,
        compiler_params=pltpu.CompilerParams(
            collective_id=0, has_side_effects=True, vmem_limit_bytes=VMEM_LIMIT
        ),
    )(*small, *large)
    dema = dema.reshape(4, NDIM, D).transpose(0, 2, 1)
    span = lambda at, n: sums[at : at + n].reshape(-1)
    dpos = span(ROW_POS, 1)
    dposition = jnp.concatenate([dpos[:1], dpos[:0:-1]])
    return (
        block_out[None],
        tokens_grad[None],
        span(ROW_N1G, 8),
        span(ROW_N1B, 8),
        dvalue,
        span(ROW_VB, 16),
        dema[0],
        dema[1],
        dema[2],
        dema[3],
        span(ROW_OMEGA, 8),
        dbase,
        span(ROW_BB, 33),
        sums[ROW_SG : ROW_SG + 2],
        span(ROW_QO, 1),
        dposition,
        dproj,
        span(ROW_PB, 8),
        span(ROW_N2G, 8),
        span(ROW_N2B, 8),
        dffn1,
        span(ROW_F1B, 32),
        dffn2,
        span(ROW_F2B, 8),
    )


def solution(mesh):
    in_specs = (
        P("batch", "seq", None),
        P("batch", "seq", None),
        P(),
        P(),
        P(("seq", "batch"), None),
        P(),
        P(),
        P(),
        P(),
        P(),
        P(),
        P(("seq", "batch"), None),
        P(),
        P(),
        P(),
        P(),
        P(("seq", "batch"), None),
        P(),
        P(),
        P(),
        P(("seq", "batch"), None),
        P(),
        P(("seq", "batch"), None),
        P(),
    )
    out_specs = (
        P("batch", "seq", None),
        P("batch", "seq", None),
        P(),
        P(),
        P(("seq", "batch"), None),
        P(),
        P(),
        P(),
        P(),
        P(),
        P(),
        P(("seq", "batch"), None),
        P(),
        P(),
        P(),
        P(),
        P(("seq", "batch"), None),
        P(),
        P(),
        P(),
        P(("seq", "batch"), None),
        P(),
        P(("seq", "batch"), None),
        P(),
    )
    one_device = fast_shards if mesh.shape['seq'] == 16 else shards
    return jax.shard_map(
        one_device, mesh=mesh, in_specs=in_specs, out_specs=out_specs, check_vma=False
    )
```

```python
import functools

import jax
import jax.numpy as jnp
from jax import lax
from jax.experimental import pallas as pl
from jax.experimental.pallas import tpu as pltpu
from jax.sharding import PartitionSpec as P

D = 1024
ZD = 128
VD = 2048
NDIM = 16


precise = lax.Precision.HIGHEST


def entering(part, axis, combine, identity):
    place = lax.axis_index(axis)
    gathered = jax.tree.map(lambda a: lax.all_gather(a, axis), part)
    state = jax.tree.map(lambda a, e: jnp.zeros_like(a) + jnp.asarray(e, a.dtype), part, identity)

    def one(step, state):
        return combine(
            state, jax.tree.map(lambda a: lax.dynamic_index_in_dim(a, step, 0, False), gathered)
        )

    return lax.fori_loop(0, place, one, state)


def prefix_2(value, axis, combine, identity):
    size, index = (lax.axis_size(axis), lax.axis_index(axis))
    everything = jax.tree.map(
        lambda part, kind: lax.all_gather(part.astype(kind), axis),
        value,
        jax.tree.map(lambda a: jnp.bfloat16 if a.dtype == jnp.float32 else a.dtype, value),
    )
    start = jax.tree.map(
        lambda part, zero: jnp.broadcast_to(jnp.asarray(zero, part.dtype), part.shape),
        value,
        identity,
    )

    def step(k, before):
        at = size - 1 - k
        reached = at > index
        new = combine(
            before, jax.tree.map(lambda part, own: part[at].astype(own.dtype), everything, value)
        )
        return jax.tree.map(lambda a, b: jnp.where(reached, a, b), new, before)

    return lax.fori_loop(0, size, step, start)


def layer_norm(values, norm_gain, norm_bias):
    center = values - jnp.mean(values, axis=-1, keepdims=True)
    spread = jnp.mean(center * center, axis=-1, keepdims=True)
    return center * lax.rsqrt(spread + 1e-05) * norm_gain + norm_bias


def decay_tables(delta, alpha):
    input_rate = jax.nn.sigmoid(delta)
    damping = jax.nn.sigmoid(alpha)
    return (input_rate, jnp.log1p(-input_rate * damping))


def toeplitz_rows(kern_part):
    chans = kern_part.shape[0]
    block_len = kern_part.shape[1]
    wrapped = jnp.concatenate(
        [kern_part[:, :1], jnp.zeros((chans, block_len), kern_part.dtype), kern_part[:, :0:-1]],
        axis=1,
    )
    tiled = jnp.tile(wrapped, (1, block_len))[:, : block_len * (2 * block_len - 1)]
    return tiled.reshape(chans, block_len, 2 * block_len - 1)[:, :, :block_len]


def local_conv(normed3, kernel):
    block_len = normed3.shape[1]
    blocks = normed3.shape[2] // 128
    kern_blocks = kernel.reshape(blocks, 128, block_len)
    data_blocks = normed3.reshape(normed3.shape[0], block_len, blocks, 128).transpose(2, 0, 1, 3)

    def one_block(block_pair):
        kern_part, data_part = block_pair
        toeplitz = toeplitz_rows(kern_part)
        return jnp.einsum("dts,bsd->btd", toeplitz, data_part, precision=precise)

    result = lax.map(one_block, (kern_blocks, data_blocks))
    return result.transpose(1, 2, 0, 3).reshape(normed3.shape)


def ema_terms(normed3, delta, alpha, beta, gamma, omega, incoming):
    block_len = normed3.shape[1]
    input_rate, log_decay = decay_tables(delta, alpha)
    step_index = jnp.arange(block_len, dtype=jnp.float32)
    ema_scale = NDIM ** (-0.5)
    powers = jnp.exp(log_decay[:, :, None] * step_index)
    kernel = ema_scale * jnp.einsum(
        "dj,djk->dk", gamma * input_rate * beta, powers, precision=precise
    )
    convolved = local_conv(normed3, kernel)
    carry_table = (
        ema_scale * gamma[:, :, None] * jnp.exp(log_decay[:, :, None] * (step_index + 1.0))
    )
    carried = jnp.einsum("djt,bdj->btd", carry_table, incoming, precision=precise)
    return convolved + carried + omega * normed3


def ema_ends(normed3, delta, alpha, beta):
    block_len = normed3.shape[1]
    input_rate, log_decay = decay_tables(delta, alpha)
    step_index = jnp.arange(block_len, dtype=jnp.float32)
    end_table = (input_rate * beta)[:, :, None] * jnp.exp(
        log_decay[:, :, None] * (block_len - 1.0 - step_index)
    )
    end_states = jnp.einsum("djs,bsd->bdj", end_table, normed3, precision=precise)
    return (jnp.exp(log_decay * block_len), end_states)


def rel_table(position_bias):
    step_index = jnp.arange(position_bias.shape[0])
    offsets = step_index[:, None] - step_index[None, :]
    return jnp.where(offsets >= 0, position_bias[jnp.maximum(offsets, 0)], 0.0)


def masked_softmax(scores):
    step_index = jnp.arange(scores.shape[-1])
    causal = step_index[:, None] >= step_index[None, :]
    masked = jnp.where(causal, scores, -jnp.inf)
    row_top = jnp.max(masked, axis=-1, keepdims=True)
    expo_vals = jnp.exp(masked - row_top)
    return expo_vals / jnp.sum(expo_vals, axis=-1, keepdims=True)


def silu_slope(values):
    logistic = jax.nn.sigmoid(values)
    return logistic * (1.0 + values * (1.0 - logistic))


def matmul(left_mat, right_mat):
    return jnp.dot(left_mat, right_mat, preferred_element_type=jnp.float32)


def left_product(left_mat, right_mat):
    return lax.dot_general(
        left_mat, right_mat, (((0,), (0,)), ((), ())), preferred_element_type=jnp.float32
    )


def right_product(left_mat, right_mat):
    return lax.dot_general(
        left_mat, right_mat, (((1,), (1,)), ((), ())), preferred_element_type=jnp.float32
    )


def column_sums(values):
    return jnp.sum(values.astype(jnp.float32), axis=0)


def shards(
    tokens,
    out_grad,
    norm1_gain,
    norm1_bias,
    value_weight,
    value_bias,
    ema_delta,
    ema_alpha,
    ema_beta,
    ema_gamma,
    ema_omega,
    base_weight,
    base_bias,
    shared_gamma,
    query_offset,
    position_bias,
    proj_weight,
    proj_bias,
    norm2_gain,
    norm2_bias,
    ffn1_weight,
    ffn1_bias,
    ffn2_weight,
    ffn2_bias,
):
    seq_local, block_len, _ = tokens.shape
    row_count = seq_local * block_len
    gathered = (
        lax.all_gather(value_weight.astype(jnp.bfloat16), ("seq", "batch"), axis=0, tiled=True),
        lax.all_gather(base_weight.astype(jnp.bfloat16), ("seq", "batch"), axis=0, tiled=True),
        lax.all_gather(proj_weight.astype(jnp.bfloat16), ("seq", "batch"), axis=0, tiled=True),
        lax.all_gather(ffn1_weight.astype(jnp.bfloat16), ("seq", "batch"), axis=0, tiled=True),
        lax.all_gather(ffn2_weight.astype(jnp.bfloat16), ("seq", "batch"), axis=0, tiled=True),
    )
    value_full, base_full, proj_full, ffn1_full, ffn2_full = gathered
    _, log_decay = decay_tables(ema_delta, ema_alpha)
    block_log = log_decay * block_len

    def chain_step(earlier_pair, later_pair):
        carried = earlier_pair[1] * jnp.exp(block_log * later_pair[0][0])
        return (earlier_pair[0] + later_pair[0], carried + later_pair[1])

    one_block = jnp.ones((1,), jnp.float32)
    no_block = jnp.zeros((1,), jnp.float32)
    tokens_flat = tokens.astype(jnp.float32).reshape(row_count, D)
    normed, norm1_back = jax.vjp(layer_norm, tokens_flat, norm1_gain, norm1_bias)
    normed_low = normed.astype(jnp.bfloat16)
    value_pre = matmul(normed_low, value_full) + value_bias
    value_low = jax.nn.silu(value_pre).astype(jnp.bfloat16)
    normed3 = normed.reshape(seq_local, block_len, D)
    (whole_decay, end_states), ends_back = jax.vjp(
        ema_ends, normed3, ema_delta, ema_alpha, ema_beta
    )
    prefix = entering(
        (one_block, end_states), "seq", chain_step, (no_block, jnp.zeros_like(end_states))
    )
    incoming = prefix[1]
    ema_out, ema_back = jax.vjp(
        ema_terms, normed3, ema_delta, ema_alpha, ema_beta, ema_gamma, ema_omega, incoming
    )
    ema_flat = ema_out.reshape(row_count, D)
    mixed_low = jax.nn.silu(ema_flat).astype(jnp.bfloat16)
    base_pre = matmul(mixed_low, base_full) + base_bias
    update = jax.nn.sigmoid(base_pre[:, :D])
    shared_pre = base_pre[:, D : D + ZD + VD]
    shared_reset = jax.nn.silu(shared_pre)
    shared = shared_reset[:, :ZD]
    reset_gate = shared_reset[:, ZD:]
    hidden_x = base_pre[:, D + ZD + VD :]
    queries = (
        (shared * shared_gamma[0] + query_offset)
        .astype(jnp.bfloat16)
        .reshape(seq_local, block_len, ZD)
    )
    key_rows = (shared * shared_gamma[1]).astype(jnp.bfloat16).reshape(seq_local, block_len, ZD)
    position, position_back = jax.vjp(rel_table, position_bias)
    scores = (
        jnp.einsum("bik,bjk->bij", queries, key_rows, preferred_element_type=jnp.float32)
        * ZD ** (-0.5)
        + position
    )
    attn = masked_softmax(scores)
    attn_low = attn.astype(jnp.bfloat16)
    values3 = value_low.reshape(seq_local, block_len, VD)
    attended = jnp.einsum(
        "bij,bjv->biv", attn_low, values3, preferred_element_type=jnp.float32
    ).reshape(row_count, VD)
    gated_low = (attended * reset_gate).astype(jnp.bfloat16)
    proj_pre = matmul(gated_low, proj_full) + proj_bias
    hidden_sum = hidden_x + proj_pre
    hidden = jax.nn.silu(hidden_sum)
    first_out = tokens_flat + update * (hidden - tokens_flat)
    normed_two, norm2_back = jax.vjp(layer_norm, first_out, norm2_gain, norm2_bias)
    normed_two_low = normed_two.astype(jnp.bfloat16)
    ffn_pre = matmul(normed_two_low, ffn1_full) + ffn1_bias
    ffn_low = jax.nn.silu(ffn_pre).astype(jnp.bfloat16)
    ffn_out = matmul(ffn_low, ffn2_full) + ffn2_bias
    block_out = (first_out + ffn_out).astype(jnp.bfloat16).reshape(seq_local, block_len, D)
    grad_ffn2 = out_grad.reshape(row_count, D)
    dffn2_weight = left_product(ffn_low, grad_ffn2)
    dffn2_bias = column_sums(grad_ffn2)
    grad_ffn1 = (right_product(grad_ffn2, ffn2_full) * silu_slope(ffn_pre)).astype(jnp.bfloat16)
    dffn1_weight = left_product(normed_two_low, grad_ffn1)
    dffn1_bias = column_sums(grad_ffn1)
    grad_first_norm, dnorm2_gain, dnorm2_bias = norm2_back(right_product(grad_ffn1, ffn1_full))
    grad_first = grad_ffn2.astype(jnp.float32) + grad_first_norm
    grad_skip = grad_first * (1.0 - update)
    grad_update = grad_first * (hidden - tokens_flat)
    grad_hidden = grad_first * update * silu_slope(hidden_sum)
    grad_proj = grad_hidden.astype(jnp.bfloat16)
    dproj_weight = left_product(gated_low, grad_proj)
    dproj_bias = column_sums(grad_proj)
    grad_gated = right_product(grad_proj, proj_full)
    grad_attended = (grad_gated * reset_gate).astype(jnp.bfloat16).reshape(seq_local, block_len, VD)
    grad_reset = grad_gated * attended
    grad_attn = jnp.einsum(
        "biv,bjv->bij", grad_attended, values3, preferred_element_type=jnp.float32
    )
    grad_values = jnp.einsum(
        "bij,biv->bjv", attn_low, grad_attended, preferred_element_type=jnp.float32
    ).reshape(row_count, VD)
    grad_scores = (attn * (grad_attn - jnp.sum(grad_attn * attn, axis=-1, keepdims=True))).astype(
        jnp.bfloat16
    )
    (dposition_bias,) = position_back(jnp.sum(grad_scores.astype(jnp.float32), axis=0))
    grad_queries = jnp.einsum(
        "bij,bjk->bik", grad_scores, key_rows, preferred_element_type=jnp.float32
    ).reshape(row_count, ZD) * ZD ** (-0.5)
    grad_keys = jnp.einsum(
        "bij,bik->bjk", grad_scores, queries, preferred_element_type=jnp.float32
    ).reshape(row_count, ZD) * ZD ** (-0.5)
    dshared_gamma = jnp.stack(
        [jnp.sum(grad_queries * shared, axis=0), jnp.sum(grad_keys * shared, axis=0)]
    )
    dquery_offset = jnp.sum(grad_queries, axis=0)
    grad_shared = grad_queries * shared_gamma[0] + grad_keys * shared_gamma[1]
    grad_shared_pre = jnp.concatenate([grad_shared, grad_reset], axis=1) * silu_slope(shared_pre)
    grad_update_pre = grad_update * update * (1.0 - update)
    grad_base = jnp.concatenate([grad_update_pre, grad_shared_pre, grad_hidden], axis=1).astype(
        jnp.bfloat16
    )
    dbase_weight = left_product(mixed_low, grad_base)
    dbase_bias = column_sums(grad_base)
    grad_ema = right_product(grad_base, base_full) * silu_slope(ema_flat)
    grad_value_pre = (grad_values * silu_slope(value_pre)).astype(jnp.bfloat16)
    dvalue_weight = left_product(normed_low, grad_value_pre)
    dvalue_bias = column_sums(grad_value_pre)
    grad_normed = right_product(grad_value_pre, value_full)
    grad_normed_ema, delta_part, alpha_part, beta_part, dema_gamma, dema_omega, grad_incoming = (
        ema_back(grad_ema.reshape(seq_local, block_len, D))
    )
    suffix = prefix_2(
        (one_block, grad_incoming), "seq", chain_step, (no_block, jnp.zeros_like(grad_incoming))
    )
    grad_ends = suffix[1]
    grad_whole = jnp.sum(grad_ends * incoming, axis=0)
    grad_normed_ends, delta_rest, alpha_rest, beta_rest = ends_back((grad_whole, grad_ends))
    dema_delta = delta_part + delta_rest
    dema_alpha = alpha_part + alpha_rest
    dema_beta = beta_part + beta_rest
    grad_normed = grad_normed + (grad_normed_ema + grad_normed_ends).reshape(row_count, D)
    grad_tokens_norm, dnorm1_gain, dnorm1_bias = norm1_back(grad_normed)
    tokens_grad = (
        (grad_skip + grad_tokens_norm).astype(jnp.bfloat16).reshape(seq_local, block_len, D)
    )
    small_sums = lax.psum(
        (
            dnorm1_gain,
            dnorm1_bias,
            dvalue_bias,
            dema_delta,
            dema_alpha,
            dema_beta,
            dema_gamma,
            dema_omega,
            dbase_bias,
            dshared_gamma,
            dquery_offset,
            dposition_bias,
            dproj_bias,
            dnorm2_gain,
            dnorm2_bias,
            dffn1_bias,
            dffn2_bias,
        ),
        ("seq", "batch"),
    )
    reduced = (
        lax.psum_scatter(dvalue_weight, ("seq", "batch"), scatter_dimension=0, tiled=True),
        lax.psum_scatter(dbase_weight, ("seq", "batch"), scatter_dimension=0, tiled=True),
        lax.psum_scatter(dproj_weight, ("seq", "batch"), scatter_dimension=0, tiled=True),
        lax.psum_scatter(dffn1_weight, ("seq", "batch"), scatter_dimension=0, tiled=True),
        lax.psum_scatter(dffn2_weight, ("seq", "batch"), scatter_dimension=0, tiled=True),
    )
    return (
        block_out,
        tokens_grad,
        small_sums[0],
        small_sums[1],
        reduced[0],
        small_sums[2],
        small_sums[3],
        small_sums[4],
        small_sums[5],
        small_sums[6],
        small_sums[7],
        reduced[1],
        small_sums[8],
        small_sums[9],
        small_sums[10],
        small_sums[11],
        reduced[2],
        small_sums[12],
        small_sums[13],
        small_sums[14],
        reduced[3],
        small_sums[15],
        reduced[4],
        small_sums[16],
    )


VMEM_LIMIT = 63 * 1024 * 1024
BF = jnp.bfloat16
F32 = jnp.float32
MESH = pl.DeviceIdType.MESH
SCALE = ZD ** (-0.5)
EMA_SCALE = NDIM ** (-0.5)
BLK = 128
VH = 1024
BASE_COLS = 2176
SM_ROWS = 400
ROW_OMEGA, ROW_N1G, ROW_N1B, ROW_N2G, ROW_N2B = 256, 264, 272, 280, 288
ROW_VB, ROW_BB, ROW_PB, ROW_F1B, ROW_F2B = 296, 312, 345, 353, 385
ROW_SG, ROW_QO, ROW_POS = 393, 395, 396
SMALL_ROWS = (
    (ROW_N1G, 8), (ROW_N1B, 8), (ROW_VB, 16), (ROW_OMEGA, 8), (ROW_BB, 33), (ROW_SG, 2), (ROW_QO, 1),
    (ROW_POS, 1), (ROW_PB, 8), (ROW_N2G, 8), (ROW_N2B, 8), (ROW_F1B, 32), (ROW_F2B, 8),
)
VALUE, BASE, PROJ, FFN1, FFN2 = range(5)
U_V, U_P, U_BA, U_BB, U_1, U_2 = range(6)
Y_FIRST = (U_V,)


def pick(flag, yes, no):
    return lax.select(flag, yes, no)


def sig(v):
    return jax.nn.sigmoid(v)


def silu(v):
    return v * sig(v)


def slope(v):
    s = sig(v)
    return s * (1.0 + v * (1.0 - s))


def dot_nn(a, b):
    return jnp.dot(a, b, preferred_element_type=F32)


def dot_nt(a, b):
    return lax.dot_general(a, b, (((1,), (1,)), ((), ())), preferred_element_type=F32)


def dot_tn(a, b):
    return lax.dot_general(a, b, (((0,), (0,)), ((), ())), preferred_element_type=F32)


def split_pair(first, second, low_lanes):
    lo = jnp.where(low_lanes, first, pltpu.roll(second, 64, 1))
    hi = jnp.where(low_lanes, pltpu.roll(first, 64, 1), second)
    return lo, hi


def fold8(v):
    rows, cols = v.shape
    return jnp.sum(v.reshape(rows // 8, 8, cols), axis=0)


def shear(v, left):
    rows = lax.broadcasted_iota(jnp.int32, (BLK, BLK), 0)
    for bit in range(7):
        step = 1 << bit
        turned = pltpu.roll(v, BLK - step if left else step, 1)
        v = jnp.where((rows & step) != 0, turned, v)
    return v


def layer_kernel(NS, *refs):
    NZ = NS // 4
    names = iter(refs)
    take = lambda n: [next(names) for _ in range(n)]
    (tok, og, n1g, n1b, vb) = take(5)
    ema_in = take(4)
    (om_in, bb, sg, qo, pbr, pbias, n2g, n2b, f1b, f2b) = take(10)
    (vw, bw, pw, f1w, f2w) = take(5)
    (o_block, o_tok, o_dv, o_db, o_dp, o_d1, o_d2, o_ema, o_sm) = take(9)
    (SM_OUT, ema, om) = take(3)
    (WV, WB, WP, W1, W2) = take(5)
    (G1, G2, GBA, GBB, RXBB) = take(5)
    RY = take(6)
    RZ = take(6)
    (FV, FB, FXV, FXB, FX1) = take(5)
    (SV, SB, NL, ML, NO, VP, VL, UH, UU, HH, SHP, RP, AD, GT, AT, PR, FO, FP, FG) = take(19)
    (AS, AR, AX, AXR, OX, OXR, OB, GH, GUS, GBS, GA, GAT, GATR, GVP, GNVR) = take(15)
    (XP, YP, GEP, GNP, HC, H8, EC, EXX, EXY, EXZ, BXX, BXY, BXZ, DEC, CIN, LAM, PIN) = take(17)
    (SMR, SMX, SMY, SMZ, SMC) = take(5)
    (in_sem, zs, zr, ys, yr, xs, xr, rxs, rxr, rys, ryr, rzs, rzr, es, er) = take(15)

    s = lax.axis_index("seq")
    b = lax.axis_index("batch")
    x = lax.rem(s, 2)
    y = lax.rem(lax.div(s, 2), 2)
    z = lax.div(s, 4)
    p = lax.div(s, 2)
    q = 2 * x + b
    xs_ = s + 1 - 2 * x
    ys_ = s + 2 - 4 * y
    C = (s, 1 - b)
    X = (xs_, b)
    XC = (xs_, 1 - b)
    Y = (ys_, b)
    ahead = lambda k: lax.rem(s + 4 * k, NS)
    behind = lambda k: lax.rem(s - 4 * k + NS * 4, NS)
    first = b == 0
    al = pl.multiple_of
    rows_of = lambda i, n: pl.ds(al(i * n, n), n)

    loads = [
        pltpu.make_async_copy(src, dst, in_sem.at[i])
        for i, (src, dst) in enumerate(
            ((vw, o_dv), (bw, o_db), (pw, o_dp), (f1w, o_d1), (f2w, o_d2))
        )
    ]
    for load in loads:
        load.start()

    barrier = pltpu.get_barrier_semaphore()
    partners = [C, X, XC, Y] + [(ahead(k), b) for k in range(1, NZ)]
    for device in partners:
        pl.semaphore_signal(barrier, inc=1, device_id=device, device_id_type=MESH)

    def remote(src, dst, send, recv, device):
        return pltpu.make_async_remote_copy(
            src_ref=src, dst_ref=dst, send_sem=send, recv_sem=recv, device_id=device, device_id_type=MESH
        )

    open_sends = []

    def settle(copy):
        open_sends[:] = [other for other in open_sends if other is not copy]

    n_ex = [0]

    def exchange(src, dst, device, landed=None):
        i = n_ex[0]
        n_ex[0] += 1
        copy = remote(src, dst, es.at[i], er.at[i], device)
        copy.start()
        open_sends.append(copy)
        arrival = copy if landed is None else remote(src, landed, es.at[i], er.at[i], device)
        return copy, arrival

    low1 = lambda n: lax.broadcasted_iota(jnp.int32, (n, BLK), 1) < 64

    my_rows = pl.ds(al(64 * s + 32 * b, 32), 32)
    other_rows = pl.ds(al(64 * s + 32 * (1 - b), 32), 32)

    def split_columns(src, src0, blocks, mine_ref, mine_rows, dst0, other_ref):
        low = low1(32)
        for t in range(blocks):
            lo, hi = split_pair(
                src[:, src0 + 256 * t : src0 + 256 * t + 128],
                src[:, src0 + 256 * t + 128 : src0 + 256 * t + 256],
                low,
            )
            cols = slice(dst0 + 128 * t, dst0 + 128 * t + 128)
            mine_ref[mine_rows, cols] = pick(first, lo, hi).astype(BF)
            other_ref[:, cols] = pick(first, hi, lo).astype(BF)

    NT = NO.at[0:512]
    OG = NO.at[512:1024]
    quad = lambda j: rows_of(j, BLK)
    q_c = q + 1 - 2 * b
    q_x = lax.rem(q + 2, 4)
    q_xc = lax.rem(q_c + 2, 4)
    OG[quad(q), :] = og[...]
    loads[0].wait()
    split_columns(o_dv, 0, 8, WV, my_rows, 0, SV)
    pl.semaphore_wait(barrier, len(partners))
    _, got_wv = exchange(SV, WV.at[my_rows], C, WV.at[other_rows])
    gather = [WV, WB, WP, W1, W2]

    def piece(w, chip):
        if w < FFN1:
            return gather[w].at[rows_of(chip, 64)]
        return gather[w].at[rows_of(lax.div(chip, 2), 128)]

    chip_of = lambda plane: 4 * plane + lax.rem(s, 4)

    def send_z(w, plane, down):
        part = piece(w, chip_of(plane))
        device = (s - 4, b) if down else (s + 4, b)
        return remote(part, part, zs.at[w, plane, down], zr.at[w, plane], device)

    def send_y(w, plane):
        part = piece(w, chip_of(plane))
        return remote(part, part, ys.at[w, plane], yr.at[w, plane], Y)

    def got_y(w, plane):
        part = piece(w, chip_of(plane) + ys_ - s)
        return remote(part, part, ys.at[w, plane], yr.at[w, plane], Y)

    def send_x(w, plane, far):
        part = piece(w, chip_of(plane) + (ys_ - s if far else 0))
        return remote(part, part, xs.at[w, far, plane], xr.at[w, far, plane], X)

    def got_x(w, plane, far):
        part = piece(w, chip_of(plane) + (ys_ - s if far else 0) + xs_ - s)
        return remote(part, part, xs.at[w, far, plane], xr.at[w, far, plane], X)

    def near_planes(visit):
        for j in range(1, NZ):
            pl.when(z >= j)(functools.partial(visit, z - j, 0, z < NZ - 1))
            pl.when(z + j <= NZ - 1)(functools.partial(visit, z + j, 1, z > 0))

    def open_gather(w):
        pl.when(z < NZ - 1)(lambda: send_z(w, z, 0).start())
        pl.when(z > 0)(lambda: send_z(w, z, 1).start())
        send_y(w, z).start()
        if w < FFN1:
            send_x(w, z, 0).start()

    def relay_z(w):
        def visit(plane, down, more):
            part = piece(w, chip_of(plane))
            remote(part, part, zs.at[w, plane, down], zr.at[w, plane], Y).wait_recv()
            pl.when(more)(lambda: send_z(w, plane, down).start())
            send_y(w, plane).start()
            if w < FFN1:
                send_x(w, plane, 0).start()

        near_planes(visit)

    def relay_y(w):
        def visit(plane, down, more):
            got_y(w, plane).wait_recv()
            if w < FFN1:
                send_x(w, plane, 1).start()

        visit(z, 0, False)
        near_planes(visit)

    def finish_x(w):
        def one(k, carry):
            got_x(w, k, 0).wait_recv()
            got_x(w, k, 1).wait_recv()
            return carry

        lax.fori_loop(0, NZ, one, 0)

    def close_gather(w):
        def one(k, carry):
            send_y(w, k).wait_send()
            if w < FFN1:
                send_x(w, k, 0).wait_send()
                send_x(w, k, 1).wait_send()
            return carry

        lax.fori_loop(0, NZ, one, 0)

        pl.when(z < NZ - 1)(lambda: send_z(w, z, 0).wait_send())
        pl.when(z > 0)(lambda: send_z(w, z, 1).wait_send())

        def visit(plane, down, more):
            pl.when(more)(lambda: send_z(w, plane, down).wait_send())

        near_planes(visit)

    def norm_rows(v):
        center = v - jnp.mean(v, axis=-1, keepdims=True)
        rstd = lax.rsqrt(jnp.mean(center * center, axis=-1, keepdims=True) + 1e-05)
        return center * rstd, rstd

    own = rows_of(b, BLK)

    def norm_one(i, carry):
        rows = rows_of(i, 32)
        n, _ = norm_rows(tok[rows, :].astype(F32))
        normed = n * n1g[...] + n1b[...]
        for g in range(8):
            XP[pl.ds(al(128 * g + 32 * i, 32), 32), :] = normed[:, 128 * g : 128 * g + 128]
        NL[pl.ds(al(128 * b + 32 * i, 32), 32), :] = normed.astype(BF)
        return carry

    for g in range(8):
        cols = slice(128 * g, 128 * g + 128)
        om[g : g + 1, :] = om_in[:, cols]
        for a in range(4):
            ema[a, :, g, :] = ema_in[a][:, cols]
    for j in range(NDIM):
        rate = sig(ema[0, j])
        DEC[j] = 1.0 - rate * sig(ema[1, j])
        CIN[j] = rate * ema[2, j]
        lam = DEC[j]
        for _ in range(7):
            lam = lam * lam
        LAM[j] = lam

    def panel(t):
        return pl.ds(t, 8, stride=BLK)

    def end_scan():
        d = [DEC[j] for j in range(NDIM)]
        c = [CIN[j] for j in range(NDIM)]

        def step(t, h):
            row = XP[panel(t), :]
            return tuple(h[j] * d[j] + c[j] * row for j in range(NDIM))

        h = lax.fori_loop(
            0, BLK, step, tuple(jnp.zeros((8, 128), F32) for _ in range(NDIM)), unroll=4
        )
        for j in range(NDIM):
            EC[0, j] = h[j]


    def scan_round_x(own_state, arrived, out, incoming, later):
        for j in range(NDIM):
            l, mine, theirs = LAM[j], own_state[j], arrived[j]
            out[j] = pick(later, l * theirs + mine, l * mine + theirs)
            incoming[j] = pick(later, theirs, jnp.zeros_like(theirs))

    def scan_round_y(own_state, arrived, out, incoming, later, inner):
        for j in range(NDIM):
            l = LAM[j]
            l2 = l * l
            mine, theirs = own_state[j], arrived[j]
            out[j] = pick(later, l2 * theirs + mine, l2 * mine + theirs)
            hop = pick(inner == 1, l, jnp.ones_like(l))
            incoming[j] += pick(later, hop * theirs, jnp.zeros_like(l))

    def scan_round_z(arrived, incoming, reach, inner):
        for j in range(NDIM):
            l = LAM[j]
            l2 = l * l
            l4 = l2 * l2
            one = jnp.ones_like(l)
            hop = pick(lax.rem(inner, 2) == 1, l, one) * pick(inner >= 2, l2, one)
            total = incoming[j]
            for k in range(1, NZ):
                total += pick(k <= reach, hop * arrived[k - 1, j], jnp.zeros_like(l))
                hop = hop * l4
            incoming[j] = total

    loads[1].wait()
    WB[my_rows, 0:512] = o_db[:, pl.ds(al(512 * b, 512), 512)].astype(BF)
    SB[:, 0:512] = o_db[:, pl.ds(al(512 * (1 - b), 512), 512)].astype(BF)
    WB[my_rows, 512:1024] = o_db[:, pl.ds(al(3200 + 512 * b, 128), 512)].astype(BF)
    SB[:, 512:1024] = o_db[:, pl.ds(al(3200 + 512 * (1 - b), 128), 512)].astype(BF)
    shared_cols = o_db[:, 1024:1152].astype(BF)
    WB[my_rows, 1024:1152] = shared_cols
    SB[:, 1024:1152] = shared_cols
    split_columns(o_db, 1152, 8, WB, my_rows, 1152, SB)
    _, got_wb = exchange(SB, WB.at[my_rows], C, WB.at[other_rows])

    copy_og_x, got_og_x = exchange(OG.at[quad(q)], OG.at[quad(q)], X, OG.at[quad(q_x)])
    loads[2].wait()
    WP[rows_of(s, 64), :] = o_dp[...].astype(BF)
    open_gather(PROJ)
    got_wv.wait_recv()
    open_gather(VALUE)
    lax.fori_loop(0, 4, norm_one, 0)
    _, got_nl = exchange(NL.at[own], NL.at[own], C, NL.at[rows_of(1 - b, BLK)])
    end_scan()
    _, got_ex = exchange(EC.at[0], EXX, X)
    got_wb.wait_recv()
    open_gather(BASE)
    loads[4].wait()
    W2[rows_of(p, 128), :] = o_d2[...].astype(BF)
    open_gather(FFN2)

    got_ex.wait_recv()
    scan_round_x(EC.at[0], EXX, EC.at[1], PIN, x == 1)
    _, got_ey = exchange(EC.at[1], EXY, Y)
    loads[3].wait()
    for j in range(4):
        for t in range(8):
            AS[32 * j : 32 * j + 32, 128 * t : 128 * t + 128] = o_d1[
                :, 128 * (4 * t + j) : 128 * (4 * t + j) + 128
            ].astype(BF)
    f1_rows = lambda j: pl.ds(al(128 * p + 32 * j, 32), 32)
    W1[f1_rows(q), :] = AS[rows_of(q, 32), :]
    f1_pairs = [
        exchange(AS.at[rows_of(j, 32)], W1.at[f1_rows(q)], device, W1.at[f1_rows(j)])
        for j, device in ((q_c, C), (q_x, X), (q_xc, XC))
    ]
    copy_og_c, got_og_c = exchange(OG.at[quad(q)], OG.at[quad(q)], C, OG.at[quad(q_c)])
    got_ey.wait_recv()
    scan_round_y(EC.at[1], EXY, EC.at[2], PIN, y == 1, x)
    got_ez = [exchange(EC.at[2], EXZ.at[k - 1], (ahead(k), b))[1] for k in range(1, NZ)]
    for copy, got in f1_pairs:
        copy.wait_send()
        settle(copy)
        got.wait_recv()
    open_gather(FFN1)
    relay_z(VALUE)
    relay_y(VALUE)
    relay_z(BASE)
    relay_y(BASE)
    for got in got_ez:
        got.wait_recv()
    scan_round_z(EXZ, PIN, z, 2 * y + x)

    def forward_scan():
        for half in range(2):
            js = range(8 * half, 8 * half + 8)
            d = [DEC[j] for j in js]
            c = [CIN[j] for j in js]
            g = [EMA_SCALE * ema[3, j] for j in js]

            def group(i, h):
                for n, j in enumerate(js):
                    HC[i, j] = h[n]
                for u in range(8):
                    t = 8 * i + u
                    row = XP[panel(t), :]
                    h = tuple(h[n] * d[n] + c[n] * row for n in range(8))
                    out = g[0] * h[0]
                    for n in range(1, 8):
                        out = out + g[n] * h[n]
                    if half == 0:
                        out = out + om[...] * row
                    else:
                        out = out + YP[panel(t), :]
                    YP[panel(t), :] = out
                return h

            lax.fori_loop(0, 16, group, tuple(PIN[j] for j in js))

    forward_scan()

    def mixed_one(i, carry):
        for g in range(8):
            v = YP[pl.ds(al(128 * g + 32 * i, 32), 32), :]
            ML[pl.ds(al(128 * b + 32 * i, 32), 32), 128 * g : 128 * g + 128] = silu(v).astype(BF)
        return carry

    lax.fori_loop(0, 4, mixed_one, 0)
    _, got_ml = exchange(ML.at[own], ML.at[own], C, ML.at[rows_of(1 - b, BLK)])
    relay_z(PROJ)
    relay_y(PROJ)

    low_row = low1(1)

    def my_half(ref, start):
        parts = []
        for t in range(8):
            lo, hi = split_pair(
                ref[:, start + 256 * t : start + 256 * t + 128],
                ref[:, start + 256 * t + 128 : start + 256 * t + 256],
                low_row,
            )
            parts.append(pick(first, lo, hi))
        return jnp.concatenate(parts, axis=1)

    got_nl.wait_recv()
    finish_x(VALUE)
    vbias = my_half(vb, 0)
    for n in range(2):
        cols = slice(512 * n, 512 * n + 512)
        v = dot_nn(NL[...], WV[:, cols]) + vbias[:, cols]
        VP[:, cols] = v.astype(BF)
        VL[:, cols] = silu(v).astype(BF)

    relay_z(FFN1)
    relay_z(FFN2)

    got_ml.wait_recv()
    finish_x(BASE)
    UH[:, 0:512] = dot_nn(ML[...], WB[:, 0:512]) + bb[:, pl.ds(al(512 * b, 512), 512)]
    UH[:, 512:1024] = dot_nn(ML[...], WB[:, 512:1024]) + bb[:, pl.ds(al(3200 + 512 * b, 128), 512)]
    theirs = rows_of(1 - b, BLK)
    my_cols = pl.ds(al(512 * b, 512), 512)
    their_cols = pl.ds(al(512 * (1 - b), 512), 512)
    copy_u, got_u = exchange(UH.at[theirs, 0:512], UU.at[:, my_cols], C, UU.at[:, their_cols])
    copy_h, got_h = exchange(UH.at[theirs, 512:1024], HH.at[:, my_cols], C, HH.at[:, their_cols])
    UU[:, my_cols] = UH[own, 0:512]
    HH[:, my_cols] = UH[own, 512:1024]
    SHP[...] = dot_nn(ML[...], WB[:, 1024:1152]) + bb[:, 1024:1152]
    rbias = my_half(bb, 1152)
    for n in range(2):
        RP[:, 512 * n : 512 * n + 512] = (
            dot_nn(ML[...], WB[:, 1152 + 512 * n : 1664 + 512 * n]) + rbias[:, 512 * n : 512 * n + 512]
        ).astype(BF)

    shared_of = lambda i: silu(SHP[128 * i : 128 * i + 128, :])

    def queries_keys(i):
        sh = shared_of(i)
        return (sh * sg[0:1, :] + qo[...]).astype(BF), (sh * sg[1:2, :]).astype(BF)

    position = jnp.transpose(shear(jnp.broadcast_to(pbr[...], (BLK, BLK)), False))
    at_row = lax.broadcasted_iota(jnp.int32, (BLK, BLK), 0)
    at_col = lax.broadcasted_iota(jnp.int32, (BLK, BLK), 1)
    causal = at_row >= at_col
    for i in range(2):
        rows = slice(128 * i, 128 * i + 128)
        qs, ks = queries_keys(i)
        scores = jnp.where(causal, dot_nt(qs, ks) * SCALE + position, -jnp.inf)
        e = jnp.exp(scores - jnp.max(scores, axis=-1, keepdims=True))
        attn = e / jnp.sum(e, axis=-1, keepdims=True)
        AT[rows, :] = attn
        low = attn.astype(BF)
        for n in range(2):
            cols = slice(512 * n, 512 * n + 512)
            att = dot_nn(low, VL[rows, cols])
            AD[rows, cols] = att.astype(BF)
            GT[rows, cols] = (att * silu(RP[rows, cols].astype(F32))).astype(BF)

    finish_x(PROJ)
    copy_u.wait_send()
    copy_h.wait_send()
    settle(copy_u)
    settle(copy_h)
    for n in range(2):
        cols = slice(512 * n, 512 * n + 512)
        UH[:, cols] = dot_nn(GT[...], WP[:, cols])
    copy_p, got_p = exchange(UH.at[theirs], PR, C)
    got_u.wait_recv()
    got_h.wait_recv()
    got_p.wait_recv()

    def residual_one(i, carry):
        rows = rows_of(i, 32)
        mine = pl.ds(al(128 * b + 32 * i, 32), 32)
        total = HH[rows, :] + ((UH[mine, :] + PR[rows, :]) + pbias[...])
        HH[rows, :] = total
        base = tok[rows, :].astype(F32)
        out = base + sig(UU[rows, :]) * (silu(total) - base)
        FO[rows, :] = out
        n, _ = norm_rows(out)
        NT[pl.ds(al(128 * q + 32 * i, 32), 32), :] = (n * n2g[...] + n2b[...]).astype(BF)
        return carry

    lax.fori_loop(0, 4, residual_one, 0)
    got_og_x.wait_recv()
    copy_og_xc, got_og_xc = exchange(OG.at[quad(q_x)], OG.at[quad(q_x)], C, OG.at[quad(q_xc)])
    copy_nt_x, got_nt_x = exchange(NT.at[quad(q)], NT.at[quad(q)], X, NT.at[quad(q_x)])
    copy_nt_c, got_nt_c = exchange(NT.at[quad(q)], NT.at[quad(q)], C, NT.at[quad(q_c)])

    relay_y(FFN1)
    relay_y(FFN2)
    got_og_c.wait_recv()
    got_og_xc.wait_recv()
    for m in range(2):
        for n in range(2):
            rows = slice(256 * m, 256 * m + 256)
            cols = slice(512 * n, 512 * n + 512)
            FP[rows, cols] = dot_nt(OG[rows, :], W2[cols, :])
    got_nt_x.wait_recv()
    copy_nt_xc, got_nt_xc = exchange(NT.at[quad(q_x)], NT.at[quad(q_x)], C, NT.at[quad(q_xc)])
    got_nt_c.wait_recv()
    got_nt_xc.wait_recv()

    FL = FG.at[0:512]
    GF = FG.at[512:1024]
    fbias = jnp.concatenate(
        [f1b[:, pl.ds(al(512 * t + 128 * q, 128), 128)] for t in range(8)], axis=1
    )
    for m in range(2):
        for n in range(2):
            rows = slice(256 * m, 256 * m + 256)
            cols = slice(512 * n, 512 * n + 512)
            pre = dot_nn(NT[rows, :], W1[:, cols]) + fbias[:, cols]
            FL[rows, cols] = silu(pre).astype(BF)
            GF[rows, cols] = (FP[rows, cols] * slope(pre)).astype(BF)
    for m in range(2):
        for n in range(2):
            rows = slice(256 * m, 256 * m + 256)
            cols = slice(512 * n, 512 * n + 512)
            AS[rows, cols] = dot_nt(GF[rows, :], W1[cols, :]).astype(BF)

    def reduce_pair(staged, landing):
        copies = []
        for c in range(2):
            there = rows_of(2 * c + 1 - b, BLK)
            copies.append(exchange(staged.at[there], landing.at[rows_of(c, BLK)], C))
        return copies

    def reduce_x(staged, landing, arrivals, out, out_landing):
        for _, arrival in arrivals:
            arrival.wait_recv()

        def one(i, carry):
            mine = pl.ds(al(128 * (2 * (1 - x) + b) + 32 * i, 32), 32)
            got = pl.ds(al(128 * (1 - x) + 32 * i, 32), 32)
            out[rows_of(i, 32), :] = (staged[mine, :].astype(F32) + landing[got, :].astype(F32)).astype(BF)
            return carry

        lax.fori_loop(0, 4, one, 0)
        return exchange(out, out_landing, X)

    def pair_sum(staged, landing, i):
        mine = pl.ds(al(128 * q + 32 * i, 32), 32)
        got = pl.ds(al(128 * x + 32 * i, 32), 32)
        return staged[mine, :].astype(F32) + landing[got, :].astype(F32)

    got_a = reduce_pair(AS, AR)

    def store_row(row, v):
        for g in range(v.shape[1] // 128):
            SM_OUT[row + g : row + g + 1, :] = v[:, 128 * g : 128 * g + 128]

    SM_OUT[...] = jnp.zeros((SM_ROWS, 128), F32)

    def weight_grad(left, right, out, right0, out0, width):
        tile = 512 if width % 512 == 0 else 384
        for m in range(2):
            for n in range(width // tile):
                out[512 * m : 512 * m + 512, out0 + tile * n : out0 + tile * n + tile] = dot_tn(
                    left[:, 512 * m : 512 * m + 512],
                    right[:, right0 + tile * n : right0 + tile * n + tile],
                ).astype(BF)

    grads = [NO, FG, GBA, GBB, G1, G2]
    RXV = W1.at[0:512]
    RXP = W1.at[512:1024]
    RXBA = W2.at[0:512]
    half = [RXV, RXP, RXBA, RXBB]

    def shard(u, chip):
        if u < U_1:
            return rows_of(chip, 64)
        return rows_of(lax.div(chip, 2), 128)

    y_first = Y_FIRST
    hop_x, hop_y = xs_ - s, ys_ - s

    def hops(u):
        return (hop_y, hop_x, Y, X) if u in y_first else (hop_x, hop_y, X, Y)

    def rs_x(u, k, far):
        hop1, hop2, device, _ = hops(u)
        chip = ahead(k) + (hop2 if far else 0)
        src = grads[u].at[shard(u, chip + hop1)]
        slot = half[u].at[pl.ds(al(64 * (2 * k + far), 64), 64)]
        return remote(src, slot, rxs.at[u, k, far], rxr.at[u, k, far], device)

    def rs_y(u, k):
        _, hop2, _, device = hops(u) if u < U_1 else (0, hop_y, X, Y)
        src = grads[u].at[shard(u, ahead(k) + hop2)]
        return remote(src, RY[u].at[k], rys.at[u, k], ryr.at[u, k], device)

    def rs_z(u, k):
        src = grads[u].at[shard(u, ahead(k))]
        return remote(src, RZ[u].at[k - 1], rzs.at[u, k], rzr.at[u, k], (ahead(k), b))

    turn = lambda i: lax.rem(i + 1, NZ)

    def rs_open(u, start=0, stop=None):
        def one(i, carry):
            k = turn(i)
            if u < U_1:
                rs_x(u, k, 1).start()
                rs_x(u, k, 0).start()
            else:
                rs_y(u, k).start()
            return carry

        lax.fori_loop(start, NZ if stop is None else stop, one, 0)

    def rs_pass_x(u, start=0, stop=None):
        def one(i, carry):
            k = turn(i)
            for far in (1, 0):
                rs_x(u, k, far).wait_recv()
                rows = shard(u, ahead(k) + (hops(u)[1] if far else 0))
                got = half[u][pl.ds(al(64 * (2 * k + far), 64), 64), :]
                grads[u][rows, :] = (grads[u][rows, :].astype(F32) + got.astype(F32)).astype(BF)
                if far == 1:
                    rs_y(u, k).start()
            return carry

        lax.fori_loop(start, NZ if stop is None else stop, one, 0)

    def rs_pass_y(u, start=0, stop=None):
        def one(i, carry):
            k = i + 1
            rs_y(u, k).wait_recv()
            rows = shard(u, ahead(k))
            grads[u][rows, :] = (grads[u][rows, :].astype(F32) + RY[u][k].astype(F32)).astype(BF)
            rs_z(u, k).start()
            return carry

        lax.fori_loop(start, NZ - 1 if stop is None else stop, one, 0)
        if stop is None:
            rs_y(u, 0).wait_recv()

    def rs_total(u, rows_in):
        rows = shard(u, s)
        size = 64 if u < U_1 else 128
        start = size * (s if u < U_1 else p)
        at = pl.ds(al(start + rows_in[0], 16), rows_in[1])
        in_ = pl.ds(al(rows_in[0], 16), rows_in[1])
        total = grads[u][at, :].astype(F32) + RY[u][0, in_, :].astype(F32)
        for k in range(1, NZ):
            total += RZ[u][k - 1, in_, :].astype(F32)
        return total

    def rs_wait_z(u):
        def one(k, carry):
            rs_z(u, k).wait_recv()
            return carry

        lax.fori_loop(1, NZ, one, 0)

    def column_sum(ref, start, width):
        def one(i, acc):
            return acc + fold8(ref[rows_of(i, 32), start : start + width].astype(F32))

        acc = lax.fori_loop(0, ref.shape[0] // 32, one, jnp.zeros((8, width), F32))
        return jnp.sum(acc, axis=0, keepdims=True)

    def back_two(i, carry):
        rows = rows_of(i, 32)
        a = pair_sum(AS, AR, i) + AXR[rows, :].astype(F32)
        n, rstd = norm_rows(FO[rows, :])
        g = a * n2g[...]
        grad = og[rows, :].astype(F32) + (
            g - jnp.mean(g, axis=-1, keepdims=True) - n * jnp.mean(g * n, axis=-1, keepdims=True)
        ) * rstd
        update = sig(UU[rows, :])
        total = HH[rows, :]
        logistic = sig(total)
        base = tok[rows, :].astype(F32)
        gh = (grad * update * (logistic * (1.0 + total * (1.0 - logistic)))).astype(BF)
        GH[pl.ds(al(128 * b + 32 * i, 32), 32), :] = gh
        GUS[rows, :] = (grad * (total * logistic - base) * update * (1.0 - update)).astype(BF)
        PR[rows, :] = grad * (1.0 - update)
        return (
            carry[0] + fold8(a * n),
            carry[1] + fold8(a),
            carry[2] + fold8(gh.astype(F32)),
            carry[3] + fold8(og[rows, :].astype(F32)),
        )

    weight_grad(FL, OG, G2, 0, 0, 1024)
    rs_open(U_2)
    close_gather(FFN1)
    a_x = reduce_x(AS, AR, got_a, AX, AXR)
    for m in range(2):
        for n in range(2):
            rows = slice(256 * m, 256 * m + 256)
            cols = slice(512 * n, 512 * n + 512)
            FP[rows, cols] = dot_nn(FL[rows, :], W2[:, cols])
    got_o = reduce_pair(FP, GNVR)
    close_gather(FFN2)
    weight_grad(NT, GF, G1, 0, 0, 1024)
    rs_open(U_1, 0, 2)
    f1_sum = column_sum(GF, 0, 1024)
    for t in range(8):
        SM_OUT[pl.ds(ROW_F1B + 4 * t + q, 1), :] = f1_sum[:, 128 * t : 128 * t + 128]
    o_x = reduce_x(FP, GNVR, got_o, OX, OXR)

    def out_one(i, carry):
        OB[rows_of(i, 32), :] = pair_sum(FP, GNVR, i)
        return carry

    lax.fori_loop(0, 4, out_one, 0)
    rs_pass_y(U_2, 0, 1)

    a_x[1].wait_recv()
    zero8 = jnp.zeros((8, 1024), F32)
    sums = lax.fori_loop(0, 4, back_two, (zero8, zero8, zero8, zero8))
    _, got_gh = exchange(GH.at[own], GH.at[own], C, GH.at[theirs])
    _, got_gu = exchange(GUS.at[:, their_cols], GBS.at[own, 0:512], C, GBS.at[theirs, 0:512])
    GBS[own, 0:512] = GUS[:, my_cols]
    for row, acc in zip((ROW_N2G, ROW_N2B, ROW_PB, ROW_F2B), sums):
        store_row(row, jnp.sum(acc, axis=0, keepdims=True))
    rs_pass_y(U_2, 1, 2)

    got_gh.wait_recv()
    got_gu.wait_recv()
    GBS[:, 512:1024] = GH[:, my_cols]
    weight_grad(ML, GBS, GBA, 0, 0, 1024)
    o_x[1].wait_recv()
    rs_open(U_BA)
    for n in range(2):
        cols = slice(512 * n, 512 * n + 512)
        gg = dot_nt(GH[...], WP[cols, :])
        pre = RP[:, cols].astype(F32)
        logistic = sig(pre)
        GA[:, cols] = (gg * (pre * logistic)).astype(BF)
        GBS[:, 1152 + 512 * n : 1664 + 512 * n] = (
            gg * AD[:, cols].astype(F32) * (logistic * (1.0 + pre * (1.0 - logistic)))
        ).astype(BF)
    for i in range(2):
        rows = slice(128 * i, 128 * i + 128)
        GAT[rows, :] = dot_nt(GA[rows, :], VL[rows, :])
    _, got_gat = exchange(GAT, GATR, C)
    weight_grad(GT, GH, FG, 0, 0, 1024)
    for i in range(2):
        rows = slice(128 * i, 128 * i + 128)
        low = AT[rows, :].astype(BF)
        for n in range(2):
            cols = slice(512 * n, 512 * n + 512)
            gv = dot_tn(low, GA[rows, cols])
            GVP[rows, cols] = (gv * slope(VP[rows, cols].astype(F32))).astype(BF)
    got_gat.wait_recv()
    for i in range(2):
        rows = slice(128 * i, 128 * i + 128)
        attn = AT[rows, :]
        gat = GAT[rows, :] + GATR[rows, :]
        gs = (attn * (gat - jnp.sum(gat * attn, axis=-1, keepdims=True))).astype(BF)
        qs, ks = queries_keys(i)
        gq = dot_nn(gs, ks) * SCALE
        gk = dot_tn(gs, qs) * SCALE
        pre = SHP[rows, :]
        sh = silu(pre)
        gsp = (gq * sg[0:1, :] + gk * sg[1:2, :]) * slope(pre)
        GBS[rows, 1024:1152] = (gsp * 0.5).astype(BF)
        mine = b == i

        @pl.when(mine)
        def _(gs=gs, gq=gq, gk=gk, sh=sh):
            SM_OUT[ROW_SG : ROW_SG + 1, :] = jnp.sum(gq * sh, axis=0, keepdims=True)
            SM_OUT[ROW_SG + 1 : ROW_SG + 2, :] = jnp.sum(gk * sh, axis=0, keepdims=True)
            SM_OUT[ROW_QO : ROW_QO + 1, :] = jnp.sum(gq, axis=0, keepdims=True)
            SM_OUT[ROW_POS : ROW_POS + 1, :] = jnp.sum(
                shear(jnp.transpose(gs.astype(F32)), True), axis=0, keepdims=True
            )

    GM = FP.at[0:256]
    GNV = FP.at[256:512]
    for copy, _ in got_o:
        copy.wait_send()
        settle(copy)
    for n in range(2):
        cols = slice(512 * n, 512 * n + 512)
        GM[:, cols] = dot_nt(GBS[...], WB[cols, :])
    _, got_gm = exchange(GM.at[theirs], GNVR.at[0:128], C)
    for n in range(2):
        cols = slice(512 * n, 512 * n + 512)
        GNV[:, cols] = dot_nt(GVP[...], WV[cols, :])
    _, got_gnv = exchange(GNV.at[theirs], GNVR.at[128:256], C)
    GBS[:, 1024:1152] = (GBS[:, 1024:1152].astype(F32) * 2.0).astype(BF)
    rs_pass_y(U_2, 2)

    def grad_ema_one(i, carry):
        for g in range(8):
            cols = slice(128 * g, 128 * g + 128)
            rows = pl.ds(al(128 * g + 32 * i, 32), 32)
            v = GM[pl.ds(al(128 * b + 32 * i, 32), 32), cols] + GNVR[rows_of(i, 32), cols]
            GEP[rows, :] = v * slope(YP[rows, :])
        return carry

    def adjoint_end():
        d = [DEC[j] for j in range(NDIM)]

        def step(i, g):
            row = GEP[panel(BLK - 1 - i), :]
            return tuple(g[j] * d[j] + row for j in range(NDIM))

        g = lax.fori_loop(
            0, BLK, step, tuple(jnp.zeros((8, 128), F32) for _ in range(NDIM)), unroll=4
        )
        for j in range(NDIM):
            EC[3, j] = g[j]

    got_gm.wait_recv()
    lax.fori_loop(0, 4, grad_ema_one, 0)
    adjoint_end()
    _, got_bx = exchange(EC.at[3], BXX, X)
    rs_open(U_P)
    rs_pass_x(U_BA, 0, 2)
    got_bx.wait_recv()
    scan_round_x(EC.at[3], BXX, EC.at[4], PIN, x == 0)
    _, got_by = exchange(EC.at[4], BXY, Y)
    rs_open(U_1, 2)
    for copy in (copy_og_c, copy_og_x, copy_og_xc, copy_nt_x, copy_nt_c, copy_nt_xc):
        copy.wait_send()
        settle(copy)
    weight_grad(NL, GVP, NO, 0, 0, 1024)
    rs_pass_y(U_1, 0, 2)
    rs_pass_x(U_BA, 2)
    got_by.wait_recv()
    scan_round_y(EC.at[4], BXY, EC.at[5], PIN, y == 0, 1 - x)
    got_bz = [
        exchange(EC.at[5], BXZ.at[k - 1], (ahead(NZ - k), b))[1] for k in range(1, NZ)
    ]
    rs_open(U_V)
    weight_grad(ML, GBS, GBB, 1024, 0, 1152)
    base_sum = column_sum(GBS, 0, BASE_COLS)
    for t in range(4):
        cols = slice(128 * t, 128 * t + 128)
        SM_OUT[pl.ds(ROW_BB + 4 * b + t, 1), :] = base_sum[:, cols]
        SM_OUT[pl.ds(ROW_BB + 25 + 4 * b + t, 1), :] = base_sum[:, 512 + 128 * t : 640 + 128 * t]
    SM_OUT[ROW_BB + 8 : ROW_BB + 9, :] = base_sum[:, 1024:1152] * 0.5

    low_float = low_row.astype(F32)
    keep = pick(first, low_float, 1.0 - low_float)

    def store_half(row, v):
        for t in range(8):
            block = v[:, 128 * t : 128 * t + 128]
            turned = pltpu.roll(block, 64, 1)
            SM_OUT[row + 2 * t : row + 2 * t + 1, :] = keep * pick(first, block, turned)
            SM_OUT[row + 2 * t + 1 : row + 2 * t + 2, :] = keep * pick(first, turned, block)

    store_half(ROW_BB + 9, base_sum[:, 1152:2176])
    store_half(ROW_VB, column_sum(GVP, 0, 1024))

    def block_out_one(i, carry):
        rows = rows_of(i, 32)
        o_block[rows, :] = (
            FO[rows, :] + ((OB[rows, :] + OXR[rows, :].astype(F32)) + f2b[...])
        ).astype(BF)
        return carry

    lax.fori_loop(0, 4, block_out_one, 0)
    rs_pass_y(U_BA, 0, 2)
    for got in got_bz:
        got.wait_recv()
    scan_round_z(BXZ, PIN, NZ - 1 - z, 2 * (1 - y) + 1 - x)
    rs_pass_y(U_1, 2)
    def backward_scan():
        for part in range(2):
            js = range(8 * part, 8 * part + 8)
            d = [DEC[j] for j in js]
            c = [CIN[j] for j in js]
            e = [EMA_SCALE * CIN[j] * ema[3, j] for j in js]

            def group(i, carry):
                at = 15 - i
                h = tuple(HC[at, j] for j in js)
                for u in range(8):
                    for n in range(8):
                        H8[u, n] = h[n]
                    if u < 7:
                        row = XP[panel(8 * at + u), :]
                        h = tuple(h[n] * d[n] + c[n] * row for n in range(8))
                g, s1, m = carry
                for u in range(7, -1, -1):
                    t = 8 * at + u
                    row = XP[panel(t), :]
                    ge = GEP[panel(t), :]
                    g = tuple(g[n] * d[n] + ge for n in range(8))
                    s1 = tuple(s1[n] + row * g[n] for n in range(8))
                    m = tuple(m[n] + g[n] * H8[u, n] for n in range(8))
                    out = e[0] * g[0]
                    for n in range(1, 8):
                        out = out + e[n] * g[n]
                    if part == 0:
                        out = out + om[...] * ge
                    else:
                        out = out + GNP[panel(t), :]
                    GNP[panel(t), :] = out
                return g, s1, m

            zeros = tuple(jnp.zeros((8, 128), F32) for _ in range(8))
            _, s1, m = lax.fori_loop(0, 16, group, (tuple(PIN[j] for j in js), zeros, zeros))
            for n, j in enumerate(js):
                SM_OUT[8 * j : 8 * j + 8, :] = s1[n]
                SM_OUT[128 + 8 * j : 128 + 8 * j + 8, :] = m[n]

    backward_scan()
    rs_pass_y(U_BA, 2)
    rs_pass_x(U_P, 0, 2)

    for g in range(8):
        rows = slice(128 * g, 128 * g + 128)
        SM_OUT[ROW_OMEGA + g : ROW_OMEGA + g + 1, :] = jnp.sum(
            fold8(XP[rows, :] * GEP[rows, :]), axis=0, keepdims=True
        )

    got_gnv.wait_recv()

    def back_one(i, carry):
        rows = rows_of(i, 32)
        wide = jnp.concatenate(
            [GNP[pl.ds(al(128 * g + 32 * i, 32), 32), :] for g in range(8)], axis=1
        )
        a = (GNV[pl.ds(al(128 * b + 32 * i, 32), 32), :] + GNVR[pl.ds(al(128 + 32 * i, 32), 32), :]) + wide
        n, rstd = norm_rows(tok[rows, :].astype(F32))
        g = a * n1g[...]
        back = (
            g - jnp.mean(g, axis=-1, keepdims=True) - n * jnp.mean(g * n, axis=-1, keepdims=True)
        ) * rstd
        o_tok[rows, :] = (PR[rows, :] + back).astype(BF)
        return carry[0] + fold8(a * n), carry[1] + fold8(a)

    sums = lax.fori_loop(0, 4, back_one, (zero8, zero8))
    for row, acc in zip((ROW_N1G, ROW_N1B), sums):
        store_row(row, jnp.sum(acc, axis=0, keepdims=True))

    half_rows = SM_ROWS // 2
    my_part = rows_of(b, half_rows)
    their_part = rows_of(1 - b, half_rows)
    copy_c, got_c = exchange(SM_OUT.at[their_part], SMR, C)
    rs_pass_x(U_P, 2)
    got_c.wait_recv()
    SMX[0] = SM_OUT[my_part, :] + SMR[...]
    _, got_sx = exchange(SMX.at[0], SMX.at[1], X)
    rs_open(U_BB)
    rs_pass_y(U_P, 0, 2)
    got_sx.wait_recv()
    SMY[0] = SMX[0] + SMX[1]
    _, got_sy = exchange(SMY.at[0], SMY.at[1], Y)
    rs_pass_x(U_V)
    rs_pass_y(U_P, 2)
    got_sy.wait_recv()
    SMZ[0] = SMY[0] + SMY[1]
    got_sz = [exchange(SMZ.at[0], SMZ.at[k], (ahead(k), b))[1] for k in range(1, NZ)]
    rs_pass_x(U_BB)
    for got in got_sz:
        got.wait_recv()
    total = SMZ[lax.rem(z, NZ)]
    for k in range(1, NZ):
        total = total + SMZ[lax.rem(z + NZ - k, NZ)]
    SM_OUT[my_part, :] = total
    _, got_cc = exchange(SM_OUT.at[my_part], SMC, C)

    rs_pass_y(U_V)
    rs_pass_y(U_BB)
    rs_wait_z(U_2)
    for i in range(4):
        o_d2[32 * i : 32 * i + 32, :] = rs_total(U_2, (32 * i, 32))
    rs_wait_z(U_1)
    for i in range(4):
        o_d1[:, 1024 * i : 1024 * i + 1024] = rs_total(U_1, (32 * i, 32))
    quarter = lambda j: pl.ds(al(1024 * j, 1024), 1024)
    d1_pairs = [
        exchange(o_d1.at[:, quarter(j)], FX1.at[q], device, FX1.at[j])
        for j, device in ((q_c, C), (q_x, X), (q_xc, XC))
    ]
    rs_wait_z(U_P)
    for i in range(2):
        o_dp[32 * i : 32 * i + 32, :] = rs_total(U_P, (32 * i, 32))
    mine32 = 32 * b
    their32 = 32 * (1 - b)
    h_mine = pl.ds(al(3200 + 512 * b, 128), 512)
    h_their = pl.ds(al(3200 + 512 * (1 - b), 128), 512)
    low = low1(32)

    def merge(out, start, own_half, other_half):
        for t in range(8):
            cols = slice(128 * t, 128 * t + 128)
            m, o = own_half[:, cols], other_half[:, cols]
            lo, hi = pick(first, m, o), pick(first, o, m)
            at = start + 256 * t
            out[:, at : at + 128] = jnp.where(low, lo, pltpu.roll(hi, 64, 1))
            out[:, at + 128 : at + 256] = jnp.where(low, pltpu.roll(lo, 64, 1), hi)

    rs_wait_z(U_BA)
    FB[:, 0:1024] = rs_total(U_BA, (their32, 32))
    _, got_ba = exchange(FB.at[:, 0:1024], FXB.at[:, 0:1024], C)
    part = rs_total(U_BA, (mine32, 32))
    o_db[:, my_cols] = part[:, 0:512]
    o_db[:, h_mine] = part[:, 512:1024]
    rs_wait_z(U_BB)
    FB[:, 1024:2176] = rs_total(U_BB, (their32, 32))
    _, got_bb = exchange(FB.at[:, 1024:2176], FXB.at[:, 1024:2176], C)
    part = rs_total(U_BB, (mine32, 32))
    o_db[:, 1024:1152] = part[:, 0:128]
    rs_wait_z(U_V)
    FV[...] = rs_total(U_V, (their32, 32))
    _, got_v = exchange(FV, FXV, C)
    part_v = rs_total(U_V, (mine32, 32))

    FX1[q] = o_d1[:, quarter(q)]
    for copy, got in d1_pairs:
        copy.wait_send()
        settle(copy)
        got.wait_recv()
    for j in range(4):
        for t in range(8):
            o_d1[:, 128 * (4 * t + j) : 128 * (4 * t + j) + 128] = FX1[j, :, 128 * t : 128 * t + 128]

    copy_c.wait_send()
    settle(copy_c)
    got_cc.wait_recv()
    SM_OUT[their_part, :] = SMC[...]
    for j in range(NDIM):
        rate, damping = sig(ema[0, j]), sig(ema[1, j])
        beta, gamma = ema[2, j], EMA_SCALE * ema[3, j]
        s1 = SM_OUT[8 * j : 8 * j + 8, :]
        m = gamma * SM_OUT[128 + 8 * j : 136 + 8 * j, :]
        o_ema[0, j] = (beta * gamma * s1 - damping * m) * rate * (1.0 - rate)
        o_ema[1, j] = -rate * m * damping * (1.0 - damping)
        o_ema[2, j] = gamma * rate * s1
        o_ema[3, j] = EMA_SCALE * rate * beta * s1

    o_sm[...] = SM_OUT[...]
    got_ba.wait_recv()
    o_db[:, their_cols] = FXB[:, 0:512]
    o_db[:, h_their] = FXB[:, 512:1024]
    got_bb.wait_recv()
    merge(o_db, 1152, part[:, 128:1152], FXB[:, 1152:2176])
    got_v.wait_recv()
    merge(o_dv, 0, part_v, FXV[...])

    for copy in open_sends:
        copy.wait_send()
    for w in (VALUE, BASE, PROJ):
        close_gather(w)

    def close_sums(u):
        def one(k, carry):
            rs_y(u, k).wait_send()
            if u < U_1:
                rs_x(u, k, 0).wait_send()
                rs_x(u, k, 1).wait_send()
            return carry

        lax.fori_loop(0, NZ, one, 0)

        def plane(k, carry):
            rs_z(u, k).wait_send()
            return carry

        lax.fori_loop(1, NZ, plane, 0)

    for u in (U_V, U_P, U_BA, U_BB, U_1, U_2):
        close_sums(u)


def hand_on_kernel(*refs):
    large, (ema, sums), outs = refs[:7], refs[7:9], refs[9:]
    for src, dst in zip(large, outs):
        dst[...] = src[...]
    for a in range(4):
        for g in range(8):
            outs[7 + a][:, 128 * g : 128 * g + 128] = ema[a, :, g, :]
    for out, (row, n) in zip(outs[11:], SMALL_ROWS):
        if out.shape[0] == 1:
            for g in range(n):
                out[:, 128 * g : 128 * g + 128] = sums[row + g : row + g + 1, :]
        else:
            out[...] = sums[row : row + n, :]


def fast_shards(
    tokens,
    out_grad,
    norm1_gain,
    norm1_bias,
    value_weight,
    value_bias,
    ema_delta,
    ema_alpha,
    ema_beta,
    ema_gamma,
    ema_omega,
    base_weight,
    base_bias,
    shared_gamma,
    query_offset,
    position_bias,
    proj_weight,
    proj_bias,
    norm2_gain,
    norm2_bias,
    ffn1_weight,
    ffn1_bias,
    ffn2_weight,
    ffn2_bias,
):
    NS = lax.axis_size("seq")
    NZ = NS // 4
    row = lambda v: v.reshape(1, -1)
    small = [
        tokens[0], out_grad[0], row(norm1_gain), row(norm1_bias), row(value_bias),
        ema_delta.T, ema_alpha.T, ema_beta.T, ema_gamma.T,
        row(ema_omega), row(base_bias), shared_gamma, row(query_offset),
        row(position_bias), row(proj_bias), row(norm2_gain), row(norm2_bias), row(ffn1_bias),
        row(ffn2_bias),
    ]
    large = [value_weight, base_weight, proj_weight, ffn1_weight, ffn2_weight]
    f = lambda *shape: jax.ShapeDtypeStruct(shape, F32)
    h = lambda *shape: jax.ShapeDtypeStruct(shape, BF)
    outs = [
        h(128, 1024), h(128, 1024), f(32, 2048), f(32, 4224), f(64, 1024), f(32, 4096), f(128, 1024),
        f(4, NDIM, 8, 128),
    ]
    outs.append(f(SM_ROWS, 128))
    vm = lambda *shape: pltpu.VMEM(shape, BF)
    vf = lambda *shape: pltpu.VMEM(shape, F32)
    dma = lambda *shape: pltpu.SemaphoreType.DMA(shape)
    scratch = [
        vf(SM_ROWS, 128), vf(4, NDIM, 8, 128), vf(8, 128),
        vm(1024, 1024), vm(1024, BASE_COLS), vm(1024, 1024), vm(1024, 1024), vm(1024, 1024),
        vm(1024, 1024), vm(1024, 1024), vm(1024, 1024), vm(1024, 1152), vm(512, 1152),
        vm(NZ, 64, 1024), vm(NZ, 64, 1024), vm(NZ, 64, 1024), vm(NZ, 64, 1152),
        vm(NZ, 128, 1024), vm(NZ, 128, 1024),
        vm(NZ - 1, 64, 1024), vm(NZ - 1, 64, 1024), vm(NZ - 1, 64, 1024), vm(NZ - 1, 64, 1152),
        vm(NZ - 1, 128, 1024), vm(NZ - 1, 128, 1024),
        vf(32, 1024), vf(32, BASE_COLS), vf(32, 1024), vf(32, BASE_COLS), vf(4, 32, 1024),
        vm(32, 1024), vm(32, BASE_COLS), vm(256, 1024), vm(256, 1024), vm(1024, 1024),
        vm(256, 1024), vm(256, 1024), vf(256, 1024), vf(128, 1024), vf(128, 1024), vf(256, 128),
        vm(256, 1024), vm(256, 1024), vm(256, 1024), vf(256, 128), vf(128, 1024), vf(128, 1024),
        vf(512, 1024), vm(1024, 1024),
        vm(512, 1024), vm(256, 1024), vm(128, 1024), vm(128, 1024), vm(128, 1024), vm(128, 1024), vf(128, 1024),
        vm(256, 1024), vm(128, 1024), vm(256, BASE_COLS), vm(256, 1024), vf(256, 128), vf(256, 128),
        vm(256, 1024), vf(256, 1024),
        vf(1024, 128), vf(1024, 128), vf(1024, 128), vf(1024, 128), vf(16, NDIM, 8, 128), vf(8, 8, 8, 128),
        vf(6, NDIM, 8, 128), vf(NDIM, 8, 128), vf(NDIM, 8, 128), vf(NZ - 1, NDIM, 8, 128),
        vf(NDIM, 8, 128), vf(NDIM, 8, 128), vf(NZ - 1, NDIM, 8, 128),
        vf(NDIM, 8, 128), vf(NDIM, 8, 128), vf(NDIM, 8, 128), vf(NDIM, 8, 128),
        vf(SM_ROWS // 2, 128), vf(2, SM_ROWS // 2, 128), vf(2, SM_ROWS // 2, 128),
        vf(NZ, SM_ROWS // 2, 128), vf(SM_ROWS // 2, 128),
        dma(5), dma(5, NZ, 2), dma(5, NZ), dma(5, NZ), dma(5, NZ), dma(3, 2, NZ), dma(3, 2, NZ),
        dma(4, NZ, 2), dma(4, NZ, 2), dma(6, NZ), dma(6, NZ), dma(6, NZ), dma(6, NZ), dma(64), dma(64),
    ]
    results = pl.pallas_call(
        functools.partial(layer_kernel, NS),
        out_shape=outs,
        in_specs=[pl.BlockSpec(memory_space=pltpu.VMEM)] * len(small)
        + [pl.BlockSpec(memory_space=pl.ANY)] * len(large),
        out_specs=[pl.BlockSpec(memory_space=pltpu.VMEM)] * len(outs),
        scratch_shapes=scratch,
        compiler_params=pltpu.CompilerParams(
            collective_id=0, has_side_effects=True, vmem_limit_bytes=VMEM_LIMIT
        ),
    )(*small, *large)
    final = list(outs[:7]) + [f(NDIM, D)] * 4
    final += [f(2, 128) if row == ROW_SG else f(1, 128 * n) for row, n in SMALL_ROWS]
    local = pl.BlockSpec(memory_space=pltpu.VMEM)
    (block_out, tokens_grad, dvalue, dbase, dproj, dffn1, dffn2, ddelta, dalpha, dbeta, dgamma, *sums) = (
        pl.pallas_call(
            hand_on_kernel,
            out_shape=final,
            in_specs=[local] * 9,
            out_specs=[local] * len(final),
        )(*results)
    )
    (dn1g, dn1b, dvb, dom, dbb, dsg, dqo, dpos, dpb, dn2g, dn2b, df1b, df2b) = [
        v if v.shape[0] == 2 else v.reshape(-1) for v in sums
    ]
    return (
        block_out[None],
        tokens_grad[None],
        dn1g,
        dn1b,
        dvalue,
        dvb,
        ddelta.T,
        dalpha.T,
        dbeta.T,
        dgamma.T,
        dom,
        dbase,
        dbb,
        dsg,
        dqo,
        dpos,
        dproj,
        dpb,
        dn2g,
        dn2b,
        dffn1,
        df1b,
        dffn2,
        df2b,
    )


def solution(mesh):
    in_specs = (
        P("batch", "seq", None),
        P("batch", "seq", None),
        P(),
        P(),
        P(("seq", "batch"), None),
        P(),
        P(),
        P(),
        P(),
        P(),
        P(),
        P(("seq", "batch"), None),
        P(),
        P(),
        P(),
        P(),
        P(("seq", "batch"), None),
        P(),
        P(),
        P(),
        P(("seq", "batch"), None),
        P(),
        P(("seq", "batch"), None),
        P(),
    )
    out_specs = (
        P("batch", "seq", None),
        P("batch", "seq", None),
        P(),
        P(),
        P(("seq", "batch"), None),
        P(),
        P(),
        P(),
        P(),
        P(),
        P(),
        P(("seq", "batch"), None),
        P(),
        P(),
        P(),
        P(),
        P(("seq", "batch"), None),
        P(),
        P(),
        P(),
        P(("seq", "batch"), None),
        P(),
        P(("seq", "batch"), None),
        P(),
    )
    one_device = fast_shards if mesh.shape['seq'] == 16 else shards
    return jax.shard_map(
        one_device, mesh=mesh, in_specs=in_specs, out_specs=out_specs, check_vma=False
    )
```

```python
import functools

import jax
import jax.numpy as jnp
from jax import lax
from jax.experimental import pallas as pl
from jax.experimental.pallas import tpu as pltpu
from jax.sharding import PartitionSpec as P

D = 1024
ZD = 128
VD = 2048
NDIM = 16


precise = lax.Precision.HIGHEST


def entering(part, axis, combine, identity):
    place = lax.axis_index(axis)
    gathered = jax.tree.map(lambda a: lax.all_gather(a, axis), part)
    state = jax.tree.map(lambda a, e: jnp.zeros_like(a) + jnp.asarray(e, a.dtype), part, identity)

    def one(step, state):
        return combine(
            state, jax.tree.map(lambda a: lax.dynamic_index_in_dim(a, step, 0, False), gathered)
        )

    return lax.fori_loop(0, place, one, state)


def prefix_2(value, axis, combine, identity):
    size, index = (lax.axis_size(axis), lax.axis_index(axis))
    everything = jax.tree.map(
        lambda part, kind: lax.all_gather(part.astype(kind), axis),
        value,
        jax.tree.map(lambda a: jnp.bfloat16 if a.dtype == jnp.float32 else a.dtype, value),
    )
    start = jax.tree.map(
        lambda part, zero: jnp.broadcast_to(jnp.asarray(zero, part.dtype), part.shape),
        value,
        identity,
    )

    def step(k, before):
        at = size - 1 - k
        reached = at > index
        new = combine(
            before, jax.tree.map(lambda part, own: part[at].astype(own.dtype), everything, value)
        )
        return jax.tree.map(lambda a, b: jnp.where(reached, a, b), new, before)

    return lax.fori_loop(0, size, step, start)


def layer_norm(values, norm_gain, norm_bias):
    center = values - jnp.mean(values, axis=-1, keepdims=True)
    spread = jnp.mean(center * center, axis=-1, keepdims=True)
    return center * lax.rsqrt(spread + 1e-05) * norm_gain + norm_bias


def decay_tables(delta, alpha):
    input_rate = jax.nn.sigmoid(delta)
    damping = jax.nn.sigmoid(alpha)
    return (input_rate, jnp.log1p(-input_rate * damping))


def toeplitz_rows(kern_part):
    chans = kern_part.shape[0]
    block_len = kern_part.shape[1]
    wrapped = jnp.concatenate(
        [kern_part[:, :1], jnp.zeros((chans, block_len), kern_part.dtype), kern_part[:, :0:-1]],
        axis=1,
    )
    tiled = jnp.tile(wrapped, (1, block_len))[:, : block_len * (2 * block_len - 1)]
    return tiled.reshape(chans, block_len, 2 * block_len - 1)[:, :, :block_len]


def local_conv(normed3, kernel):
    block_len = normed3.shape[1]
    blocks = normed3.shape[2] // 128
    kern_blocks = kernel.reshape(blocks, 128, block_len)
    data_blocks = normed3.reshape(normed3.shape[0], block_len, blocks, 128).transpose(2, 0, 1, 3)

    def one_block(block_pair):
        kern_part, data_part = block_pair
        toeplitz = toeplitz_rows(kern_part)
        return jnp.einsum("dts,bsd->btd", toeplitz, data_part, precision=precise)

    result = lax.map(one_block, (kern_blocks, data_blocks))
    return result.transpose(1, 2, 0, 3).reshape(normed3.shape)


def ema_terms(normed3, delta, alpha, beta, gamma, omega, incoming):
    block_len = normed3.shape[1]
    input_rate, log_decay = decay_tables(delta, alpha)
    step_index = jnp.arange(block_len, dtype=jnp.float32)
    ema_scale = NDIM ** (-0.5)
    powers = jnp.exp(log_decay[:, :, None] * step_index)
    kernel = ema_scale * jnp.einsum(
        "dj,djk->dk", gamma * input_rate * beta, powers, precision=precise
    )
    convolved = local_conv(normed3, kernel)
    carry_table = (
        ema_scale * gamma[:, :, None] * jnp.exp(log_decay[:, :, None] * (step_index + 1.0))
    )
    carried = jnp.einsum("djt,bdj->btd", carry_table, incoming, precision=precise)
    return convolved + carried + omega * normed3


def ema_ends(normed3, delta, alpha, beta):
    block_len = normed3.shape[1]
    input_rate, log_decay = decay_tables(delta, alpha)
    step_index = jnp.arange(block_len, dtype=jnp.float32)
    end_table = (input_rate * beta)[:, :, None] * jnp.exp(
        log_decay[:, :, None] * (block_len - 1.0 - step_index)
    )
    end_states = jnp.einsum("djs,bsd->bdj", end_table, normed3, precision=precise)
    return (jnp.exp(log_decay * block_len), end_states)


def rel_table(position_bias):
    step_index = jnp.arange(position_bias.shape[0])
    offsets = step_index[:, None] - step_index[None, :]
    return jnp.where(offsets >= 0, position_bias[jnp.maximum(offsets, 0)], 0.0)


def masked_softmax(scores):
    step_index = jnp.arange(scores.shape[-1])
    causal = step_index[:, None] >= step_index[None, :]
    masked = jnp.where(causal, scores, -jnp.inf)
    row_top = jnp.max(masked, axis=-1, keepdims=True)
    expo_vals = jnp.exp(masked - row_top)
    return expo_vals / jnp.sum(expo_vals, axis=-1, keepdims=True)


def silu_slope(values):
    logistic = jax.nn.sigmoid(values)
    return logistic * (1.0 + values * (1.0 - logistic))


def matmul(left_mat, right_mat):
    return jnp.dot(left_mat, right_mat, preferred_element_type=jnp.float32)


def left_product(left_mat, right_mat):
    return lax.dot_general(
        left_mat, right_mat, (((0,), (0,)), ((), ())), preferred_element_type=jnp.float32
    )


def right_product(left_mat, right_mat):
    return lax.dot_general(
        left_mat, right_mat, (((1,), (1,)), ((), ())), preferred_element_type=jnp.float32
    )


def column_sums(values):
    return jnp.sum(values.astype(jnp.float32), axis=0)


def shards(
    tokens,
    out_grad,
    norm1_gain,
    norm1_bias,
    value_weight,
    value_bias,
    ema_delta,
    ema_alpha,
    ema_beta,
    ema_gamma,
    ema_omega,
    base_weight,
    base_bias,
    shared_gamma,
    query_offset,
    position_bias,
    proj_weight,
    proj_bias,
    norm2_gain,
    norm2_bias,
    ffn1_weight,
    ffn1_bias,
    ffn2_weight,
    ffn2_bias,
):
    seq_local, block_len, _ = tokens.shape
    row_count = seq_local * block_len
    gathered = (
        lax.all_gather(value_weight.astype(jnp.bfloat16), ("seq", "batch"), axis=0, tiled=True),
        lax.all_gather(base_weight.astype(jnp.bfloat16), ("seq", "batch"), axis=0, tiled=True),
        lax.all_gather(proj_weight.astype(jnp.bfloat16), ("seq", "batch"), axis=0, tiled=True),
        lax.all_gather(ffn1_weight.astype(jnp.bfloat16), ("seq", "batch"), axis=0, tiled=True),
        lax.all_gather(ffn2_weight.astype(jnp.bfloat16), ("seq", "batch"), axis=0, tiled=True),
    )
    value_full, base_full, proj_full, ffn1_full, ffn2_full = gathered
    _, log_decay = decay_tables(ema_delta, ema_alpha)
    block_log = log_decay * block_len

    def chain_step(earlier_pair, later_pair):
        carried = earlier_pair[1] * jnp.exp(block_log * later_pair[0][0])
        return (earlier_pair[0] + later_pair[0], carried + later_pair[1])

    one_block = jnp.ones((1,), jnp.float32)
    no_block = jnp.zeros((1,), jnp.float32)
    tokens_flat = tokens.astype(jnp.float32).reshape(row_count, D)
    normed, norm1_back = jax.vjp(layer_norm, tokens_flat, norm1_gain, norm1_bias)
    normed_low = normed.astype(jnp.bfloat16)
    value_pre = matmul(normed_low, value_full) + value_bias
    value_low = jax.nn.silu(value_pre).astype(jnp.bfloat16)
    normed3 = normed.reshape(seq_local, block_len, D)
    (whole_decay, end_states), ends_back = jax.vjp(
        ema_ends, normed3, ema_delta, ema_alpha, ema_beta
    )
    prefix = entering(
        (one_block, end_states), "seq", chain_step, (no_block, jnp.zeros_like(end_states))
    )
    incoming = prefix[1]
    ema_out, ema_back = jax.vjp(
        ema_terms, normed3, ema_delta, ema_alpha, ema_beta, ema_gamma, ema_omega, incoming
    )
    ema_flat = ema_out.reshape(row_count, D)
    mixed_low = jax.nn.silu(ema_flat).astype(jnp.bfloat16)
    base_pre = matmul(mixed_low, base_full) + base_bias
    update = jax.nn.sigmoid(base_pre[:, :D])
    shared_pre = base_pre[:, D : D + ZD + VD]
    shared_reset = jax.nn.silu(shared_pre)
    shared = shared_reset[:, :ZD]
    reset_gate = shared_reset[:, ZD:]
    hidden_x = base_pre[:, D + ZD + VD :]
    queries = (
        (shared * shared_gamma[0] + query_offset)
        .astype(jnp.bfloat16)
        .reshape(seq_local, block_len, ZD)
    )
    key_rows = (shared * shared_gamma[1]).astype(jnp.bfloat16).reshape(seq_local, block_len, ZD)
    position, position_back = jax.vjp(rel_table, position_bias)
    scores = (
        jnp.einsum("bik,bjk->bij", queries, key_rows, preferred_element_type=jnp.float32)
        * ZD ** (-0.5)
        + position
    )
    attn = masked_softmax(scores)
    attn_low = attn.astype(jnp.bfloat16)
    values3 = value_low.reshape(seq_local, block_len, VD)
    attended = jnp.einsum(
        "bij,bjv->biv", attn_low, values3, preferred_element_type=jnp.float32
    ).reshape(row_count, VD)
    gated_low = (attended * reset_gate).astype(jnp.bfloat16)
    proj_pre = matmul(gated_low, proj_full) + proj_bias
    hidden_sum = hidden_x + proj_pre
    hidden = jax.nn.silu(hidden_sum)
    first_out = tokens_flat + update * (hidden - tokens_flat)
    normed_two, norm2_back = jax.vjp(layer_norm, first_out, norm2_gain, norm2_bias)
    normed_two_low = normed_two.astype(jnp.bfloat16)
    ffn_pre = matmul(normed_two_low, ffn1_full) + ffn1_bias
    ffn_low = jax.nn.silu(ffn_pre).astype(jnp.bfloat16)
    ffn_out = matmul(ffn_low, ffn2_full) + ffn2_bias
    block_out = (first_out + ffn_out).astype(jnp.bfloat16).reshape(seq_local, block_len, D)
    grad_ffn2 = out_grad.reshape(row_count, D)
    dffn2_weight = left_product(ffn_low, grad_ffn2)
    dffn2_bias = column_sums(grad_ffn2)
    grad_ffn1 = (right_product(grad_ffn2, ffn2_full) * silu_slope(ffn_pre)).astype(jnp.bfloat16)
    dffn1_weight = left_product(normed_two_low, grad_ffn1)
    dffn1_bias = column_sums(grad_ffn1)
    grad_first_norm, dnorm2_gain, dnorm2_bias = norm2_back(right_product(grad_ffn1, ffn1_full))
    grad_first = grad_ffn2.astype(jnp.float32) + grad_first_norm
    grad_skip = grad_first * (1.0 - update)
    grad_update = grad_first * (hidden - tokens_flat)
    grad_hidden = grad_first * update * silu_slope(hidden_sum)
    grad_proj = grad_hidden.astype(jnp.bfloat16)
    dproj_weight = left_product(gated_low, grad_proj)
    dproj_bias = column_sums(grad_proj)
    grad_gated = right_product(grad_proj, proj_full)
    grad_attended = (grad_gated * reset_gate).astype(jnp.bfloat16).reshape(seq_local, block_len, VD)
    grad_reset = grad_gated * attended
    grad_attn = jnp.einsum(
        "biv,bjv->bij", grad_attended, values3, preferred_element_type=jnp.float32
    )
    grad_values = jnp.einsum(
        "bij,biv->bjv", attn_low, grad_attended, preferred_element_type=jnp.float32
    ).reshape(row_count, VD)
    grad_scores = (attn * (grad_attn - jnp.sum(grad_attn * attn, axis=-1, keepdims=True))).astype(
        jnp.bfloat16
    )
    (dposition_bias,) = position_back(jnp.sum(grad_scores.astype(jnp.float32), axis=0))
    grad_queries = jnp.einsum(
        "bij,bjk->bik", grad_scores, key_rows, preferred_element_type=jnp.float32
    ).reshape(row_count, ZD) * ZD ** (-0.5)
    grad_keys = jnp.einsum(
        "bij,bik->bjk", grad_scores, queries, preferred_element_type=jnp.float32
    ).reshape(row_count, ZD) * ZD ** (-0.5)
    dshared_gamma = jnp.stack(
        [jnp.sum(grad_queries * shared, axis=0), jnp.sum(grad_keys * shared, axis=0)]
    )
    dquery_offset = jnp.sum(grad_queries, axis=0)
    grad_shared = grad_queries * shared_gamma[0] + grad_keys * shared_gamma[1]
    grad_shared_pre = jnp.concatenate([grad_shared, grad_reset], axis=1) * silu_slope(shared_pre)
    grad_update_pre = grad_update * update * (1.0 - update)
    grad_base = jnp.concatenate([grad_update_pre, grad_shared_pre, grad_hidden], axis=1).astype(
        jnp.bfloat16
    )
    dbase_weight = left_product(mixed_low, grad_base)
    dbase_bias = column_sums(grad_base)
    grad_ema = right_product(grad_base, base_full) * silu_slope(ema_flat)
    grad_value_pre = (grad_values * silu_slope(value_pre)).astype(jnp.bfloat16)
    dvalue_weight = left_product(normed_low, grad_value_pre)
    dvalue_bias = column_sums(grad_value_pre)
    grad_normed = right_product(grad_value_pre, value_full)
    grad_normed_ema, delta_part, alpha_part, beta_part, dema_gamma, dema_omega, grad_incoming = (
        ema_back(grad_ema.reshape(seq_local, block_len, D))
    )
    suffix = prefix_2(
        (one_block, grad_incoming), "seq", chain_step, (no_block, jnp.zeros_like(grad_incoming))
    )
    grad_ends = suffix[1]
    grad_whole = jnp.sum(grad_ends * incoming, axis=0)
    grad_normed_ends, delta_rest, alpha_rest, beta_rest = ends_back((grad_whole, grad_ends))
    dema_delta = delta_part + delta_rest
    dema_alpha = alpha_part + alpha_rest
    dema_beta = beta_part + beta_rest
    grad_normed = grad_normed + (grad_normed_ema + grad_normed_ends).reshape(row_count, D)
    grad_tokens_norm, dnorm1_gain, dnorm1_bias = norm1_back(grad_normed)
    tokens_grad = (
        (grad_skip + grad_tokens_norm).astype(jnp.bfloat16).reshape(seq_local, block_len, D)
    )
    small_sums = lax.psum(
        (
            dnorm1_gain,
            dnorm1_bias,
            dvalue_bias,
            dema_delta,
            dema_alpha,
            dema_beta,
            dema_gamma,
            dema_omega,
            dbase_bias,
            dshared_gamma,
            dquery_offset,
            dposition_bias,
            dproj_bias,
            dnorm2_gain,
            dnorm2_bias,
            dffn1_bias,
            dffn2_bias,
        ),
        ("seq", "batch"),
    )
    reduced = (
        lax.psum_scatter(dvalue_weight, ("seq", "batch"), scatter_dimension=0, tiled=True),
        lax.psum_scatter(dbase_weight, ("seq", "batch"), scatter_dimension=0, tiled=True),
        lax.psum_scatter(dproj_weight, ("seq", "batch"), scatter_dimension=0, tiled=True),
        lax.psum_scatter(dffn1_weight, ("seq", "batch"), scatter_dimension=0, tiled=True),
        lax.psum_scatter(dffn2_weight, ("seq", "batch"), scatter_dimension=0, tiled=True),
    )
    return (
        block_out,
        tokens_grad,
        small_sums[0],
        small_sums[1],
        reduced[0],
        small_sums[2],
        small_sums[3],
        small_sums[4],
        small_sums[5],
        small_sums[6],
        small_sums[7],
        reduced[1],
        small_sums[8],
        small_sums[9],
        small_sums[10],
        small_sums[11],
        reduced[2],
        small_sums[12],
        small_sums[13],
        small_sums[14],
        reduced[3],
        small_sums[15],
        reduced[4],
        small_sums[16],
    )


VMEM_LIMIT = 63 * 1024 * 1024
BF = jnp.bfloat16
F32 = jnp.float32
MESH = pl.DeviceIdType.MESH
SCALE = ZD ** (-0.5)
EMA_SCALE = NDIM ** (-0.5)
BLK = 128
VH = 1024
BASE_COLS = 2176
SM_ROWS = 400
ROW_OMEGA, ROW_N1G, ROW_N1B, ROW_N2G, ROW_N2B = 256, 264, 272, 280, 288
ROW_VB, ROW_BB, ROW_PB, ROW_F1B, ROW_F2B = 296, 312, 345, 353, 385
ROW_SG, ROW_QO, ROW_POS = 393, 395, 396
SMALL_ROWS = (
    (ROW_N1G, 8), (ROW_N1B, 8), (ROW_VB, 16), (ROW_OMEGA, 8), (ROW_BB, 33), (ROW_SG, 2), (ROW_QO, 1),
    (ROW_POS, 1), (ROW_PB, 8), (ROW_N2G, 8), (ROW_N2B, 8), (ROW_F1B, 32), (ROW_F2B, 8),
)
VALUE, BASE, PROJ, FFN1, FFN2 = range(5)
U_V, U_P, U_BA, U_BB, U_1, U_2 = range(6)
Y_FIRST = (U_V,)
X_THEN_Y = (VALUE,)


def pick(flag, yes, no):
    return lax.select(flag, yes, no)


def sig(v):
    return jax.nn.sigmoid(v)


def silu(v):
    return v * sig(v)


def slope(v):
    s = sig(v)
    return s * (1.0 + v * (1.0 - s))


def dot_nn(a, b):
    return jnp.dot(a, b, preferred_element_type=F32)


def dot_nt(a, b):
    return lax.dot_general(a, b, (((1,), (1,)), ((), ())), preferred_element_type=F32)


def dot_tn(a, b):
    return lax.dot_general(a, b, (((0,), (0,)), ((), ())), preferred_element_type=F32)


def split_pair(first, second, low_lanes):
    lo = jnp.where(low_lanes, first, pltpu.roll(second, 64, 1))
    hi = jnp.where(low_lanes, pltpu.roll(first, 64, 1), second)
    return lo, hi


def fold8(v):
    rows, cols = v.shape
    return jnp.sum(v.reshape(rows // 8, 8, cols), axis=0)


def shear(v, left):
    rows = lax.broadcasted_iota(jnp.int32, (BLK, BLK), 0)
    for bit in range(7):
        step = 1 << bit
        turned = pltpu.roll(v, BLK - step if left else step, 1)
        v = jnp.where((rows & step) != 0, turned, v)
    return v


def layer_kernel(NS, *refs):
    NZ = NS // 4
    names = iter(refs)
    take = lambda n: [next(names) for _ in range(n)]
    (tok, og, n1g, n1b, vb) = take(5)
    ema_in = take(4)
    (om_in, bb, sg, qo, pbr, pbias, n2g, n2b, f1b, f2b) = take(10)
    (vw, bw, pw, f1w, f2w) = take(5)
    (o_block, o_tok, o_dv, o_db, o_dp, o_d1, o_d2, o_ema, o_sm) = take(9)
    (SM_OUT, ema, om) = take(3)
    (WV, WB, WP, W1, W2) = take(5)
    (G1, G2, GBA, GBB, RXBB) = take(5)
    RY = take(6)
    RZ = take(6)
    (FV, FB, FXV, FXB, FX1) = take(5)
    (SV, SB, NL, ML, NO, VP, VL, UH, UU, HH, SHP, RP, AD, GT, AT, PR, FO, FP, FG) = take(19)
    (AS, AR, AX, AXR, OX, OXR, OB, GH, GUS, GBS, GA, GAT, GATR, GVP, GNVR) = take(15)
    (XP, YP, GEP, GNP, HC, H8, EC, EXX, EXY, EXZ, BXX, BXY, BXZ, DEC, CIN, LAM, PIN) = take(17)
    (SMR, SMX, SMY, SMZ, SMC) = take(5)
    (in_sem, zs, zr, ys, yr, xs, xr, rxs, rxr, rys, ryr, rzs, rzr, es, er) = take(15)

    s = lax.axis_index("seq")
    b = lax.axis_index("batch")
    x = lax.rem(s, 2)
    y = lax.rem(lax.div(s, 2), 2)
    z = lax.div(s, 4)
    p = lax.div(s, 2)
    q = 2 * x + b
    xs_ = s + 1 - 2 * x
    ys_ = s + 2 - 4 * y
    C = (s, 1 - b)
    X = (xs_, b)
    XC = (xs_, 1 - b)
    Y = (ys_, b)
    ahead = lambda k: lax.rem(s + 4 * k, NS)
    behind = lambda k: lax.rem(s - 4 * k + NS * 4, NS)
    first = b == 0
    al = pl.multiple_of
    rows_of = lambda i, n: pl.ds(al(i * n, n), n)

    loads = [
        pltpu.make_async_copy(src, dst, in_sem.at[i])
        for i, (src, dst) in enumerate(
            ((vw, o_dv), (bw, o_db), (pw, o_dp), (f1w, o_d1), (f2w, o_d2))
        )
    ]
    for load in loads:
        load.start()

    barrier = pltpu.get_barrier_semaphore()
    partners = [C, X, XC, Y] + [(ahead(k), b) for k in range(1, NZ)]
    for device in partners:
        pl.semaphore_signal(barrier, inc=1, device_id=device, device_id_type=MESH)

    def remote(src, dst, send, recv, device):
        return pltpu.make_async_remote_copy(
            src_ref=src, dst_ref=dst, send_sem=send, recv_sem=recv, device_id=device, device_id_type=MESH
        )

    open_sends = []

    def settle(copy):
        open_sends[:] = [other for other in open_sends if other is not copy]

    n_ex = [0]

    def exchange(src, dst, device, landed=None):
        i = n_ex[0]
        n_ex[0] += 1
        copy = remote(src, dst, es.at[i], er.at[i], device)
        copy.start()
        open_sends.append(copy)
        arrival = copy if landed is None else remote(src, landed, es.at[i], er.at[i], device)
        return copy, arrival

    low1 = lambda n: lax.broadcasted_iota(jnp.int32, (n, BLK), 1) < 64

    my_rows = pl.ds(al(64 * s + 32 * b, 32), 32)
    other_rows = pl.ds(al(64 * s + 32 * (1 - b), 32), 32)

    def split_columns(src, src0, blocks, mine_ref, mine_rows, dst0, other_ref):
        low = low1(32)
        for t in range(blocks):
            lo, hi = split_pair(
                src[:, src0 + 256 * t : src0 + 256 * t + 128],
                src[:, src0 + 256 * t + 128 : src0 + 256 * t + 256],
                low,
            )
            cols = slice(dst0 + 128 * t, dst0 + 128 * t + 128)
            mine_ref[mine_rows, cols] = pick(first, lo, hi).astype(BF)
            other_ref[:, cols] = pick(first, hi, lo).astype(BF)

    NT = NO.at[0:512]
    OG = NO.at[512:1024]
    quad = lambda j: rows_of(j, BLK)
    q_c = q + 1 - 2 * b
    q_x = lax.rem(q + 2, 4)
    q_xc = lax.rem(q_c + 2, 4)
    OG[quad(q), :] = og[...]
    loads[0].wait()
    split_columns(o_dv, 0, 8, WV, my_rows, 0, SV)
    pl.semaphore_wait(barrier, len(partners))
    _, got_wv = exchange(SV, WV.at[my_rows], C, WV.at[other_rows])
    gather = [WV, WB, WP, W1, W2]

    def piece(w, chip):
        if w < FFN1:
            return gather[w].at[rows_of(chip, 64)]
        return gather[w].at[rows_of(lax.div(chip, 2), 128)]

    chip_of = lambda plane: 4 * plane + lax.rem(s, 4)

    def route(w):
        return (xs_ - s, ys_ - s, X, Y) if w in X_THEN_Y else (ys_ - s, xs_ - s, Y, X)

    def send_z(w, plane, down, side=0):
        part = piece(w, chip_of(plane) + (ys_ - s if side else 0))
        device = (s - 4, b) if down else (s + 4, b)
        return remote(part, part, zs.at[w, plane, down, side], zr.at[w, plane, side], device)

    def got_z(w, plane, side=0):
        part = piece(w, chip_of(plane) + (ys_ - s if side else 0))
        return remote(part, part, zs.at[w, plane, 0, side], zr.at[w, plane, side], Y)

    def send_y(w, plane):
        part = piece(w, chip_of(plane))
        return remote(part, part, ys.at[w, plane], yr.at[w, plane], route(w)[2])

    def got_y(w, plane):
        part = piece(w, chip_of(plane) + route(w)[0])
        return remote(part, part, ys.at[w, plane], yr.at[w, plane], route(w)[2])

    def send_x(w, plane, far):
        part = piece(w, chip_of(plane) + (route(w)[0] if far else 0))
        return remote(part, part, xs.at[w, far, plane], xr.at[w, far, plane], route(w)[3])

    def got_x(w, plane, far):
        part = piece(w, chip_of(plane) + (route(w)[0] if far else 0) + route(w)[1])
        return remote(part, part, xs.at[w, far, plane], xr.at[w, far, plane], route(w)[3])

    def near_planes(visit, start=1, stop=NZ):
        for j in range(start, stop):
            pl.when(z >= j)(functools.partial(visit, z - j, 0, z < NZ - 1))
            pl.when(z + j <= NZ - 1)(functools.partial(visit, z + j, 1, z > 0))

    def spread_z(w, side=0):
        pl.when(z < NZ - 1)(lambda: send_z(w, z, 0, side).start())
        pl.when(z > 0)(lambda: send_z(w, z, 1, side).start())

    def open_gather(w):
        send_y(w, z).start()
        spread_z(w)
        if w < FFN1:
            send_x(w, z, 0).start()

    def relay_z(w, start=1, stop=NZ):
        def visit(plane, down, more):
            for side in range(2 if w == FFN2 else 1):
                got_z(w, plane, side).wait_recv()
                pl.when(more)(lambda side=side: send_z(w, plane, down, side).start())
            if w < FFN2:
                send_y(w, plane).start()
            if w < FFN1:
                send_x(w, plane, 0).start()

        near_planes(visit, start, stop)

    def relay_y(w):
        def visit(plane, down, more):
            got_y(w, plane).wait_recv()
            if w < FFN1:
                send_x(w, plane, 1).start()

        visit(z, 0, False)
        if w < FFN2:
            near_planes(visit)
        else:
            spread_z(w, 1)

    def finish_x(w):
        def one(k, carry):
            got_x(w, k, 0).wait_recv()
            got_x(w, k, 1).wait_recv()
            return carry

        lax.fori_loop(0, NZ, one, 0)

    def close_gather(w):
        def one(k, carry):
            send_y(w, k).wait_send()
            if w < FFN1:
                send_x(w, k, 0).wait_send()
                send_x(w, k, 1).wait_send()
            return carry

        if w < FFN2:
            lax.fori_loop(0, NZ, one, 0)
        else:
            send_y(w, z).wait_send()
        for side in range(2 if w == FFN2 else 1):
            pl.when(z < NZ - 1)(lambda side=side: send_z(w, z, 0, side).wait_send())
            pl.when(z > 0)(lambda side=side: send_z(w, z, 1, side).wait_send())

            def visit(plane, down, more, side=side):
                pl.when(more)(lambda: send_z(w, plane, down, side).wait_send())

            near_planes(visit)

    def norm_rows(v):
        center = v - jnp.mean(v, axis=-1, keepdims=True)
        rstd = lax.rsqrt(jnp.mean(center * center, axis=-1, keepdims=True) + 1e-05)
        return center * rstd, rstd

    own = rows_of(b, BLK)

    def norm_one(i, carry):
        rows = rows_of(i, 32)
        n, _ = norm_rows(tok[rows, :].astype(F32))
        normed = n * n1g[...] + n1b[...]
        for g in range(8):
            XP[pl.ds(al(128 * g + 32 * i, 32), 32), :] = normed[:, 128 * g : 128 * g + 128]
        NL[pl.ds(al(128 * b + 32 * i, 32), 32), :] = normed.astype(BF)
        return carry

    for g in range(8):
        cols = slice(128 * g, 128 * g + 128)
        om[g : g + 1, :] = om_in[:, cols]
        for a in range(4):
            ema[a, :, g, :] = ema_in[a][:, cols]
    for j in range(NDIM):
        rate = sig(ema[0, j])
        DEC[j] = 1.0 - rate * sig(ema[1, j])
        CIN[j] = rate * ema[2, j]
        lam = DEC[j]
        for _ in range(7):
            lam = lam * lam
        LAM[j] = lam

    def panel(t):
        return pl.ds(t, 8, stride=BLK)

    def end_scan():
        d = [DEC[j] for j in range(NDIM)]
        c = [CIN[j] for j in range(NDIM)]

        def step(t, h):
            row = XP[panel(t), :]
            return tuple(h[j] * d[j] + c[j] * row for j in range(NDIM))

        h = lax.fori_loop(
            0, BLK, step, tuple(jnp.zeros((8, 128), F32) for _ in range(NDIM)), unroll=4
        )
        for j in range(NDIM):
            EC[0, j] = h[j]


    def scan_round_x(own_state, arrived, out, incoming, later):
        for j in range(NDIM):
            l, mine, theirs = LAM[j], own_state[j], arrived[j]
            out[j] = pick(later, l * theirs + mine, l * mine + theirs)
            incoming[j] = pick(later, theirs, jnp.zeros_like(theirs))

    def scan_round_y(own_state, arrived, out, incoming, later, inner):
        for j in range(NDIM):
            l = LAM[j]
            l2 = l * l
            mine, theirs = own_state[j], arrived[j]
            out[j] = pick(later, l2 * theirs + mine, l2 * mine + theirs)
            hop = pick(inner == 1, l, jnp.ones_like(l))
            incoming[j] += pick(later, hop * theirs, jnp.zeros_like(l))

    def scan_round_z(arrived, incoming, reach, inner):
        for j in range(NDIM):
            l = LAM[j]
            l2 = l * l
            l4 = l2 * l2
            one = jnp.ones_like(l)
            hop = pick(lax.rem(inner, 2) == 1, l, one) * pick(inner >= 2, l2, one)
            total = incoming[j]
            for k in range(1, NZ):
                total += pick(k <= reach, hop * arrived[k - 1, j], jnp.zeros_like(l))
                hop = hop * l4
            incoming[j] = total

    loads[1].wait()
    WB[my_rows, 0:512] = o_db[:, pl.ds(al(512 * b, 512), 512)].astype(BF)
    SB[:, 0:512] = o_db[:, pl.ds(al(512 * (1 - b), 512), 512)].astype(BF)
    WB[my_rows, 512:1024] = o_db[:, pl.ds(al(3200 + 512 * b, 128), 512)].astype(BF)
    SB[:, 512:1024] = o_db[:, pl.ds(al(3200 + 512 * (1 - b), 128), 512)].astype(BF)
    shared_cols = o_db[:, 1024:1152].astype(BF)
    WB[my_rows, 1024:1152] = shared_cols
    SB[:, 1024:1152] = shared_cols
    split_columns(o_db, 1152, 8, WB, my_rows, 1152, SB)
    _, got_wb = exchange(SB, WB.at[my_rows], C, WB.at[other_rows])

    copy_og_x, got_og_x = exchange(OG.at[quad(q)], OG.at[quad(q)], X, OG.at[quad(q_x)])
    loads[2].wait()
    WP[rows_of(s, 64), :] = o_dp[...].astype(BF)
    open_gather(PROJ)
    got_wv.wait_recv()
    open_gather(VALUE)
    lax.fori_loop(0, 4, norm_one, 0)
    _, got_nl = exchange(NL.at[own], NL.at[own], C, NL.at[rows_of(1 - b, BLK)])
    end_scan()
    _, got_ex = exchange(EC.at[0], EXX, X)
    got_wb.wait_recv()
    open_gather(BASE)
    loads[4].wait()
    W2[rows_of(p, 128), :] = o_d2[...].astype(BF)
    open_gather(FFN2)

    got_ex.wait_recv()
    scan_round_x(EC.at[0], EXX, EC.at[1], PIN, x == 1)
    _, got_ey = exchange(EC.at[1], EXY, Y)
    loads[3].wait()
    for j in range(4):
        for t in range(8):
            AS[32 * j : 32 * j + 32, 128 * t : 128 * t + 128] = o_d1[
                :, 128 * (4 * t + j) : 128 * (4 * t + j) + 128
            ].astype(BF)
    f1_rows = lambda j: pl.ds(al(128 * p + 32 * j, 32), 32)
    W1[f1_rows(q), :] = AS[rows_of(q, 32), :]
    f1_pairs = [
        exchange(AS.at[rows_of(j, 32)], W1.at[f1_rows(q)], device, W1.at[f1_rows(j)])
        for j, device in ((q_c, C), (q_x, X), (q_xc, XC))
    ]
    copy_og_c, got_og_c = exchange(OG.at[quad(q)], OG.at[quad(q)], C, OG.at[quad(q_c)])
    got_ey.wait_recv()
    scan_round_y(EC.at[1], EXY, EC.at[2], PIN, y == 1, x)
    got_ez = [exchange(EC.at[2], EXZ.at[k - 1], (ahead(k), b))[1] for k in range(1, NZ)]
    for copy, got in f1_pairs:
        copy.wait_send()
        settle(copy)
        got.wait_recv()
    open_gather(FFN1)
    relay_z(VALUE)
    relay_y(FFN2)
    relay_y(VALUE)
    relay_z(BASE)
    relay_y(BASE)
    for got in got_ez:
        got.wait_recv()
    scan_round_z(EXZ, PIN, z, 2 * y + x)

    def forward_scan():
        for half in range(2):
            js = range(8 * half, 8 * half + 8)
            d = [DEC[j] for j in js]
            c = [CIN[j] for j in js]
            g = [EMA_SCALE * ema[3, j] for j in js]

            def group(i, h):
                for n, j in enumerate(js):
                    HC[i, j] = h[n]
                for u in range(8):
                    t = 8 * i + u
                    row = XP[panel(t), :]
                    h = tuple(h[n] * d[n] + c[n] * row for n in range(8))
                    out = g[0] * h[0]
                    for n in range(1, 8):
                        out = out + g[n] * h[n]
                    if half == 0:
                        out = out + om[...] * row
                    else:
                        out = out + YP[panel(t), :]
                    YP[panel(t), :] = out
                return h

            lax.fori_loop(0, 16, group, tuple(PIN[j] for j in js))

    forward_scan()

    def mixed_one(i, carry):
        for g in range(8):
            v = YP[pl.ds(al(128 * g + 32 * i, 32), 32), :]
            ML[pl.ds(al(128 * b + 32 * i, 32), 32), 128 * g : 128 * g + 128] = silu(v).astype(BF)
        return carry

    lax.fori_loop(0, 4, mixed_one, 0)
    _, got_ml = exchange(ML.at[own], ML.at[own], C, ML.at[rows_of(1 - b, BLK)])
    relay_z(PROJ)
    relay_y(PROJ)

    low_row = low1(1)

    def my_half(ref, start):
        parts = []
        for t in range(8):
            lo, hi = split_pair(
                ref[:, start + 256 * t : start + 256 * t + 128],
                ref[:, start + 256 * t + 128 : start + 256 * t + 256],
                low_row,
            )
            parts.append(pick(first, lo, hi))
        return jnp.concatenate(parts, axis=1)

    got_nl.wait_recv()
    finish_x(VALUE)
    vbias = my_half(vb, 0)
    for n in range(2):
        cols = slice(512 * n, 512 * n + 512)
        v = dot_nn(NL[...], WV[:, cols]) + vbias[:, cols]
        VP[:, cols] = v.astype(BF)
        VL[:, cols] = silu(v).astype(BF)

    relay_z(FFN1, 1, 3)
    relay_z(FFN2, 1, 2)

    got_ml.wait_recv()
    finish_x(BASE)
    UH[:, 0:512] = dot_nn(ML[...], WB[:, 0:512]) + bb[:, pl.ds(al(512 * b, 512), 512)]
    UH[:, 512:1024] = dot_nn(ML[...], WB[:, 512:1024]) + bb[:, pl.ds(al(3200 + 512 * b, 128), 512)]
    theirs = rows_of(1 - b, BLK)
    my_cols = pl.ds(al(512 * b, 512), 512)
    their_cols = pl.ds(al(512 * (1 - b), 512), 512)
    copy_u, got_u = exchange(UH.at[theirs, 0:512], UU.at[:, my_cols], C, UU.at[:, their_cols])
    copy_h, got_h = exchange(UH.at[theirs, 512:1024], HH.at[:, my_cols], C, HH.at[:, their_cols])
    UU[:, my_cols] = UH[own, 0:512]
    HH[:, my_cols] = UH[own, 512:1024]
    SHP[...] = dot_nn(ML[...], WB[:, 1024:1152]) + bb[:, 1024:1152]
    rbias = my_half(bb, 1152)
    for n in range(2):
        RP[:, 512 * n : 512 * n + 512] = (
            dot_nn(ML[...], WB[:, 1152 + 512 * n : 1664 + 512 * n]) + rbias[:, 512 * n : 512 * n + 512]
        ).astype(BF)

    relay_z(FFN1, 3)
    relay_z(FFN2, 2, 3)

    shared_of = lambda i: silu(SHP[128 * i : 128 * i + 128, :])

    def queries_keys(i):
        sh = shared_of(i)
        return (sh * sg[0:1, :] + qo[...]).astype(BF), (sh * sg[1:2, :]).astype(BF)

    position = jnp.transpose(shear(jnp.broadcast_to(pbr[...], (BLK, BLK)), False))
    at_row = lax.broadcasted_iota(jnp.int32, (BLK, BLK), 0)
    at_col = lax.broadcasted_iota(jnp.int32, (BLK, BLK), 1)
    causal = at_row >= at_col
    for i in range(2):
        rows = slice(128 * i, 128 * i + 128)
        qs, ks = queries_keys(i)
        scores = jnp.where(causal, dot_nt(qs, ks) * SCALE + position, -jnp.inf)
        e = jnp.exp(scores - jnp.max(scores, axis=-1, keepdims=True))
        attn = e / jnp.sum(e, axis=-1, keepdims=True)
        AT[rows, :] = attn
        low = attn.astype(BF)
        for n in range(2):
            cols = slice(512 * n, 512 * n + 512)
            att = dot_nn(low, VL[rows, cols])
            AD[rows, cols] = att.astype(BF)
            GT[rows, cols] = (att * silu(RP[rows, cols].astype(F32))).astype(BF)

    relay_z(FFN2, 3)

    finish_x(PROJ)
    copy_u.wait_send()
    copy_h.wait_send()
    settle(copy_u)
    settle(copy_h)
    for n in range(2):
        cols = slice(512 * n, 512 * n + 512)
        UH[:, cols] = dot_nn(GT[...], WP[:, cols])
    copy_p, got_p = exchange(UH.at[theirs], PR, C)
    got_u.wait_recv()
    got_h.wait_recv()
    got_p.wait_recv()

    def residual_one(i, carry):
        rows = rows_of(i, 32)
        mine = pl.ds(al(128 * b + 32 * i, 32), 32)
        total = HH[rows, :] + ((UH[mine, :] + PR[rows, :]) + pbias[...])
        HH[rows, :] = total
        base = tok[rows, :].astype(F32)
        out = base + sig(UU[rows, :]) * (silu(total) - base)
        FO[rows, :] = out
        n, _ = norm_rows(out)
        NT[pl.ds(al(128 * q + 32 * i, 32), 32), :] = (n * n2g[...] + n2b[...]).astype(BF)
        return carry

    lax.fori_loop(0, 4, residual_one, 0)
    got_og_x.wait_recv()
    copy_og_xc, got_og_xc = exchange(OG.at[quad(q_x)], OG.at[quad(q_x)], C, OG.at[quad(q_xc)])
    copy_nt_x, got_nt_x = exchange(NT.at[quad(q)], NT.at[quad(q)], X, NT.at[quad(q_x)])
    copy_nt_c, got_nt_c = exchange(NT.at[quad(q)], NT.at[quad(q)], C, NT.at[quad(q_c)])

    relay_y(FFN1)
    got_og_c.wait_recv()
    got_og_xc.wait_recv()
    for m in range(2):
        for n in range(2):
            rows = slice(256 * m, 256 * m + 256)
            cols = slice(512 * n, 512 * n + 512)
            FP[rows, cols] = dot_nt(OG[rows, :], W2[cols, :])
    got_nt_x.wait_recv()
    copy_nt_xc, got_nt_xc = exchange(NT.at[quad(q_x)], NT.at[quad(q_x)], C, NT.at[quad(q_xc)])
    got_nt_c.wait_recv()
    got_nt_xc.wait_recv()

    FL = FG.at[0:512]
    GF = FG.at[512:1024]
    fbias = jnp.concatenate(
        [f1b[:, pl.ds(al(512 * t + 128 * q, 128), 128)] for t in range(8)], axis=1
    )
    for m in range(2):
        for n in range(2):
            rows = slice(256 * m, 256 * m + 256)
            cols = slice(512 * n, 512 * n + 512)
            pre = dot_nn(NT[rows, :], W1[:, cols]) + fbias[:, cols]
            FL[rows, cols] = silu(pre).astype(BF)
            GF[rows, cols] = (FP[rows, cols] * slope(pre)).astype(BF)
    for m in range(2):
        for n in range(2):
            rows = slice(256 * m, 256 * m + 256)
            cols = slice(512 * n, 512 * n + 512)
            AS[rows, cols] = dot_nt(GF[rows, :], W1[cols, :]).astype(BF)

    def reduce_pair(staged, landing):
        copies = []
        for c in range(2):
            there = rows_of(2 * c + 1 - b, BLK)
            copies.append(exchange(staged.at[there], landing.at[rows_of(c, BLK)], C))
        return copies

    def reduce_x(staged, landing, arrivals, out, out_landing):
        for _, arrival in arrivals:
            arrival.wait_recv()

        def one(i, carry):
            mine = pl.ds(al(128 * (2 * (1 - x) + b) + 32 * i, 32), 32)
            got = pl.ds(al(128 * (1 - x) + 32 * i, 32), 32)
            out[rows_of(i, 32), :] = (staged[mine, :].astype(F32) + landing[got, :].astype(F32)).astype(BF)
            return carry

        lax.fori_loop(0, 4, one, 0)
        return exchange(out, out_landing, X)

    def pair_sum(staged, landing, i):
        mine = pl.ds(al(128 * q + 32 * i, 32), 32)
        got = pl.ds(al(128 * x + 32 * i, 32), 32)
        return staged[mine, :].astype(F32) + landing[got, :].astype(F32)

    got_a = reduce_pair(AS, AR)

    def store_row(row, v):
        for g in range(v.shape[1] // 128):
            SM_OUT[row + g : row + g + 1, :] = v[:, 128 * g : 128 * g + 128]

    SM_OUT[...] = jnp.zeros((SM_ROWS, 128), F32)

    def weight_grad(left, right, out, right0, out0, width):
        tile = 512 if width % 512 == 0 else 384
        for m in range(2):
            for n in range(width // tile):
                out[512 * m : 512 * m + 512, out0 + tile * n : out0 + tile * n + tile] = dot_tn(
                    left[:, 512 * m : 512 * m + 512],
                    right[:, right0 + tile * n : right0 + tile * n + tile],
                ).astype(BF)

    grads = [NO, FG, GBA, GBB, G1, G2]
    RXV = W1.at[0:512]
    RXP = W1.at[512:1024]
    RXBA = W2.at[0:512]
    half = [RXV, RXP, RXBA, RXBB]

    def shard(u, chip):
        if u < U_1:
            return rows_of(chip, 64)
        return rows_of(lax.div(chip, 2), 128)

    y_first = Y_FIRST
    hop_x, hop_y = xs_ - s, ys_ - s

    def hops(u):
        return (hop_y, hop_x, Y, X) if u in y_first else (hop_x, hop_y, X, Y)

    def rs_x(u, k, far):
        hop1, hop2, device, _ = hops(u)
        chip = ahead(k) + (hop2 if far else 0)
        src = grads[u].at[shard(u, chip + hop1)]
        slot = half[u].at[pl.ds(al(64 * (2 * k + far), 64), 64)]
        return remote(src, slot, rxs.at[u, k, far], rxr.at[u, k, far], device)

    def rs_y(u, k):
        _, hop2, _, device = hops(u) if u < U_1 else (0, hop_y, X, Y)
        src = grads[u].at[shard(u, ahead(k) + hop2)]
        return remote(src, RY[u].at[k], rys.at[u, k], ryr.at[u, k], device)

    def rs_z(u, k):
        src = grads[u].at[shard(u, ahead(k))]
        return remote(src, RZ[u].at[k - 1], rzs.at[u, k], rzr.at[u, k], (ahead(k), b))

    turn = lambda i: lax.rem(i + 1, NZ)

    def rs_open(u, start=0, stop=None):
        def one(i, carry):
            k = turn(i)
            if u < U_1:
                rs_x(u, k, 1).start()
                rs_x(u, k, 0).start()
            else:
                rs_y(u, k).start()
            return carry

        lax.fori_loop(start, NZ if stop is None else stop, one, 0)

    def rs_pass_x(u, start=0, stop=None):
        def one(i, carry):
            k = turn(i)
            for far in (1, 0):
                rs_x(u, k, far).wait_recv()
                rows = shard(u, ahead(k) + (hops(u)[1] if far else 0))
                got = half[u][pl.ds(al(64 * (2 * k + far), 64), 64), :]
                grads[u][rows, :] = (grads[u][rows, :].astype(F32) + got.astype(F32)).astype(BF)
                if far == 1:
                    rs_y(u, k).start()
            return carry

        lax.fori_loop(start, NZ if stop is None else stop, one, 0)

    def rs_pass_y(u, start=0, stop=None):
        def one(i, carry):
            k = i + 1
            rs_y(u, k).wait_recv()
            rows = shard(u, ahead(k))
            grads[u][rows, :] = (grads[u][rows, :].astype(F32) + RY[u][k].astype(F32)).astype(BF)
            rs_z(u, k).start()
            return carry

        lax.fori_loop(start, NZ - 1 if stop is None else stop, one, 0)
        if stop is None:
            rs_y(u, 0).wait_recv()

    def rs_total(u, rows_in):
        rows = shard(u, s)
        size = 64 if u < U_1 else 128
        start = size * (s if u < U_1 else p)
        at = pl.ds(al(start + rows_in[0], 16), rows_in[1])
        in_ = pl.ds(al(rows_in[0], 16), rows_in[1])
        total = grads[u][at, :].astype(F32) + RY[u][0, in_, :].astype(F32)
        for k in range(1, NZ):
            total += RZ[u][k - 1, in_, :].astype(F32)
        return total

    def rs_wait_z(u):
        def one(k, carry):
            rs_z(u, k).wait_recv()
            return carry

        lax.fori_loop(1, NZ, one, 0)

    def column_sum(ref, start, width):
        def one(i, acc):
            return acc + fold8(ref[rows_of(i, 32), start : start + width].astype(F32))

        acc = lax.fori_loop(0, ref.shape[0] // 32, one, jnp.zeros((8, width), F32))
        return jnp.sum(acc, axis=0, keepdims=True)

    def back_two(i, carry):
        rows = rows_of(i, 32)
        a = pair_sum(AS, AR, i) + AXR[rows, :].astype(F32)
        n, rstd = norm_rows(FO[rows, :])
        g = a * n2g[...]
        grad = og[rows, :].astype(F32) + (
            g - jnp.mean(g, axis=-1, keepdims=True) - n * jnp.mean(g * n, axis=-1, keepdims=True)
        ) * rstd
        update = sig(UU[rows, :])
        total = HH[rows, :]
        logistic = sig(total)
        base = tok[rows, :].astype(F32)
        gh = (grad * update * (logistic * (1.0 + total * (1.0 - logistic)))).astype(BF)
        GH[pl.ds(al(128 * b + 32 * i, 32), 32), :] = gh
        GUS[rows, :] = (grad * (total * logistic - base) * update * (1.0 - update)).astype(BF)
        PR[rows, :] = grad * (1.0 - update)
        return (
            carry[0] + fold8(a * n),
            carry[1] + fold8(a),
            carry[2] + fold8(gh.astype(F32)),
            carry[3] + fold8(og[rows, :].astype(F32)),
        )

    weight_grad(FL, OG, G2, 0, 0, 1024)
    rs_open(U_2)
    close_gather(FFN1)
    a_x = reduce_x(AS, AR, got_a, AX, AXR)
    for m in range(2):
        for n in range(2):
            rows = slice(256 * m, 256 * m + 256)
            cols = slice(512 * n, 512 * n + 512)
            FP[rows, cols] = dot_nn(FL[rows, :], W2[:, cols])
    got_o = reduce_pair(FP, GNVR)
    close_gather(FFN2)
    weight_grad(NT, GF, G1, 0, 0, 1024)
    rs_open(U_1, 0, 2)
    f1_sum = column_sum(GF, 0, 1024)
    for t in range(8):
        SM_OUT[pl.ds(ROW_F1B + 4 * t + q, 1), :] = f1_sum[:, 128 * t : 128 * t + 128]
    o_x = reduce_x(FP, GNVR, got_o, OX, OXR)

    def out_one(i, carry):
        OB[rows_of(i, 32), :] = pair_sum(FP, GNVR, i)
        return carry

    lax.fori_loop(0, 4, out_one, 0)
    rs_pass_y(U_2, 0, 1)

    a_x[1].wait_recv()
    zero8 = jnp.zeros((8, 1024), F32)
    sums = lax.fori_loop(0, 4, back_two, (zero8, zero8, zero8, zero8))
    _, got_gh = exchange(GH.at[own], GH.at[own], C, GH.at[theirs])
    _, got_gu = exchange(GUS.at[:, their_cols], GBS.at[own, 0:512], C, GBS.at[theirs, 0:512])
    GBS[own, 0:512] = GUS[:, my_cols]
    for row, acc in zip((ROW_N2G, ROW_N2B, ROW_PB, ROW_F2B), sums):
        store_row(row, jnp.sum(acc, axis=0, keepdims=True))
    rs_pass_y(U_2, 1, 2)

    got_gh.wait_recv()
    got_gu.wait_recv()
    GBS[:, 512:1024] = GH[:, my_cols]
    weight_grad(ML, GBS, GBA, 0, 0, 1024)
    o_x[1].wait_recv()
    rs_open(U_BA)
    for n in range(2):
        cols = slice(512 * n, 512 * n + 512)
        gg = dot_nt(GH[...], WP[cols, :])
        pre = RP[:, cols].astype(F32)
        logistic = sig(pre)
        GA[:, cols] = (gg * (pre * logistic)).astype(BF)
        GBS[:, 1152 + 512 * n : 1664 + 512 * n] = (
            gg * AD[:, cols].astype(F32) * (logistic * (1.0 + pre * (1.0 - logistic)))
        ).astype(BF)
    for i in range(2):
        rows = slice(128 * i, 128 * i + 128)
        GAT[rows, :] = dot_nt(GA[rows, :], VL[rows, :])
    _, got_gat = exchange(GAT, GATR, C)
    weight_grad(GT, GH, FG, 0, 0, 1024)
    for i in range(2):
        rows = slice(128 * i, 128 * i + 128)
        low = AT[rows, :].astype(BF)
        for n in range(2):
            cols = slice(512 * n, 512 * n + 512)
            gv = dot_tn(low, GA[rows, cols])
            GVP[rows, cols] = (gv * slope(VP[rows, cols].astype(F32))).astype(BF)
    got_gat.wait_recv()
    for i in range(2):
        rows = slice(128 * i, 128 * i + 128)
        attn = AT[rows, :]
        gat = GAT[rows, :] + GATR[rows, :]
        gs = (attn * (gat - jnp.sum(gat * attn, axis=-1, keepdims=True))).astype(BF)
        qs, ks = queries_keys(i)
        gq = dot_nn(gs, ks) * SCALE
        gk = dot_tn(gs, qs) * SCALE
        pre = SHP[rows, :]
        sh = silu(pre)
        gsp = (gq * sg[0:1, :] + gk * sg[1:2, :]) * slope(pre)
        GBS[rows, 1024:1152] = (gsp * 0.5).astype(BF)
        mine = b == i

        @pl.when(mine)
        def _(gs=gs, gq=gq, gk=gk, sh=sh):
            SM_OUT[ROW_SG : ROW_SG + 1, :] = jnp.sum(gq * sh, axis=0, keepdims=True)
            SM_OUT[ROW_SG + 1 : ROW_SG + 2, :] = jnp.sum(gk * sh, axis=0, keepdims=True)
            SM_OUT[ROW_QO : ROW_QO + 1, :] = jnp.sum(gq, axis=0, keepdims=True)
            SM_OUT[ROW_POS : ROW_POS + 1, :] = jnp.sum(
                shear(jnp.transpose(gs.astype(F32)), True), axis=0, keepdims=True
            )

    GM = FP.at[0:256]
    GNV = FP.at[256:512]
    for copy, _ in got_o:
        copy.wait_send()
        settle(copy)
    for n in range(2):
        cols = slice(512 * n, 512 * n + 512)
        GM[:, cols] = dot_nt(GBS[...], WB[cols, :])
    _, got_gm = exchange(GM.at[theirs], GNVR.at[0:128], C)
    for n in range(2):
        cols = slice(512 * n, 512 * n + 512)
        GNV[:, cols] = dot_nt(GVP[...], WV[cols, :])
    _, got_gnv = exchange(GNV.at[theirs], GNVR.at[128:256], C)
    GBS[:, 1024:1152] = (GBS[:, 1024:1152].astype(F32) * 2.0).astype(BF)
    rs_pass_y(U_2, 2)

    def grad_ema_one(i, carry):
        for g in range(8):
            cols = slice(128 * g, 128 * g + 128)
            rows = pl.ds(al(128 * g + 32 * i, 32), 32)
            v = GM[pl.ds(al(128 * b + 32 * i, 32), 32), cols] + GNVR[rows_of(i, 32), cols]
            GEP[rows, :] = v * slope(YP[rows, :])
        return carry

    def adjoint_end():
        d = [DEC[j] for j in range(NDIM)]

        def step(i, g):
            row = GEP[panel(BLK - 1 - i), :]
            return tuple(g[j] * d[j] + row for j in range(NDIM))

        g = lax.fori_loop(
            0, BLK, step, tuple(jnp.zeros((8, 128), F32) for _ in range(NDIM)), unroll=4
        )
        for j in range(NDIM):
            EC[3, j] = g[j]

    got_gm.wait_recv()
    lax.fori_loop(0, 4, grad_ema_one, 0)
    adjoint_end()
    _, got_bx = exchange(EC.at[3], BXX, X)
    rs_open(U_P)
    rs_pass_x(U_BA, 0, 2)
    got_bx.wait_recv()
    scan_round_x(EC.at[3], BXX, EC.at[4], PIN, x == 0)
    _, got_by = exchange(EC.at[4], BXY, Y)
    rs_open(U_1, 2)
    for copy in (copy_og_c, copy_og_x, copy_og_xc, copy_nt_x, copy_nt_c, copy_nt_xc):
        copy.wait_send()
        settle(copy)
    weight_grad(NL, GVP, NO, 0, 0, 1024)
    rs_pass_y(U_1, 0, 2)
    rs_pass_x(U_BA, 2)
    got_by.wait_recv()
    scan_round_y(EC.at[4], BXY, EC.at[5], PIN, y == 0, 1 - x)
    got_bz = [
        exchange(EC.at[5], BXZ.at[k - 1], (ahead(NZ - k), b))[1] for k in range(1, NZ)
    ]
    rs_open(U_V)
    weight_grad(ML, GBS, GBB, 1024, 0, 1152)
    rs_open(U_BB, 0, 2)
    base_sum = column_sum(GBS, 0, BASE_COLS)
    for t in range(4):
        cols = slice(128 * t, 128 * t + 128)
        SM_OUT[pl.ds(ROW_BB + 4 * b + t, 1), :] = base_sum[:, cols]
        SM_OUT[pl.ds(ROW_BB + 25 + 4 * b + t, 1), :] = base_sum[:, 512 + 128 * t : 640 + 128 * t]
    SM_OUT[ROW_BB + 8 : ROW_BB + 9, :] = base_sum[:, 1024:1152] * 0.5

    low_float = low_row.astype(F32)
    keep = pick(first, low_float, 1.0 - low_float)

    def store_half(row, v):
        for t in range(8):
            block = v[:, 128 * t : 128 * t + 128]
            turned = pltpu.roll(block, 64, 1)
            SM_OUT[row + 2 * t : row + 2 * t + 1, :] = keep * pick(first, block, turned)
            SM_OUT[row + 2 * t + 1 : row + 2 * t + 2, :] = keep * pick(first, turned, block)

    store_half(ROW_BB + 9, base_sum[:, 1152:2176])
    store_half(ROW_VB, column_sum(GVP, 0, 1024))

    def block_out_one(i, carry):
        rows = rows_of(i, 32)
        o_block[rows, :] = (
            FO[rows, :] + ((OB[rows, :] + OXR[rows, :].astype(F32)) + f2b[...])
        ).astype(BF)
        return carry

    lax.fori_loop(0, 4, block_out_one, 0)
    rs_pass_y(U_BA, 0, 2)
    for got in got_bz:
        got.wait_recv()
    scan_round_z(BXZ, PIN, NZ - 1 - z, 2 * (1 - y) + 1 - x)
    rs_pass_y(U_1, 2)
    def backward_scan():
        for part in range(2):
            js = range(8 * part, 8 * part + 8)
            d = [DEC[j] for j in js]
            c = [CIN[j] for j in js]
            e = [EMA_SCALE * CIN[j] * ema[3, j] for j in js]

            def group(i, carry):
                at = 15 - i
                h = tuple(HC[at, j] for j in js)
                for u in range(8):
                    for n in range(8):
                        H8[u, n] = h[n]
                    if u < 7:
                        row = XP[panel(8 * at + u), :]
                        h = tuple(h[n] * d[n] + c[n] * row for n in range(8))
                g, s1, m = carry
                for u in range(7, -1, -1):
                    t = 8 * at + u
                    row = XP[panel(t), :]
                    ge = GEP[panel(t), :]
                    g = tuple(g[n] * d[n] + ge for n in range(8))
                    s1 = tuple(s1[n] + row * g[n] for n in range(8))
                    m = tuple(m[n] + g[n] * H8[u, n] for n in range(8))
                    out = e[0] * g[0]
                    for n in range(1, 8):
                        out = out + e[n] * g[n]
                    if part == 0:
                        out = out + om[...] * ge
                    else:
                        out = out + GNP[panel(t), :]
                    GNP[panel(t), :] = out
                return g, s1, m

            zeros = tuple(jnp.zeros((8, 128), F32) for _ in range(8))
            _, s1, m = lax.fori_loop(0, 16, group, (tuple(PIN[j] for j in js), zeros, zeros))
            for n, j in enumerate(js):
                SM_OUT[8 * j : 8 * j + 8, :] = s1[n]
                SM_OUT[128 + 8 * j : 128 + 8 * j + 8, :] = m[n]

    backward_scan()
    rs_pass_y(U_BA, 2)
    rs_pass_x(U_P, 0, 2)

    for g in range(8):
        rows = slice(128 * g, 128 * g + 128)
        SM_OUT[ROW_OMEGA + g : ROW_OMEGA + g + 1, :] = jnp.sum(
            fold8(XP[rows, :] * GEP[rows, :]), axis=0, keepdims=True
        )

    got_gnv.wait_recv()

    def back_one(i, carry):
        rows = rows_of(i, 32)
        wide = jnp.concatenate(
            [GNP[pl.ds(al(128 * g + 32 * i, 32), 32), :] for g in range(8)], axis=1
        )
        a = (GNV[pl.ds(al(128 * b + 32 * i, 32), 32), :] + GNVR[pl.ds(al(128 + 32 * i, 32), 32), :]) + wide
        n, rstd = norm_rows(tok[rows, :].astype(F32))
        g = a * n1g[...]
        back = (
            g - jnp.mean(g, axis=-1, keepdims=True) - n * jnp.mean(g * n, axis=-1, keepdims=True)
        ) * rstd
        o_tok[rows, :] = (PR[rows, :] + back).astype(BF)
        return carry[0] + fold8(a * n), carry[1] + fold8(a)

    sums = lax.fori_loop(0, 4, back_one, (zero8, zero8))
    for row, acc in zip((ROW_N1G, ROW_N1B), sums):
        store_row(row, jnp.sum(acc, axis=0, keepdims=True))

    half_rows = SM_ROWS // 2
    my_part = rows_of(b, half_rows)
    their_part = rows_of(1 - b, half_rows)
    copy_c, got_c = exchange(SM_OUT.at[their_part], SMR, C)
    rs_pass_x(U_P, 2)
    got_c.wait_recv()
    SMX[0] = SM_OUT[my_part, :] + SMR[...]
    _, got_sx = exchange(SMX.at[0], SMX.at[1], X)
    rs_open(U_BB, 2)
    rs_pass_y(U_P, 0, 2)
    rs_pass_x(U_BB, 0, 2)
    got_sx.wait_recv()
    SMY[0] = SMX[0] + SMX[1]
    _, got_sy = exchange(SMY.at[0], SMY.at[1], Y)
    rs_pass_x(U_V)
    rs_pass_y(U_P, 2)
    rs_pass_x(U_BB, 2)
    got_sy.wait_recv()
    SMZ[0] = SMY[0] + SMY[1]
    got_sz = [exchange(SMZ.at[0], SMZ.at[k], (ahead(k), b))[1] for k in range(1, NZ)]
    rs_wait_z(U_2)
    for i in range(4):
        o_d2[32 * i : 32 * i + 32, :] = rs_total(U_2, (32 * i, 32))
    rs_wait_z(U_1)
    for i in range(4):
        o_d1[:, 1024 * i : 1024 * i + 1024] = rs_total(U_1, (32 * i, 32))
    quarter = lambda j: pl.ds(al(1024 * j, 1024), 1024)
    d1_pairs = [
        exchange(o_d1.at[:, quarter(j)], FX1.at[q], device, FX1.at[j])
        for j, device in ((q_c, C), (q_x, X), (q_xc, XC))
    ]
    mine32 = 32 * b
    their32 = 32 * (1 - b)
    h_mine = pl.ds(al(3200 + 512 * b, 128), 512)
    h_their = pl.ds(al(3200 + 512 * (1 - b), 128), 512)
    low = low1(32)

    def merge(out, start, own_half, other_half):
        for t in range(8):
            cols = slice(128 * t, 128 * t + 128)
            m, o = own_half[:, cols], other_half[:, cols]
            lo, hi = pick(first, m, o), pick(first, o, m)
            at = start + 256 * t
            out[:, at : at + 128] = jnp.where(low, lo, pltpu.roll(hi, 64, 1))
            out[:, at + 128 : at + 256] = jnp.where(low, pltpu.roll(lo, 64, 1), hi)

    rs_wait_z(U_BA)
    FB[:, 0:1024] = rs_total(U_BA, (their32, 32))
    _, got_ba = exchange(FB.at[:, 0:1024], FXB.at[:, 0:1024], C)
    part = rs_total(U_BA, (mine32, 32))
    o_db[:, my_cols] = part[:, 0:512]
    o_db[:, h_mine] = part[:, 512:1024]
    rs_pass_y(U_V)
    rs_pass_y(U_BB, 0, 2)
    for got in got_sz:
        got.wait_recv()
    total = SMZ[lax.rem(z, NZ)]
    for k in range(1, NZ):
        total = total + SMZ[lax.rem(z + NZ - k, NZ)]
    SM_OUT[my_part, :] = total
    _, got_cc = exchange(SM_OUT.at[my_part], SMC, C)

    rs_wait_z(U_P)
    for i in range(2):
        o_dp[32 * i : 32 * i + 32, :] = rs_total(U_P, (32 * i, 32))
    rs_pass_y(U_BB, 2)
    copy_c.wait_send()
    settle(copy_c)
    got_cc.wait_recv()
    SM_OUT[their_part, :] = SMC[...]
    for j in range(NDIM):
        rate, damping = sig(ema[0, j]), sig(ema[1, j])
        beta, gamma = ema[2, j], EMA_SCALE * ema[3, j]
        s1 = SM_OUT[8 * j : 8 * j + 8, :]
        m = gamma * SM_OUT[128 + 8 * j : 136 + 8 * j, :]
        o_ema[0, j] = (beta * gamma * s1 - damping * m) * rate * (1.0 - rate)
        o_ema[1, j] = -rate * m * damping * (1.0 - damping)
        o_ema[2, j] = gamma * rate * s1
        o_ema[3, j] = EMA_SCALE * rate * beta * s1

    o_sm[...] = SM_OUT[...]
    rs_wait_z(U_V)
    FV[...] = rs_total(U_V, (their32, 32))
    _, got_v = exchange(FV, FXV, C)
    part_v = rs_total(U_V, (mine32, 32))

    got_ba.wait_recv()
    o_db[:, their_cols] = FXB[:, 0:512]
    o_db[:, h_their] = FXB[:, 512:1024]
    FX1[q] = o_d1[:, quarter(q)]
    for copy, got in d1_pairs:
        copy.wait_send()
        settle(copy)
        got.wait_recv()
    for j in range(4):
        for t in range(8):
            o_d1[:, 128 * (4 * t + j) : 128 * (4 * t + j) + 128] = FX1[j, :, 128 * t : 128 * t + 128]

    rs_wait_z(U_BB)
    FB[:, 1024:2176] = rs_total(U_BB, (their32, 32))
    _, got_bb = exchange(FB.at[:, 1024:2176], FXB.at[:, 1024:2176], C)
    part = rs_total(U_BB, (mine32, 32))
    o_db[:, 1024:1152] = part[:, 0:128]
    got_bb.wait_recv()
    merge(o_db, 1152, part[:, 128:1152], FXB[:, 1152:2176])
    got_v.wait_recv()
    merge(o_dv, 0, part_v, FXV[...])

    for copy in open_sends:
        copy.wait_send()
    for w in (VALUE, BASE, PROJ):
        close_gather(w)

    def close_sums(u):
        def one(k, carry):
            rs_y(u, k).wait_send()
            if u < U_1:
                rs_x(u, k, 0).wait_send()
                rs_x(u, k, 1).wait_send()
            return carry

        lax.fori_loop(0, NZ, one, 0)

        def plane(k, carry):
            rs_z(u, k).wait_send()
            return carry

        lax.fori_loop(1, NZ, plane, 0)

    for u in (U_V, U_P, U_BA, U_BB, U_1, U_2):
        close_sums(u)


def hand_on_kernel(*refs):
    large, (ema, sums), outs = refs[:7], refs[7:9], refs[9:]
    for src, dst in zip(large, outs):
        dst[...] = src[...]
    for a in range(4):
        for g in range(8):
            outs[7 + a][:, 128 * g : 128 * g + 128] = ema[a, :, g, :]
    for out, (row, n) in zip(outs[11:], SMALL_ROWS):
        if out.shape[0] == 1:
            for g in range(n):
                out[:, 128 * g : 128 * g + 128] = sums[row + g : row + g + 1, :]
        else:
            out[...] = sums[row : row + n, :]


def fast_shards(
    tokens,
    out_grad,
    norm1_gain,
    norm1_bias,
    value_weight,
    value_bias,
    ema_delta,
    ema_alpha,
    ema_beta,
    ema_gamma,
    ema_omega,
    base_weight,
    base_bias,
    shared_gamma,
    query_offset,
    position_bias,
    proj_weight,
    proj_bias,
    norm2_gain,
    norm2_bias,
    ffn1_weight,
    ffn1_bias,
    ffn2_weight,
    ffn2_bias,
):
    NS = lax.axis_size("seq")
    NZ = NS // 4
    row = lambda v: v.reshape(1, -1)
    small = [
        tokens[0], out_grad[0], row(norm1_gain), row(norm1_bias), row(value_bias),
        ema_delta.T, ema_alpha.T, ema_beta.T, ema_gamma.T,
        row(ema_omega), row(base_bias), shared_gamma, row(query_offset),
        row(position_bias), row(proj_bias), row(norm2_gain), row(norm2_bias), row(ffn1_bias),
        row(ffn2_bias),
    ]
    large = [value_weight, base_weight, proj_weight, ffn1_weight, ffn2_weight]
    f = lambda *shape: jax.ShapeDtypeStruct(shape, F32)
    h = lambda *shape: jax.ShapeDtypeStruct(shape, BF)
    outs = [
        h(128, 1024), h(128, 1024), f(32, 2048), f(32, 4224), f(64, 1024), f(32, 4096), f(128, 1024),
        f(4, NDIM, 8, 128),
    ]
    outs.append(f(SM_ROWS, 128))
    vm = lambda *shape: pltpu.VMEM(shape, BF)
    vf = lambda *shape: pltpu.VMEM(shape, F32)
    dma = lambda *shape: pltpu.SemaphoreType.DMA(shape)
    scratch = [
        vf(SM_ROWS, 128), vf(4, NDIM, 8, 128), vf(8, 128),
        vm(1024, 1024), vm(1024, BASE_COLS), vm(1024, 1024), vm(1024, 1024), vm(1024, 1024),
        vm(1024, 1024), vm(1024, 1024), vm(1024, 1024), vm(1024, 1152), vm(512, 1152),
        vm(NZ, 64, 1024), vm(NZ, 64, 1024), vm(NZ, 64, 1024), vm(NZ, 64, 1152),
        vm(NZ, 128, 1024), vm(NZ, 128, 1024),
        vm(NZ - 1, 64, 1024), vm(NZ - 1, 64, 1024), vm(NZ - 1, 64, 1024), vm(NZ - 1, 64, 1152),
        vm(NZ - 1, 128, 1024), vm(NZ - 1, 128, 1024),
        vf(32, 1024), vf(32, BASE_COLS), vf(32, 1024), vf(32, BASE_COLS), vf(4, 32, 1024),
        vm(32, 1024), vm(32, BASE_COLS), vm(256, 1024), vm(256, 1024), vm(1024, 1024),
        vm(256, 1024), vm(256, 1024), vf(256, 1024), vf(128, 1024), vf(128, 1024), vf(256, 128),
        vm(256, 1024), vm(256, 1024), vm(256, 1024), vf(256, 128), vf(128, 1024), vf(128, 1024),
        vf(512, 1024), vm(1024, 1024),
        vm(512, 1024), vm(256, 1024), vm(128, 1024), vm(128, 1024), vm(128, 1024), vm(128, 1024), vf(128, 1024),
        vm(256, 1024), vm(128, 1024), vm(256, BASE_COLS), vm(256, 1024), vf(256, 128), vf(256, 128),
        vm(256, 1024), vf(256, 1024),
        vf(1024, 128), vf(1024, 128), vf(1024, 128), vf(1024, 128), vf(16, NDIM, 8, 128), vf(8, 8, 8, 128),
        vf(6, NDIM, 8, 128), vf(NDIM, 8, 128), vf(NDIM, 8, 128), vf(NZ - 1, NDIM, 8, 128),
        vf(NDIM, 8, 128), vf(NDIM, 8, 128), vf(NZ - 1, NDIM, 8, 128),
        vf(NDIM, 8, 128), vf(NDIM, 8, 128), vf(NDIM, 8, 128), vf(NDIM, 8, 128),
        vf(SM_ROWS // 2, 128), vf(2, SM_ROWS // 2, 128), vf(2, SM_ROWS // 2, 128),
        vf(NZ, SM_ROWS // 2, 128), vf(SM_ROWS // 2, 128),
        dma(5), dma(5, NZ, 2, 2), dma(5, NZ, 2), dma(5, NZ), dma(5, NZ), dma(3, 2, NZ), dma(3, 2, NZ),
        dma(4, NZ, 2), dma(4, NZ, 2), dma(6, NZ), dma(6, NZ), dma(6, NZ), dma(6, NZ), dma(64), dma(64),
    ]
    results = pl.pallas_call(
        functools.partial(layer_kernel, NS),
        out_shape=outs,
        in_specs=[pl.BlockSpec(memory_space=pltpu.VMEM)] * len(small)
        + [pl.BlockSpec(memory_space=pl.ANY)] * len(large),
        out_specs=[pl.BlockSpec(memory_space=pltpu.VMEM)] * len(outs),
        scratch_shapes=scratch,
        compiler_params=pltpu.CompilerParams(
            collective_id=0, has_side_effects=True, vmem_limit_bytes=VMEM_LIMIT
        ),
    )(*small, *large)
    final = list(outs[:7]) + [f(NDIM, D)] * 4
    final += [f(2, 128) if row == ROW_SG else f(1, 128 * n) for row, n in SMALL_ROWS]
    local = pl.BlockSpec(memory_space=pltpu.VMEM)
    (block_out, tokens_grad, dvalue, dbase, dproj, dffn1, dffn2, ddelta, dalpha, dbeta, dgamma, *sums) = (
        pl.pallas_call(
            hand_on_kernel,
            out_shape=final,
            in_specs=[local] * 9,
            out_specs=[local] * len(final),
        )(*results)
    )
    (dn1g, dn1b, dvb, dom, dbb, dsg, dqo, dpos, dpb, dn2g, dn2b, df1b, df2b) = [
        v if v.shape[0] == 2 else v.reshape(-1) for v in sums
    ]
    return (
        block_out[None],
        tokens_grad[None],
        dn1g,
        dn1b,
        dvalue,
        dvb,
        ddelta.T,
        dalpha.T,
        dbeta.T,
        dgamma.T,
        dom,
        dbase,
        dbb,
        dsg,
        dqo,
        dpos,
        dproj,
        dpb,
        dn2g,
        dn2b,
        dffn1,
        df1b,
        dffn2,
        df2b,
    )


def solution(mesh):
    in_specs = (
        P("batch", "seq", None),
        P("batch", "seq", None),
        P(),
        P(),
        P(("seq", "batch"), None),
        P(),
        P(),
        P(),
        P(),
        P(),
        P(),
        P(("seq", "batch"), None),
        P(),
        P(),
        P(),
        P(),
        P(("seq", "batch"), None),
        P(),
        P(),
        P(),
        P(("seq", "batch"), None),
        P(),
        P(("seq", "batch"), None),
        P(),
    )
    out_specs = (
        P("batch", "seq", None),
        P("batch", "seq", None),
        P(),
        P(),
        P(("seq", "batch"), None),
        P(),
        P(),
        P(),
        P(),
        P(),
        P(),
        P(("seq", "batch"), None),
        P(),
        P(),
        P(),
        P(),
        P(("seq", "batch"), None),
        P(),
        P(),
        P(),
        P(("seq", "batch"), None),
        P(),
        P(("seq", "batch"), None),
        P(),
    )
    one_device = fast_shards if mesh.shape['seq'] == 16 else shards
    return jax.shard_map(
        one_device, mesh=mesh, in_specs=in_specs, out_specs=out_specs, check_vma=False
    )
```

```python
import functools

import jax
import jax.numpy as jnp
from jax import lax
from jax.experimental import pallas as pl
from jax.experimental.pallas import tpu as pltpu
from jax.sharding import PartitionSpec as P

D = 1024
ZD = 128
VD = 2048
NDIM = 16


precise = lax.Precision.HIGHEST


def entering(part, axis, combine, identity):
    place = lax.axis_index(axis)
    gathered = jax.tree.map(lambda a: lax.all_gather(a, axis), part)
    state = jax.tree.map(lambda a, e: jnp.zeros_like(a) + jnp.asarray(e, a.dtype), part, identity)

    def one(step, state):
        return combine(
            state, jax.tree.map(lambda a: lax.dynamic_index_in_dim(a, step, 0, False), gathered)
        )

    return lax.fori_loop(0, place, one, state)


def prefix_2(value, axis, combine, identity):
    size, index = (lax.axis_size(axis), lax.axis_index(axis))
    everything = jax.tree.map(
        lambda part, kind: lax.all_gather(part.astype(kind), axis),
        value,
        jax.tree.map(lambda a: jnp.bfloat16 if a.dtype == jnp.float32 else a.dtype, value),
    )
    start = jax.tree.map(
        lambda part, zero: jnp.broadcast_to(jnp.asarray(zero, part.dtype), part.shape),
        value,
        identity,
    )

    def step(k, before):
        at = size - 1 - k
        reached = at > index
        new = combine(
            before, jax.tree.map(lambda part, own: part[at].astype(own.dtype), everything, value)
        )
        return jax.tree.map(lambda a, b: jnp.where(reached, a, b), new, before)

    return lax.fori_loop(0, size, step, start)


def layer_norm(values, norm_gain, norm_bias):
    center = values - jnp.mean(values, axis=-1, keepdims=True)
    spread = jnp.mean(center * center, axis=-1, keepdims=True)
    return center * lax.rsqrt(spread + 1e-05) * norm_gain + norm_bias


def decay_tables(delta, alpha):
    input_rate = jax.nn.sigmoid(delta)
    damping = jax.nn.sigmoid(alpha)
    return (input_rate, jnp.log1p(-input_rate * damping))


def toeplitz_rows(kern_part):
    chans = kern_part.shape[0]
    block_len = kern_part.shape[1]
    wrapped = jnp.concatenate(
        [kern_part[:, :1], jnp.zeros((chans, block_len), kern_part.dtype), kern_part[:, :0:-1]],
        axis=1,
    )
    tiled = jnp.tile(wrapped, (1, block_len))[:, : block_len * (2 * block_len - 1)]
    return tiled.reshape(chans, block_len, 2 * block_len - 1)[:, :, :block_len]


def local_conv(normed3, kernel):
    block_len = normed3.shape[1]
    blocks = normed3.shape[2] // 128
    kern_blocks = kernel.reshape(blocks, 128, block_len)
    data_blocks = normed3.reshape(normed3.shape[0], block_len, blocks, 128).transpose(2, 0, 1, 3)

    def one_block(block_pair):
        kern_part, data_part = block_pair
        toeplitz = toeplitz_rows(kern_part)
        return jnp.einsum("dts,bsd->btd", toeplitz, data_part, precision=precise)

    result = lax.map(one_block, (kern_blocks, data_blocks))
    return result.transpose(1, 2, 0, 3).reshape(normed3.shape)


def ema_terms(normed3, delta, alpha, beta, gamma, omega, incoming):
    block_len = normed3.shape[1]
    input_rate, log_decay = decay_tables(delta, alpha)
    step_index = jnp.arange(block_len, dtype=jnp.float32)
    ema_scale = NDIM ** (-0.5)
    powers = jnp.exp(log_decay[:, :, None] * step_index)
    kernel = ema_scale * jnp.einsum(
        "dj,djk->dk", gamma * input_rate * beta, powers, precision=precise
    )
    convolved = local_conv(normed3, kernel)
    carry_table = (
        ema_scale * gamma[:, :, None] * jnp.exp(log_decay[:, :, None] * (step_index + 1.0))
    )
    carried = jnp.einsum("djt,bdj->btd", carry_table, incoming, precision=precise)
    return convolved + carried + omega * normed3


def ema_ends(normed3, delta, alpha, beta):
    block_len = normed3.shape[1]
    input_rate, log_decay = decay_tables(delta, alpha)
    step_index = jnp.arange(block_len, dtype=jnp.float32)
    end_table = (input_rate * beta)[:, :, None] * jnp.exp(
        log_decay[:, :, None] * (block_len - 1.0 - step_index)
    )
    end_states = jnp.einsum("djs,bsd->bdj", end_table, normed3, precision=precise)
    return (jnp.exp(log_decay * block_len), end_states)


def rel_table(position_bias):
    step_index = jnp.arange(position_bias.shape[0])
    offsets = step_index[:, None] - step_index[None, :]
    return jnp.where(offsets >= 0, position_bias[jnp.maximum(offsets, 0)], 0.0)


def masked_softmax(scores):
    step_index = jnp.arange(scores.shape[-1])
    causal = step_index[:, None] >= step_index[None, :]
    masked = jnp.where(causal, scores, -jnp.inf)
    row_top = jnp.max(masked, axis=-1, keepdims=True)
    expo_vals = jnp.exp(masked - row_top)
    return expo_vals / jnp.sum(expo_vals, axis=-1, keepdims=True)


def silu_slope(values):
    logistic = jax.nn.sigmoid(values)
    return logistic * (1.0 + values * (1.0 - logistic))


def matmul(left_mat, right_mat):
    return jnp.dot(left_mat, right_mat, preferred_element_type=jnp.float32)


def left_product(left_mat, right_mat):
    return lax.dot_general(
        left_mat, right_mat, (((0,), (0,)), ((), ())), preferred_element_type=jnp.float32
    )


def right_product(left_mat, right_mat):
    return lax.dot_general(
        left_mat, right_mat, (((1,), (1,)), ((), ())), preferred_element_type=jnp.float32
    )


def column_sums(values):
    return jnp.sum(values.astype(jnp.float32), axis=0)


def shards(
    tokens,
    out_grad,
    norm1_gain,
    norm1_bias,
    value_weight,
    value_bias,
    ema_delta,
    ema_alpha,
    ema_beta,
    ema_gamma,
    ema_omega,
    base_weight,
    base_bias,
    shared_gamma,
    query_offset,
    position_bias,
    proj_weight,
    proj_bias,
    norm2_gain,
    norm2_bias,
    ffn1_weight,
    ffn1_bias,
    ffn2_weight,
    ffn2_bias,
):
    seq_local, block_len, _ = tokens.shape
    row_count = seq_local * block_len
    gathered = (
        lax.all_gather(value_weight.astype(jnp.bfloat16), ("seq", "batch"), axis=0, tiled=True),
        lax.all_gather(base_weight.astype(jnp.bfloat16), ("seq", "batch"), axis=0, tiled=True),
        lax.all_gather(proj_weight.astype(jnp.bfloat16), ("seq", "batch"), axis=0, tiled=True),
        lax.all_gather(ffn1_weight.astype(jnp.bfloat16), ("seq", "batch"), axis=0, tiled=True),
        lax.all_gather(ffn2_weight.astype(jnp.bfloat16), ("seq", "batch"), axis=0, tiled=True),
    )
    value_full, base_full, proj_full, ffn1_full, ffn2_full = gathered
    _, log_decay = decay_tables(ema_delta, ema_alpha)
    block_log = log_decay * block_len

    def chain_step(earlier_pair, later_pair):
        carried = earlier_pair[1] * jnp.exp(block_log * later_pair[0][0])
        return (earlier_pair[0] + later_pair[0], carried + later_pair[1])

    one_block = jnp.ones((1,), jnp.float32)
    no_block = jnp.zeros((1,), jnp.float32)
    tokens_flat = tokens.astype(jnp.float32).reshape(row_count, D)
    normed, norm1_back = jax.vjp(layer_norm, tokens_flat, norm1_gain, norm1_bias)
    normed_low = normed.astype(jnp.bfloat16)
    value_pre = matmul(normed_low, value_full) + value_bias
    value_low = jax.nn.silu(value_pre).astype(jnp.bfloat16)
    normed3 = normed.reshape(seq_local, block_len, D)
    (whole_decay, end_states), ends_back = jax.vjp(
        ema_ends, normed3, ema_delta, ema_alpha, ema_beta
    )
    prefix = entering(
        (one_block, end_states), "seq", chain_step, (no_block, jnp.zeros_like(end_states))
    )
    incoming = prefix[1]
    ema_out, ema_back = jax.vjp(
        ema_terms, normed3, ema_delta, ema_alpha, ema_beta, ema_gamma, ema_omega, incoming
    )
    ema_flat = ema_out.reshape(row_count, D)
    mixed_low = jax.nn.silu(ema_flat).astype(jnp.bfloat16)
    base_pre = matmul(mixed_low, base_full) + base_bias
    update = jax.nn.sigmoid(base_pre[:, :D])
    shared_pre = base_pre[:, D : D + ZD + VD]
    shared_reset = jax.nn.silu(shared_pre)
    shared = shared_reset[:, :ZD]
    reset_gate = shared_reset[:, ZD:]
    hidden_x = base_pre[:, D + ZD + VD :]
    queries = (
        (shared * shared_gamma[0] + query_offset)
        .astype(jnp.bfloat16)
        .reshape(seq_local, block_len, ZD)
    )
    key_rows = (shared * shared_gamma[1]).astype(jnp.bfloat16).reshape(seq_local, block_len, ZD)
    position, position_back = jax.vjp(rel_table, position_bias)
    scores = (
        jnp.einsum("bik,bjk->bij", queries, key_rows, preferred_element_type=jnp.float32)
        * ZD ** (-0.5)
        + position
    )
    attn = masked_softmax(scores)
    attn_low = attn.astype(jnp.bfloat16)
    values3 = value_low.reshape(seq_local, block_len, VD)
    attended = jnp.einsum(
        "bij,bjv->biv", attn_low, values3, preferred_element_type=jnp.float32
    ).reshape(row_count, VD)
    gated_low = (attended * reset_gate).astype(jnp.bfloat16)
    proj_pre = matmul(gated_low, proj_full) + proj_bias
    hidden_sum = hidden_x + proj_pre
    hidden = jax.nn.silu(hidden_sum)
    first_out = tokens_flat + update * (hidden - tokens_flat)
    normed_two, norm2_back = jax.vjp(layer_norm, first_out, norm2_gain, norm2_bias)
    normed_two_low = normed_two.astype(jnp.bfloat16)
    ffn_pre = matmul(normed_two_low, ffn1_full) + ffn1_bias
    ffn_low = jax.nn.silu(ffn_pre).astype(jnp.bfloat16)
    ffn_out = matmul(ffn_low, ffn2_full) + ffn2_bias
    block_out = (first_out + ffn_out).astype(jnp.bfloat16).reshape(seq_local, block_len, D)
    grad_ffn2 = out_grad.reshape(row_count, D)
    dffn2_weight = left_product(ffn_low, grad_ffn2)
    dffn2_bias = column_sums(grad_ffn2)
    grad_ffn1 = (right_product(grad_ffn2, ffn2_full) * silu_slope(ffn_pre)).astype(jnp.bfloat16)
    dffn1_weight = left_product(normed_two_low, grad_ffn1)
    dffn1_bias = column_sums(grad_ffn1)
    grad_first_norm, dnorm2_gain, dnorm2_bias = norm2_back(right_product(grad_ffn1, ffn1_full))
    grad_first = grad_ffn2.astype(jnp.float32) + grad_first_norm
    grad_skip = grad_first * (1.0 - update)
    grad_update = grad_first * (hidden - tokens_flat)
    grad_hidden = grad_first * update * silu_slope(hidden_sum)
    grad_proj = grad_hidden.astype(jnp.bfloat16)
    dproj_weight = left_product(gated_low, grad_proj)
    dproj_bias = column_sums(grad_proj)
    grad_gated = right_product(grad_proj, proj_full)
    grad_attended = (grad_gated * reset_gate).astype(jnp.bfloat16).reshape(seq_local, block_len, VD)
    grad_reset = grad_gated * attended
    grad_attn = jnp.einsum(
        "biv,bjv->bij", grad_attended, values3, preferred_element_type=jnp.float32
    )
    grad_values = jnp.einsum(
        "bij,biv->bjv", attn_low, grad_attended, preferred_element_type=jnp.float32
    ).reshape(row_count, VD)
    grad_scores = (attn * (grad_attn - jnp.sum(grad_attn * attn, axis=-1, keepdims=True))).astype(
        jnp.bfloat16
    )
    (dposition_bias,) = position_back(jnp.sum(grad_scores.astype(jnp.float32), axis=0))
    grad_queries = jnp.einsum(
        "bij,bjk->bik", grad_scores, key_rows, preferred_element_type=jnp.float32
    ).reshape(row_count, ZD) * ZD ** (-0.5)
    grad_keys = jnp.einsum(
        "bij,bik->bjk", grad_scores, queries, preferred_element_type=jnp.float32
    ).reshape(row_count, ZD) * ZD ** (-0.5)
    dshared_gamma = jnp.stack(
        [jnp.sum(grad_queries * shared, axis=0), jnp.sum(grad_keys * shared, axis=0)]
    )
    dquery_offset = jnp.sum(grad_queries, axis=0)
    grad_shared = grad_queries * shared_gamma[0] + grad_keys * shared_gamma[1]
    grad_shared_pre = jnp.concatenate([grad_shared, grad_reset], axis=1) * silu_slope(shared_pre)
    grad_update_pre = grad_update * update * (1.0 - update)
    grad_base = jnp.concatenate([grad_update_pre, grad_shared_pre, grad_hidden], axis=1).astype(
        jnp.bfloat16
    )
    dbase_weight = left_product(mixed_low, grad_base)
    dbase_bias = column_sums(grad_base)
    grad_ema = right_product(grad_base, base_full) * silu_slope(ema_flat)
    grad_value_pre = (grad_values * silu_slope(value_pre)).astype(jnp.bfloat16)
    dvalue_weight = left_product(normed_low, grad_value_pre)
    dvalue_bias = column_sums(grad_value_pre)
    grad_normed = right_product(grad_value_pre, value_full)
    grad_normed_ema, delta_part, alpha_part, beta_part, dema_gamma, dema_omega, grad_incoming = (
        ema_back(grad_ema.reshape(seq_local, block_len, D))
    )
    suffix = prefix_2(
        (one_block, grad_incoming), "seq", chain_step, (no_block, jnp.zeros_like(grad_incoming))
    )
    grad_ends = suffix[1]
    grad_whole = jnp.sum(grad_ends * incoming, axis=0)
    grad_normed_ends, delta_rest, alpha_rest, beta_rest = ends_back((grad_whole, grad_ends))
    dema_delta = delta_part + delta_rest
    dema_alpha = alpha_part + alpha_rest
    dema_beta = beta_part + beta_rest
    grad_normed = grad_normed + (grad_normed_ema + grad_normed_ends).reshape(row_count, D)
    grad_tokens_norm, dnorm1_gain, dnorm1_bias = norm1_back(grad_normed)
    tokens_grad = (
        (grad_skip + grad_tokens_norm).astype(jnp.bfloat16).reshape(seq_local, block_len, D)
    )
    small_sums = lax.psum(
        (
            dnorm1_gain,
            dnorm1_bias,
            dvalue_bias,
            dema_delta,
            dema_alpha,
            dema_beta,
            dema_gamma,
            dema_omega,
            dbase_bias,
            dshared_gamma,
            dquery_offset,
            dposition_bias,
            dproj_bias,
            dnorm2_gain,
            dnorm2_bias,
            dffn1_bias,
            dffn2_bias,
        ),
        ("seq", "batch"),
    )
    reduced = (
        lax.psum_scatter(dvalue_weight, ("seq", "batch"), scatter_dimension=0, tiled=True),
        lax.psum_scatter(dbase_weight, ("seq", "batch"), scatter_dimension=0, tiled=True),
        lax.psum_scatter(dproj_weight, ("seq", "batch"), scatter_dimension=0, tiled=True),
        lax.psum_scatter(dffn1_weight, ("seq", "batch"), scatter_dimension=0, tiled=True),
        lax.psum_scatter(dffn2_weight, ("seq", "batch"), scatter_dimension=0, tiled=True),
    )
    return (
        block_out,
        tokens_grad,
        small_sums[0],
        small_sums[1],
        reduced[0],
        small_sums[2],
        small_sums[3],
        small_sums[4],
        small_sums[5],
        small_sums[6],
        small_sums[7],
        reduced[1],
        small_sums[8],
        small_sums[9],
        small_sums[10],
        small_sums[11],
        reduced[2],
        small_sums[12],
        small_sums[13],
        small_sums[14],
        reduced[3],
        small_sums[15],
        reduced[4],
        small_sums[16],
    )


VMEM_LIMIT = 63 * 1024 * 1024
BF = jnp.bfloat16
F32 = jnp.float32
MESH = pl.DeviceIdType.MESH
SCALE = ZD ** (-0.5)
EMA_SCALE = NDIM ** (-0.5)
BLK = 128
VH = 1024
BASE_COLS = 2176
SM_ROWS = 400
ROW_OMEGA, ROW_N1G, ROW_N1B, ROW_N2G, ROW_N2B = 256, 264, 272, 280, 288
ROW_VB, ROW_BB, ROW_PB, ROW_F1B, ROW_F2B = 296, 312, 345, 353, 385
ROW_SG, ROW_QO, ROW_POS = 393, 395, 396
SMALL_ROWS = (
    (ROW_N1G, 8), (ROW_N1B, 8), (ROW_VB, 16), (ROW_OMEGA, 8), (ROW_BB, 33), (ROW_SG, 2), (ROW_QO, 1),
    (ROW_POS, 1), (ROW_PB, 8), (ROW_N2G, 8), (ROW_N2B, 8), (ROW_F1B, 32), (ROW_F2B, 8),
)
VALUE, BASE, PROJ, FFN1, FFN2 = range(5)
U_V, U_P, U_BA, U_BB, U_1, U_2 = range(6)
Y_FIRST = (U_V,)
X_THEN_Y = (VALUE,)


def pick(flag, yes, no):
    return lax.select(flag, yes, no)


def sig(v):
    return jax.nn.sigmoid(v)


def silu(v):
    return v * sig(v)


def slope(v):
    s = sig(v)
    return s * (1.0 + v * (1.0 - s))


def dot_nn(a, b):
    return jnp.dot(a, b, preferred_element_type=F32)


def dot_nt(a, b):
    return lax.dot_general(a, b, (((1,), (1,)), ((), ())), preferred_element_type=F32)


def dot_tn(a, b):
    return lax.dot_general(a, b, (((0,), (0,)), ((), ())), preferred_element_type=F32)


def split_pair(first, second, low_lanes):
    lo = jnp.where(low_lanes, first, pltpu.roll(second, 64, 1))
    hi = jnp.where(low_lanes, pltpu.roll(first, 64, 1), second)
    return lo, hi


def fold8(v):
    rows, cols = v.shape
    return jnp.sum(v.reshape(rows // 8, 8, cols), axis=0)


def shear(v, left):
    rows = lax.broadcasted_iota(jnp.int32, (BLK, BLK), 0)
    for bit in range(7):
        step = 1 << bit
        turned = pltpu.roll(v, BLK - step if left else step, 1)
        v = jnp.where((rows & step) != 0, turned, v)
    return v


def layer_kernel(NS, *refs):
    NZ = NS // 4
    names = iter(refs)
    take = lambda n: [next(names) for _ in range(n)]
    (tok, og, n1g, n1b, vb) = take(5)
    ema_in = take(4)
    (om_in, bb, sg, qo, pbr, pbias, n2g, n2b, f1b, f2b) = take(10)
    (vw, bw, pw, f1w, f2w) = take(5)
    (o_block, o_tok, o_dv, o_db, o_dp, o_d1, o_d2, o_ema, o_sm) = take(9)
    (SM_OUT, ema, om) = take(3)
    (WV, WB, WP, W1, W2) = take(5)
    (G1, G2, GBA, GBB, RXBB) = take(5)
    RY = take(6)
    RZ = take(6)
    (FV, FB, FXV, FXB, FX1) = take(5)
    (SV, SB, NL, ML, NO, VP, VL, UH, UU, HH, SHP, RP, AD, GT, AT, PR, FO, FP, FG) = take(19)
    (AS, AR, AX, AXR, OX, OXR, OB, GH, GUS, GBS, GA, GAT, GATR, GVP, GNVR) = take(15)
    (XP, YP, GEP, GNP, HC, H8, EC, EXX, EXY, EXZ, BXX, BXY, BXZ, DEC, CIN, LAM, PIN) = take(17)
    (SMR, SMX, SMY, SMZ, SMC) = take(5)
    (in_sem, zs, zr, ys, yr, xs, xr, rxs, rxr, rys, ryr, rzs, rzr, es, er) = take(15)

    s = lax.axis_index("seq")
    b = lax.axis_index("batch")
    x = lax.rem(s, 2)
    y = lax.rem(lax.div(s, 2), 2)
    z = lax.div(s, 4)
    p = lax.div(s, 2)
    q = 2 * x + b
    xs_ = s + 1 - 2 * x
    ys_ = s + 2 - 4 * y
    C = (s, 1 - b)
    X = (xs_, b)
    XC = (xs_, 1 - b)
    Y = (ys_, b)
    ahead = lambda k: lax.rem(s + 4 * k, NS)
    behind = lambda k: lax.rem(s - 4 * k + NS * 4, NS)
    first = b == 0
    al = pl.multiple_of
    rows_of = lambda i, n: pl.ds(al(i * n, n), n)

    loads = [
        pltpu.make_async_copy(src, dst, in_sem.at[i])
        for i, (src, dst) in enumerate(
            ((vw, o_dv), (bw, o_db), (pw, o_dp), (f1w, o_d1), (f2w, o_d2))
        )
    ]
    for load in loads:
        load.start()

    barrier = pltpu.get_barrier_semaphore()
    partners = [C, X, XC, Y] + [(ahead(k), b) for k in range(1, NZ)]
    for device in partners:
        pl.semaphore_signal(barrier, inc=1, device_id=device, device_id_type=MESH)

    def remote(src, dst, send, recv, device):
        return pltpu.make_async_remote_copy(
            src_ref=src, dst_ref=dst, send_sem=send, recv_sem=recv, device_id=device, device_id_type=MESH
        )

    open_sends = []

    def settle(copy):
        open_sends[:] = [other for other in open_sends if other is not copy]

    n_ex = [0]

    def exchange(src, dst, device, landed=None):
        i = n_ex[0]
        n_ex[0] += 1
        copy = remote(src, dst, es.at[i], er.at[i], device)
        copy.start()
        open_sends.append(copy)
        arrival = copy if landed is None else remote(src, landed, es.at[i], er.at[i], device)
        return copy, arrival

    low1 = lambda n: lax.broadcasted_iota(jnp.int32, (n, BLK), 1) < 64

    my_rows = pl.ds(al(64 * s + 32 * b, 32), 32)
    other_rows = pl.ds(al(64 * s + 32 * (1 - b), 32), 32)

    def split_columns(src, src0, blocks, mine_ref, mine_rows, dst0, other_ref):
        low = low1(32)
        for t in range(blocks):
            lo, hi = split_pair(
                src[:, src0 + 256 * t : src0 + 256 * t + 128],
                src[:, src0 + 256 * t + 128 : src0 + 256 * t + 256],
                low,
            )
            cols = slice(dst0 + 128 * t, dst0 + 128 * t + 128)
            mine_ref[mine_rows, cols] = pick(first, lo, hi).astype(BF)
            other_ref[:, cols] = pick(first, hi, lo).astype(BF)

    NT = NO.at[0:512]
    OG = NO.at[512:1024]
    quad = lambda j: rows_of(j, BLK)
    q_c = q + 1 - 2 * b
    q_x = lax.rem(q + 2, 4)
    q_xc = lax.rem(q_c + 2, 4)
    OG[quad(q), :] = og[...]
    loads[0].wait()
    split_columns(o_dv, 0, 8, WV, my_rows, 0, SV)
    pl.semaphore_wait(barrier, len(partners))
    _, got_wv = exchange(SV, WV.at[my_rows], C, WV.at[other_rows])
    gather = [WV, WB, WP, W1, W2]

    def piece(w, chip):
        if w < FFN1:
            return gather[w].at[rows_of(chip, 64)]
        return gather[w].at[rows_of(lax.div(chip, 2), 128)]

    chip_of = lambda plane: 4 * plane + lax.rem(s, 4)

    def route(w):
        return (xs_ - s, ys_ - s, X, Y) if w in X_THEN_Y else (ys_ - s, xs_ - s, Y, X)

    def send_z(w, plane, down, side=0):
        part = piece(w, chip_of(plane) + (ys_ - s if side else 0))
        device = (s - 4, b) if down else (s + 4, b)
        return remote(part, part, zs.at[w, plane, down, side], zr.at[w, plane, side], device)

    def got_z(w, plane, side=0):
        part = piece(w, chip_of(plane) + (ys_ - s if side else 0))
        return remote(part, part, zs.at[w, plane, 0, side], zr.at[w, plane, side], Y)

    def send_y(w, plane):
        part = piece(w, chip_of(plane))
        return remote(part, part, ys.at[w, plane], yr.at[w, plane], route(w)[2])

    def got_y(w, plane):
        part = piece(w, chip_of(plane) + route(w)[0])
        return remote(part, part, ys.at[w, plane], yr.at[w, plane], route(w)[2])

    def send_x(w, plane, far):
        part = piece(w, chip_of(plane) + (route(w)[0] if far else 0))
        return remote(part, part, xs.at[w, far, plane], xr.at[w, far, plane], route(w)[3])

    def got_x(w, plane, far):
        part = piece(w, chip_of(plane) + (route(w)[0] if far else 0) + route(w)[1])
        return remote(part, part, xs.at[w, far, plane], xr.at[w, far, plane], route(w)[3])

    def near_planes(visit, start=1, stop=NZ):
        for j in range(start, stop):
            pl.when(z >= j)(functools.partial(visit, z - j, 0, z < NZ - 1))
            pl.when(z + j <= NZ - 1)(functools.partial(visit, z + j, 1, z > 0))

    def spread_z(w, side=0):
        pl.when(z < NZ - 1)(lambda: send_z(w, z, 0, side).start())
        pl.when(z > 0)(lambda: send_z(w, z, 1, side).start())

    def open_gather(w):
        send_y(w, z).start()
        spread_z(w)
        if w < FFN1:
            send_x(w, z, 0).start()

    def relay_z(w, start=1, stop=NZ):
        def visit(plane, down, more):
            for side in range(2 if w == FFN2 else 1):
                got_z(w, plane, side).wait_recv()
                pl.when(more)(lambda side=side: send_z(w, plane, down, side).start())
            if w < FFN2:
                send_y(w, plane).start()
            if w < FFN1:
                send_x(w, plane, 0).start()

        near_planes(visit, start, stop)

    def relay_y(w):
        def visit(plane, down, more):
            got_y(w, plane).wait_recv()
            if w < FFN1:
                send_x(w, plane, 1).start()

        visit(z, 0, False)
        if w < FFN2:
            near_planes(visit)
        else:
            spread_z(w, 1)

    def finish_x(w):
        def one(k, carry):
            got_x(w, k, 0).wait_recv()
            got_x(w, k, 1).wait_recv()
            return carry

        lax.fori_loop(0, NZ, one, 0)

    def close_gather(w):
        def one(k, carry):
            send_y(w, k).wait_send()
            if w < FFN1:
                send_x(w, k, 0).wait_send()
                send_x(w, k, 1).wait_send()
            return carry

        if w < FFN2:
            lax.fori_loop(0, NZ, one, 0)
        else:
            send_y(w, z).wait_send()
        for side in range(2 if w == FFN2 else 1):
            pl.when(z < NZ - 1)(lambda side=side: send_z(w, z, 0, side).wait_send())
            pl.when(z > 0)(lambda side=side: send_z(w, z, 1, side).wait_send())

            def visit(plane, down, more, side=side):
                pl.when(more)(lambda: send_z(w, plane, down, side).wait_send())

            near_planes(visit)

    def norm_rows(v):
        center = v - jnp.mean(v, axis=-1, keepdims=True)
        rstd = lax.rsqrt(jnp.mean(center * center, axis=-1, keepdims=True) + 1e-05)
        return center * rstd, rstd

    own = rows_of(b, BLK)

    def norm_one(i, carry):
        rows = rows_of(i, 32)
        n, _ = norm_rows(tok[rows, :].astype(F32))
        normed = n * n1g[...] + n1b[...]
        for g in range(8):
            XP[pl.ds(al(128 * g + 32 * i, 32), 32), :] = normed[:, 128 * g : 128 * g + 128]
        NL[pl.ds(al(128 * b + 32 * i, 32), 32), :] = normed.astype(BF)
        return carry

    for g in range(8):
        cols = slice(128 * g, 128 * g + 128)
        om[g : g + 1, :] = om_in[:, cols]
        for a in range(4):
            ema[a, :, g, :] = ema_in[a][:, cols]
    for j in range(NDIM):
        rate = sig(ema[0, j])
        DEC[j] = 1.0 - rate * sig(ema[1, j])
        CIN[j] = rate * ema[2, j]
        lam = DEC[j]
        for _ in range(7):
            lam = lam * lam
        LAM[j] = lam

    def panel(t):
        return pl.ds(t, 8, stride=BLK)

    def end_scan():
        d = [DEC[j] for j in range(NDIM)]
        c = [CIN[j] for j in range(NDIM)]

        def step(t, h):
            row = XP[panel(t), :]
            return tuple(h[j] * d[j] + c[j] * row for j in range(NDIM))

        h = lax.fori_loop(
            0, BLK, step, tuple(jnp.zeros((8, 128), F32) for _ in range(NDIM)), unroll=4
        )
        for j in range(NDIM):
            EC[0, j] = h[j]


    def scan_round_x(own_state, arrived, out, incoming, later):
        for j in range(NDIM):
            l, mine, theirs = LAM[j], own_state[j], arrived[j]
            out[j] = pick(later, l * theirs + mine, l * mine + theirs)
            incoming[j] = pick(later, theirs, jnp.zeros_like(theirs))

    def scan_round_y(own_state, arrived, out, incoming, later, inner):
        for j in range(NDIM):
            l = LAM[j]
            l2 = l * l
            mine, theirs = own_state[j], arrived[j]
            out[j] = pick(later, l2 * theirs + mine, l2 * mine + theirs)
            hop = pick(inner == 1, l, jnp.ones_like(l))
            incoming[j] += pick(later, hop * theirs, jnp.zeros_like(l))

    def scan_round_z(arrived, incoming, reach, inner):
        for j in range(NDIM):
            l = LAM[j]
            l2 = l * l
            l4 = l2 * l2
            one = jnp.ones_like(l)
            hop = pick(lax.rem(inner, 2) == 1, l, one) * pick(inner >= 2, l2, one)
            total = incoming[j]
            for k in range(1, NZ):
                total += pick(k <= reach, hop * arrived[k - 1, j], jnp.zeros_like(l))
                hop = hop * l4
            incoming[j] = total

    loads[1].wait()
    WB[my_rows, 0:512] = o_db[:, pl.ds(al(512 * b, 512), 512)].astype(BF)
    SB[:, 0:512] = o_db[:, pl.ds(al(512 * (1 - b), 512), 512)].astype(BF)
    WB[my_rows, 512:1024] = o_db[:, pl.ds(al(3200 + 512 * b, 128), 512)].astype(BF)
    SB[:, 512:1024] = o_db[:, pl.ds(al(3200 + 512 * (1 - b), 128), 512)].astype(BF)
    shared_cols = o_db[:, 1024:1152].astype(BF)
    WB[my_rows, 1024:1152] = shared_cols
    SB[:, 1024:1152] = shared_cols
    split_columns(o_db, 1152, 8, WB, my_rows, 1152, SB)
    _, got_wb = exchange(SB, WB.at[my_rows], C, WB.at[other_rows])

    copy_og_x, got_og_x = exchange(OG.at[quad(q)], OG.at[quad(q)], X, OG.at[quad(q_x)])
    loads[2].wait()
    WP[rows_of(s, 64), :] = o_dp[...].astype(BF)
    open_gather(PROJ)
    got_wv.wait_recv()
    open_gather(VALUE)
    lax.fori_loop(0, 4, norm_one, 0)
    _, got_nl = exchange(NL.at[own], NL.at[own], C, NL.at[rows_of(1 - b, BLK)])
    end_scan()
    _, got_ex = exchange(EC.at[0], EXX, X)
    got_wb.wait_recv()
    open_gather(BASE)
    loads[4].wait()
    W2[rows_of(p, 128), :] = o_d2[...].astype(BF)
    open_gather(FFN2)

    got_ex.wait_recv()
    scan_round_x(EC.at[0], EXX, EC.at[1], PIN, x == 1)
    _, got_ey = exchange(EC.at[1], EXY, Y)
    loads[3].wait()
    for j in range(4):
        for t in range(8):
            AS[32 * j : 32 * j + 32, 128 * t : 128 * t + 128] = o_d1[
                :, 128 * (4 * t + j) : 128 * (4 * t + j) + 128
            ].astype(BF)
    f1_rows = lambda j: pl.ds(al(128 * p + 32 * j, 32), 32)
    W1[f1_rows(q), :] = AS[rows_of(q, 32), :]
    f1_pairs = [
        exchange(AS.at[rows_of(j, 32)], W1.at[f1_rows(q)], device, W1.at[f1_rows(j)])
        for j, device in ((q_c, C), (q_x, X), (q_xc, XC))
    ]
    copy_og_c, got_og_c = exchange(OG.at[quad(q)], OG.at[quad(q)], C, OG.at[quad(q_c)])
    got_ey.wait_recv()
    scan_round_y(EC.at[1], EXY, EC.at[2], PIN, y == 1, x)
    got_ez = [exchange(EC.at[2], EXZ.at[k - 1], (ahead(k), b))[1] for k in range(1, NZ)]
    for copy, got in f1_pairs:
        copy.wait_send()
        settle(copy)
        got.wait_recv()
    open_gather(FFN1)
    relay_z(VALUE)
    relay_y(FFN2)
    relay_y(VALUE)
    relay_z(BASE)
    relay_y(BASE)
    relay_z(PROJ)
    for got in got_ez:
        got.wait_recv()
    scan_round_z(EXZ, PIN, z, 2 * y + x)

    def forward_scan():
        for half in range(2):
            js = range(8 * half, 8 * half + 8)
            d = [DEC[j] for j in js]
            c = [CIN[j] for j in js]
            g = [EMA_SCALE * ema[3, j] for j in js]

            def group(i, h):
                for n, j in enumerate(js):
                    HC[i, j] = h[n]
                for u in range(8):
                    t = 8 * i + u
                    row = XP[panel(t), :]
                    h = tuple(h[n] * d[n] + c[n] * row for n in range(8))
                    out = g[0] * h[0]
                    for n in range(1, 8):
                        out = out + g[n] * h[n]
                    if half == 0:
                        out = out + om[...] * row
                    else:
                        out = out + YP[panel(t), :]
                    YP[panel(t), :] = out
                return h

            lax.fori_loop(0, 16, group, tuple(PIN[j] for j in js))

    forward_scan()

    def mixed_one(i, carry):
        for g in range(8):
            v = YP[pl.ds(al(128 * g + 32 * i, 32), 32), :]
            ML[pl.ds(al(128 * b + 32 * i, 32), 32), 128 * g : 128 * g + 128] = silu(v).astype(BF)
        return carry

    lax.fori_loop(0, 4, mixed_one, 0)
    _, got_ml = exchange(ML.at[own], ML.at[own], C, ML.at[rows_of(1 - b, BLK)])
    relay_y(PROJ)

    low_row = low1(1)

    def my_half(ref, start):
        parts = []
        for t in range(8):
            lo, hi = split_pair(
                ref[:, start + 256 * t : start + 256 * t + 128],
                ref[:, start + 256 * t + 128 : start + 256 * t + 256],
                low_row,
            )
            parts.append(pick(first, lo, hi))
        return jnp.concatenate(parts, axis=1)

    got_nl.wait_recv()
    finish_x(VALUE)
    vbias = my_half(vb, 0)
    for n in range(2):
        cols = slice(512 * n, 512 * n + 512)
        v = dot_nn(NL[...], WV[:, cols]) + vbias[:, cols]
        VP[:, cols] = v.astype(BF)
        VL[:, cols] = silu(v).astype(BF)

    relay_z(FFN1, 1, 3)
    relay_z(FFN2, 1, 2)

    got_ml.wait_recv()
    finish_x(BASE)
    UH[:, 0:512] = dot_nn(ML[...], WB[:, 0:512]) + bb[:, pl.ds(al(512 * b, 512), 512)]
    UH[:, 512:1024] = dot_nn(ML[...], WB[:, 512:1024]) + bb[:, pl.ds(al(3200 + 512 * b, 128), 512)]
    theirs = rows_of(1 - b, BLK)
    my_cols = pl.ds(al(512 * b, 512), 512)
    their_cols = pl.ds(al(512 * (1 - b), 512), 512)
    copy_u, got_u = exchange(UH.at[theirs, 0:512], UU.at[:, my_cols], C, UU.at[:, their_cols])
    copy_h, got_h = exchange(UH.at[theirs, 512:1024], HH.at[:, my_cols], C, HH.at[:, their_cols])
    UU[:, my_cols] = UH[own, 0:512]
    HH[:, my_cols] = UH[own, 512:1024]
    SHP[...] = dot_nn(ML[...], WB[:, 1024:1152]) + bb[:, 1024:1152]
    rbias = my_half(bb, 1152)
    for n in range(2):
        RP[:, 512 * n : 512 * n + 512] = (
            dot_nn(ML[...], WB[:, 1152 + 512 * n : 1664 + 512 * n]) + rbias[:, 512 * n : 512 * n + 512]
        ).astype(BF)

    relay_z(FFN1, 3)
    relay_z(FFN2, 2, 3)

    shared_of = lambda i: silu(SHP[128 * i : 128 * i + 128, :])

    def queries_keys(i):
        sh = shared_of(i)
        return (sh * sg[0:1, :] + qo[...]).astype(BF), (sh * sg[1:2, :]).astype(BF)

    position = jnp.transpose(shear(jnp.broadcast_to(pbr[...], (BLK, BLK)), False))
    at_row = lax.broadcasted_iota(jnp.int32, (BLK, BLK), 0)
    at_col = lax.broadcasted_iota(jnp.int32, (BLK, BLK), 1)
    causal = at_row >= at_col
    for i in range(2):
        rows = slice(128 * i, 128 * i + 128)
        qs, ks = queries_keys(i)
        scores = jnp.where(causal, dot_nt(qs, ks) * SCALE + position, -jnp.inf)
        e = jnp.exp(scores - jnp.max(scores, axis=-1, keepdims=True))
        attn = e / jnp.sum(e, axis=-1, keepdims=True)
        AT[rows, :] = attn
        low = attn.astype(BF)
        for n in range(2):
            cols = slice(512 * n, 512 * n + 512)
            att = dot_nn(low, VL[rows, cols])
            AD[rows, cols] = att.astype(BF)
            GT[rows, cols] = (att * silu(RP[rows, cols].astype(F32))).astype(BF)

    relay_z(FFN2, 3)

    finish_x(PROJ)
    copy_u.wait_send()
    copy_h.wait_send()
    settle(copy_u)
    settle(copy_h)
    for n in range(2):
        cols = slice(512 * n, 512 * n + 512)
        UH[:, cols] = dot_nn(GT[...], WP[:, cols])
    copy_p, got_p = exchange(UH.at[theirs], PR, C)
    got_u.wait_recv()
    got_h.wait_recv()
    got_p.wait_recv()

    def residual_one(i, carry):
        rows = rows_of(i, 32)
        mine = pl.ds(al(128 * b + 32 * i, 32), 32)
        total = HH[rows, :] + ((UH[mine, :] + PR[rows, :]) + pbias[...])
        HH[rows, :] = total
        base = tok[rows, :].astype(F32)
        out = base + sig(UU[rows, :]) * (silu(total) - base)
        FO[rows, :] = out
        n, _ = norm_rows(out)
        NT[pl.ds(al(128 * q + 32 * i, 32), 32), :] = (n * n2g[...] + n2b[...]).astype(BF)
        return carry

    lax.fori_loop(0, 4, residual_one, 0)
    got_og_x.wait_recv()
    copy_og_xc, got_og_xc = exchange(OG.at[quad(q_x)], OG.at[quad(q_x)], C, OG.at[quad(q_xc)])
    copy_nt_x, got_nt_x = exchange(NT.at[quad(q)], NT.at[quad(q)], X, NT.at[quad(q_x)])
    copy_nt_c, got_nt_c = exchange(NT.at[quad(q)], NT.at[quad(q)], C, NT.at[quad(q_c)])

    relay_y(FFN1)
    got_og_c.wait_recv()
    got_og_xc.wait_recv()
    for m in range(2):
        for n in range(2):
            rows = slice(256 * m, 256 * m + 256)
            cols = slice(512 * n, 512 * n + 512)
            FP[rows, cols] = dot_nt(OG[rows, :], W2[cols, :])
    got_nt_x.wait_recv()
    copy_nt_xc, got_nt_xc = exchange(NT.at[quad(q_x)], NT.at[quad(q_x)], C, NT.at[quad(q_xc)])
    got_nt_c.wait_recv()
    got_nt_xc.wait_recv()

    FL = FG.at[0:512]
    GF = FG.at[512:1024]
    fbias = jnp.concatenate(
        [f1b[:, pl.ds(al(512 * t + 128 * q, 128), 128)] for t in range(8)], axis=1
    )
    for m in range(2):
        for n in range(2):
            rows = slice(256 * m, 256 * m + 256)
            cols = slice(512 * n, 512 * n + 512)
            pre = dot_nn(NT[rows, :], W1[:, cols]) + fbias[:, cols]
            FL[rows, cols] = silu(pre).astype(BF)
            GF[rows, cols] = (FP[rows, cols] * slope(pre)).astype(BF)
    for m in range(2):
        for n in range(2):
            rows = slice(256 * m, 256 * m + 256)
            cols = slice(512 * n, 512 * n + 512)
            AS[rows, cols] = dot_nt(GF[rows, :], W1[cols, :]).astype(BF)

    def reduce_pair(staged, landing):
        copies = []
        for c in range(2):
            there = rows_of(2 * c + 1 - b, BLK)
            copies.append(exchange(staged.at[there], landing.at[rows_of(c, BLK)], C))
        return copies

    def reduce_x(staged, landing, arrivals, out, out_landing):
        for _, arrival in arrivals:
            arrival.wait_recv()

        def one(i, carry):
            mine = pl.ds(al(128 * (2 * (1 - x) + b) + 32 * i, 32), 32)
            got = pl.ds(al(128 * (1 - x) + 32 * i, 32), 32)
            out[rows_of(i, 32), :] = (staged[mine, :].astype(F32) + landing[got, :].astype(F32)).astype(BF)
            return carry

        lax.fori_loop(0, 4, one, 0)
        return exchange(out, out_landing, X)

    def pair_sum(staged, landing, i):
        mine = pl.ds(al(128 * q + 32 * i, 32), 32)
        got = pl.ds(al(128 * x + 32 * i, 32), 32)
        return staged[mine, :].astype(F32) + landing[got, :].astype(F32)

    got_a = reduce_pair(AS, AR)

    def store_row(row, v):
        for g in range(v.shape[1] // 128):
            SM_OUT[row + g : row + g + 1, :] = v[:, 128 * g : 128 * g + 128]

    SM_OUT[...] = jnp.zeros((SM_ROWS, 128), F32)

    def weight_grad(left, right, out, right0, out0, width):
        tile = 512 if width % 512 == 0 else 384
        for m in range(2):
            for n in range(width // tile):
                out[512 * m : 512 * m + 512, out0 + tile * n : out0 + tile * n + tile] = dot_tn(
                    left[:, 512 * m : 512 * m + 512],
                    right[:, right0 + tile * n : right0 + tile * n + tile],
                ).astype(BF)

    grads = [NO, FG, GBA, GBB, G1, G2]
    RXV = W1.at[0:512]
    RXP = W1.at[512:1024]
    RXBA = W2.at[0:512]
    half = [RXV, RXP, RXBA, RXBB]

    def shard(u, chip):
        if u < U_1:
            return rows_of(chip, 64)
        return rows_of(lax.div(chip, 2), 128)

    y_first = Y_FIRST
    hop_x, hop_y = xs_ - s, ys_ - s

    def hops(u):
        return (hop_y, hop_x, Y, X) if u in y_first else (hop_x, hop_y, X, Y)

    def rs_x(u, k, far):
        hop1, hop2, device, _ = hops(u)
        chip = ahead(k) + (hop2 if far else 0)
        src = grads[u].at[shard(u, chip + hop1)]
        slot = half[u].at[pl.ds(al(64 * (2 * k + far), 64), 64)]
        return remote(src, slot, rxs.at[u, k, far], rxr.at[u, k, far], device)

    def rs_y(u, k):
        _, hop2, _, device = hops(u) if u < U_1 else (0, hop_y, X, Y)
        src = grads[u].at[shard(u, ahead(k) + hop2)]
        return remote(src, RY[u].at[k], rys.at[u, k], ryr.at[u, k], device)

    def rs_z(u, k):
        src = grads[u].at[shard(u, ahead(k))]
        return remote(src, RZ[u].at[k - 1], rzs.at[u, k], rzr.at[u, k], (ahead(k), b))

    turn = lambda i: lax.rem(i + 1, NZ)

    def rs_open(u, start=0, stop=None):
        def one(i, carry):
            k = turn(i)
            if u < U_1:
                rs_x(u, k, 1).start()
                rs_x(u, k, 0).start()
            else:
                rs_y(u, k).start()
            return carry

        lax.fori_loop(start, NZ if stop is None else stop, one, 0)

    def rs_pass_x(u, start=0, stop=None):
        def one(i, carry):
            k = turn(i)
            for far in (1, 0):
                rs_x(u, k, far).wait_recv()
                rows = shard(u, ahead(k) + (hops(u)[1] if far else 0))
                got = half[u][pl.ds(al(64 * (2 * k + far), 64), 64), :]
                grads[u][rows, :] = (grads[u][rows, :].astype(F32) + got.astype(F32)).astype(BF)
                if far == 1:
                    rs_y(u, k).start()
            return carry

        lax.fori_loop(start, NZ if stop is None else stop, one, 0)

    def rs_pass_y(u, start=0, stop=None):
        def one(i, carry):
            k = i + 1
            rs_y(u, k).wait_recv()
            rows = shard(u, ahead(k))
            grads[u][rows, :] = (grads[u][rows, :].astype(F32) + RY[u][k].astype(F32)).astype(BF)
            rs_z(u, k).start()
            return carry

        lax.fori_loop(start, NZ - 1 if stop is None else stop, one, 0)
        if stop is None:
            rs_y(u, 0).wait_recv()

    def rs_total(u, rows_in):
        rows = shard(u, s)
        size = 64 if u < U_1 else 128
        start = size * (s if u < U_1 else p)
        at = pl.ds(al(start + rows_in[0], 16), rows_in[1])
        in_ = pl.ds(al(rows_in[0], 16), rows_in[1])
        total = grads[u][at, :].astype(F32) + RY[u][0, in_, :].astype(F32)
        for k in range(1, NZ):
            total += RZ[u][k - 1, in_, :].astype(F32)
        return total

    def rs_wait_z(u):
        def one(k, carry):
            rs_z(u, k).wait_recv()
            return carry

        lax.fori_loop(1, NZ, one, 0)

    def column_sum(ref, start, width):
        def one(i, acc):
            return acc + fold8(ref[rows_of(i, 32), start : start + width].astype(F32))

        acc = lax.fori_loop(0, ref.shape[0] // 32, one, jnp.zeros((8, width), F32))
        return jnp.sum(acc, axis=0, keepdims=True)

    def back_two(i, carry):
        rows = rows_of(i, 32)
        a = pair_sum(AS, AR, i) + AXR[rows, :].astype(F32)
        n, rstd = norm_rows(FO[rows, :])
        g = a * n2g[...]
        grad = og[rows, :].astype(F32) + (
            g - jnp.mean(g, axis=-1, keepdims=True) - n * jnp.mean(g * n, axis=-1, keepdims=True)
        ) * rstd
        update = sig(UU[rows, :])
        total = HH[rows, :]
        logistic = sig(total)
        base = tok[rows, :].astype(F32)
        gh = (grad * update * (logistic * (1.0 + total * (1.0 - logistic)))).astype(BF)
        GH[pl.ds(al(128 * b + 32 * i, 32), 32), :] = gh
        GUS[rows, :] = (grad * (total * logistic - base) * update * (1.0 - update)).astype(BF)
        PR[rows, :] = grad * (1.0 - update)
        return (
            carry[0] + fold8(a * n),
            carry[1] + fold8(a),
            carry[2] + fold8(gh.astype(F32)),
            carry[3] + fold8(og[rows, :].astype(F32)),
        )

    weight_grad(FL, OG, G2, 0, 0, 1024)
    rs_open(U_2)
    close_gather(FFN1)
    a_x = reduce_x(AS, AR, got_a, AX, AXR)
    for m in range(2):
        for n in range(2):
            rows = slice(256 * m, 256 * m + 256)
            cols = slice(512 * n, 512 * n + 512)
            FP[rows, cols] = dot_nn(FL[rows, :], W2[:, cols])
    got_o = reduce_pair(FP, GNVR)
    close_gather(FFN2)
    weight_grad(NT, GF, G1, 0, 0, 1024)
    rs_open(U_1, 0, 2)
    f1_sum = column_sum(GF, 0, 1024)
    for t in range(8):
        SM_OUT[pl.ds(ROW_F1B + 4 * t + q, 1), :] = f1_sum[:, 128 * t : 128 * t + 128]
    o_x = reduce_x(FP, GNVR, got_o, OX, OXR)

    def out_one(i, carry):
        OB[rows_of(i, 32), :] = pair_sum(FP, GNVR, i)
        return carry

    lax.fori_loop(0, 4, out_one, 0)
    rs_pass_y(U_2, 0, 1)

    a_x[1].wait_recv()
    zero8 = jnp.zeros((8, 1024), F32)
    sums = lax.fori_loop(0, 4, back_two, (zero8, zero8, zero8, zero8))
    _, got_gh = exchange(GH.at[own], GH.at[own], C, GH.at[theirs])
    _, got_gu = exchange(GUS.at[:, their_cols], GBS.at[own, 0:512], C, GBS.at[theirs, 0:512])
    GBS[own, 0:512] = GUS[:, my_cols]
    for row, acc in zip((ROW_N2G, ROW_N2B, ROW_PB, ROW_F2B), sums):
        store_row(row, jnp.sum(acc, axis=0, keepdims=True))
    rs_pass_y(U_2, 1, 2)

    got_gh.wait_recv()
    got_gu.wait_recv()
    GBS[:, 512:1024] = GH[:, my_cols]
    weight_grad(ML, GBS, GBA, 0, 0, 1024)
    o_x[1].wait_recv()
    rs_open(U_BA)
    for n in range(2):
        cols = slice(512 * n, 512 * n + 512)
        gg = dot_nt(GH[...], WP[cols, :])
        pre = RP[:, cols].astype(F32)
        logistic = sig(pre)
        GA[:, cols] = (gg * (pre * logistic)).astype(BF)
        GBS[:, 1152 + 512 * n : 1664 + 512 * n] = (
            gg * AD[:, cols].astype(F32) * (logistic * (1.0 + pre * (1.0 - logistic)))
        ).astype(BF)
    for i in range(2):
        rows = slice(128 * i, 128 * i + 128)
        GAT[rows, :] = dot_nt(GA[rows, :], VL[rows, :])
    _, got_gat = exchange(GAT, GATR, C)
    weight_grad(GT, GH, FG, 0, 0, 1024)
    for i in range(2):
        rows = slice(128 * i, 128 * i + 128)
        low = AT[rows, :].astype(BF)
        for n in range(2):
            cols = slice(512 * n, 512 * n + 512)
            gv = dot_tn(low, GA[rows, cols])
            GVP[rows, cols] = (gv * slope(VP[rows, cols].astype(F32))).astype(BF)
    got_gat.wait_recv()
    for i in range(2):
        rows = slice(128 * i, 128 * i + 128)
        attn = AT[rows, :]
        gat = GAT[rows, :] + GATR[rows, :]
        gs = (attn * (gat - jnp.sum(gat * attn, axis=-1, keepdims=True))).astype(BF)
        qs, ks = queries_keys(i)
        gq = dot_nn(gs, ks) * SCALE
        gk = dot_tn(gs, qs) * SCALE
        pre = SHP[rows, :]
        sh = silu(pre)
        gsp = (gq * sg[0:1, :] + gk * sg[1:2, :]) * slope(pre)
        GBS[rows, 1024:1152] = (gsp * 0.5).astype(BF)
        mine = b == i

        @pl.when(mine)
        def _(gs=gs, gq=gq, gk=gk, sh=sh):
            SM_OUT[ROW_SG : ROW_SG + 1, :] = jnp.sum(gq * sh, axis=0, keepdims=True)
            SM_OUT[ROW_SG + 1 : ROW_SG + 2, :] = jnp.sum(gk * sh, axis=0, keepdims=True)
            SM_OUT[ROW_QO : ROW_QO + 1, :] = jnp.sum(gq, axis=0, keepdims=True)
            SM_OUT[ROW_POS : ROW_POS + 1, :] = jnp.sum(
                shear(jnp.transpose(gs.astype(F32)), True), axis=0, keepdims=True
            )

    GM = FP.at[0:256]
    GNV = FP.at[256:512]
    for copy, _ in got_o:
        copy.wait_send()
        settle(copy)
    for n in range(2):
        cols = slice(512 * n, 512 * n + 512)
        GM[:, cols] = dot_nt(GBS[...], WB[cols, :])
    _, got_gm = exchange(GM.at[theirs], GNVR.at[0:128], C)
    for n in range(2):
        cols = slice(512 * n, 512 * n + 512)
        GNV[:, cols] = dot_nt(GVP[...], WV[cols, :])
    _, got_gnv = exchange(GNV.at[theirs], GNVR.at[128:256], C)
    GBS[:, 1024:1152] = (GBS[:, 1024:1152].astype(F32) * 2.0).astype(BF)
    rs_pass_y(U_2, 2)

    def grad_ema_one(i, carry):
        for g in range(8):
            cols = slice(128 * g, 128 * g + 128)
            rows = pl.ds(al(128 * g + 32 * i, 32), 32)
            v = GM[pl.ds(al(128 * b + 32 * i, 32), 32), cols] + GNVR[rows_of(i, 32), cols]
            GEP[rows, :] = v * slope(YP[rows, :])
        return carry

    def adjoint_end():
        d = [DEC[j] for j in range(NDIM)]

        def step(i, g):
            row = GEP[panel(BLK - 1 - i), :]
            return tuple(g[j] * d[j] + row for j in range(NDIM))

        g = lax.fori_loop(
            0, BLK, step, tuple(jnp.zeros((8, 128), F32) for _ in range(NDIM)), unroll=4
        )
        for j in range(NDIM):
            EC[3, j] = g[j]

    got_gm.wait_recv()
    lax.fori_loop(0, 4, grad_ema_one, 0)
    adjoint_end()
    _, got_bx = exchange(EC.at[3], BXX, X)
    rs_open(U_P)
    rs_pass_x(U_BA, 0, 2)
    got_bx.wait_recv()
    scan_round_x(EC.at[3], BXX, EC.at[4], PIN, x == 0)
    _, got_by = exchange(EC.at[4], BXY, Y)
    rs_open(U_1, 2)
    for copy in (copy_og_c, copy_og_x, copy_og_xc, copy_nt_x, copy_nt_c, copy_nt_xc):
        copy.wait_send()
        settle(copy)
    weight_grad(NL, GVP, NO, 0, 0, 1024)
    rs_pass_y(U_1, 0, 2)
    rs_pass_x(U_BA, 2)
    got_by.wait_recv()
    scan_round_y(EC.at[4], BXY, EC.at[5], PIN, y == 0, 1 - x)
    got_bz = [
        exchange(EC.at[5], BXZ.at[k - 1], (ahead(NZ - k), b))[1] for k in range(1, NZ)
    ]
    rs_open(U_V)
    weight_grad(ML, GBS, GBB, 1024, 0, 1152)
    rs_open(U_BB, 0, 2)
    base_sum = column_sum(GBS, 0, BASE_COLS)
    for t in range(4):
        cols = slice(128 * t, 128 * t + 128)
        SM_OUT[pl.ds(ROW_BB + 4 * b + t, 1), :] = base_sum[:, cols]
        SM_OUT[pl.ds(ROW_BB + 25 + 4 * b + t, 1), :] = base_sum[:, 512 + 128 * t : 640 + 128 * t]
    SM_OUT[ROW_BB + 8 : ROW_BB + 9, :] = base_sum[:, 1024:1152] * 0.5

    low_float = low_row.astype(F32)
    keep = pick(first, low_float, 1.0 - low_float)

    def store_half(row, v):
        for t in range(8):
            block = v[:, 128 * t : 128 * t + 128]
            turned = pltpu.roll(block, 64, 1)
            SM_OUT[row + 2 * t : row + 2 * t + 1, :] = keep * pick(first, block, turned)
            SM_OUT[row + 2 * t + 1 : row + 2 * t + 2, :] = keep * pick(first, turned, block)

    store_half(ROW_BB + 9, base_sum[:, 1152:2176])
    store_half(ROW_VB, column_sum(GVP, 0, 1024))

    def block_out_one(i, carry):
        rows = rows_of(i, 32)
        o_block[rows, :] = (
            FO[rows, :] + ((OB[rows, :] + OXR[rows, :].astype(F32)) + f2b[...])
        ).astype(BF)
        return carry

    lax.fori_loop(0, 4, block_out_one, 0)
    rs_pass_y(U_BA, 0, 2)
    for got in got_bz:
        got.wait_recv()
    scan_round_z(BXZ, PIN, NZ - 1 - z, 2 * (1 - y) + 1 - x)
    rs_pass_y(U_1, 2)
    def backward_scan():
        for part in range(2):
            js = range(8 * part, 8 * part + 8)
            d = [DEC[j] for j in js]
            c = [CIN[j] for j in js]
            e = [EMA_SCALE * CIN[j] * ema[3, j] for j in js]

            def group(i, carry):
                at = 15 - i
                h = tuple(HC[at, j] for j in js)
                for u in range(8):
                    for n in range(8):
                        H8[u, n] = h[n]
                    if u < 7:
                        row = XP[panel(8 * at + u), :]
                        h = tuple(h[n] * d[n] + c[n] * row for n in range(8))
                g, s1, m = carry
                for u in range(7, -1, -1):
                    t = 8 * at + u
                    row = XP[panel(t), :]
                    ge = GEP[panel(t), :]
                    g = tuple(g[n] * d[n] + ge for n in range(8))
                    s1 = tuple(s1[n] + row * g[n] for n in range(8))
                    m = tuple(m[n] + g[n] * H8[u, n] for n in range(8))
                    out = e[0] * g[0]
                    for n in range(1, 8):
                        out = out + e[n] * g[n]
                    if part == 0:
                        out = out + om[...] * ge
                    else:
                        out = out + GNP[panel(t), :]
                    GNP[panel(t), :] = out
                return g, s1, m

            zeros = tuple(jnp.zeros((8, 128), F32) for _ in range(8))
            _, s1, m = lax.fori_loop(0, 16, group, (tuple(PIN[j] for j in js), zeros, zeros))
            for n, j in enumerate(js):
                SM_OUT[8 * j : 8 * j + 8, :] = s1[n]
                SM_OUT[128 + 8 * j : 128 + 8 * j + 8, :] = m[n]

    backward_scan()
    rs_pass_y(U_BA, 2)
    rs_pass_x(U_P, 0, 2)

    for g in range(8):
        rows = slice(128 * g, 128 * g + 128)
        SM_OUT[ROW_OMEGA + g : ROW_OMEGA + g + 1, :] = jnp.sum(
            fold8(XP[rows, :] * GEP[rows, :]), axis=0, keepdims=True
        )

    got_gnv.wait_recv()

    def back_one(i, carry):
        rows = rows_of(i, 32)
        wide = jnp.concatenate(
            [GNP[pl.ds(al(128 * g + 32 * i, 32), 32), :] for g in range(8)], axis=1
        )
        a = (GNV[pl.ds(al(128 * b + 32 * i, 32), 32), :] + GNVR[pl.ds(al(128 + 32 * i, 32), 32), :]) + wide
        n, rstd = norm_rows(tok[rows, :].astype(F32))
        g = a * n1g[...]
        back = (
            g - jnp.mean(g, axis=-1, keepdims=True) - n * jnp.mean(g * n, axis=-1, keepdims=True)
        ) * rstd
        o_tok[rows, :] = (PR[rows, :] + back).astype(BF)
        return carry[0] + fold8(a * n), carry[1] + fold8(a)

    sums = lax.fori_loop(0, 4, back_one, (zero8, zero8))
    for row, acc in zip((ROW_N1G, ROW_N1B), sums):
        store_row(row, jnp.sum(acc, axis=0, keepdims=True))

    half_rows = SM_ROWS // 2
    my_part = rows_of(b, half_rows)
    their_part = rows_of(1 - b, half_rows)
    copy_c, got_c = exchange(SM_OUT.at[their_part], SMR, C)
    rs_pass_x(U_P, 2)
    got_c.wait_recv()
    SMX[0] = SM_OUT[my_part, :] + SMR[...]
    _, got_sx = exchange(SMX.at[0], SMX.at[1], X)
    rs_open(U_BB, 2)
    rs_pass_y(U_P, 0, 2)
    rs_pass_x(U_BB, 0, 2)
    got_sx.wait_recv()
    SMY[0] = SMX[0] + SMX[1]
    _, got_sy = exchange(SMY.at[0], SMY.at[1], Y)
    rs_pass_x(U_V)
    rs_pass_y(U_P, 2)
    rs_pass_x(U_BB, 2)
    got_sy.wait_recv()
    SMZ[0] = SMY[0] + SMY[1]
    got_sz = [exchange(SMZ.at[0], SMZ.at[k], (ahead(k), b))[1] for k in range(1, NZ)]
    rs_wait_z(U_2)
    for i in range(4):
        o_d2[32 * i : 32 * i + 32, :] = rs_total(U_2, (32 * i, 32))
    rs_wait_z(U_1)
    for i in range(4):
        o_d1[:, 1024 * i : 1024 * i + 1024] = rs_total(U_1, (32 * i, 32))
    quarter = lambda j: pl.ds(al(1024 * j, 1024), 1024)
    d1_pairs = [
        exchange(o_d1.at[:, quarter(j)], FX1.at[q], device, FX1.at[j])
        for j, device in ((q_c, C), (q_x, X), (q_xc, XC))
    ]
    mine32 = 32 * b
    their32 = 32 * (1 - b)
    h_mine = pl.ds(al(3200 + 512 * b, 128), 512)
    h_their = pl.ds(al(3200 + 512 * (1 - b), 128), 512)
    low = low1(32)

    def merge(out, start, own_half, other_half):
        for t in range(8):
            cols = slice(128 * t, 128 * t + 128)
            m, o = own_half[:, cols], other_half[:, cols]
            lo, hi = pick(first, m, o), pick(first, o, m)
            at = start + 256 * t
            out[:, at : at + 128] = jnp.where(low, lo, pltpu.roll(hi, 64, 1))
            out[:, at + 128 : at + 256] = jnp.where(low, pltpu.roll(lo, 64, 1), hi)

    rs_wait_z(U_BA)
    FB[:, 0:1024] = rs_total(U_BA, (their32, 32))
    _, got_ba = exchange(FB.at[:, 0:1024], FXB.at[:, 0:1024], C)
    part = rs_total(U_BA, (mine32, 32))
    o_db[:, my_cols] = part[:, 0:512]
    o_db[:, h_mine] = part[:, 512:1024]
    rs_pass_y(U_V)
    rs_pass_y(U_BB, 0, 2)
    for got in got_sz:
        got.wait_recv()
    total = SMZ[lax.rem(z, NZ)]
    for k in range(1, NZ):
        total = total + SMZ[lax.rem(z + NZ - k, NZ)]
    SM_OUT[my_part, :] = total
    _, got_cc = exchange(SM_OUT.at[my_part], SMC, C)

    rs_wait_z(U_P)
    for i in range(2):
        o_dp[32 * i : 32 * i + 32, :] = rs_total(U_P, (32 * i, 32))
    rs_pass_y(U_BB, 2)
    copy_c.wait_send()
    settle(copy_c)
    got_cc.wait_recv()
    SM_OUT[their_part, :] = SMC[...]
    for j in range(NDIM):
        rate, damping = sig(ema[0, j]), sig(ema[1, j])
        beta, gamma = ema[2, j], EMA_SCALE * ema[3, j]
        s1 = SM_OUT[8 * j : 8 * j + 8, :]
        m = gamma * SM_OUT[128 + 8 * j : 136 + 8 * j, :]
        o_ema[0, j] = (beta * gamma * s1 - damping * m) * rate * (1.0 - rate)
        o_ema[1, j] = -rate * m * damping * (1.0 - damping)
        o_ema[2, j] = gamma * rate * s1
        o_ema[3, j] = EMA_SCALE * rate * beta * s1

    o_sm[...] = SM_OUT[...]
    rs_wait_z(U_V)
    FV[...] = rs_total(U_V, (their32, 32))
    _, got_v = exchange(FV, FXV, C)
    part_v = rs_total(U_V, (mine32, 32))

    got_ba.wait_recv()
    o_db[:, their_cols] = FXB[:, 0:512]
    o_db[:, h_their] = FXB[:, 512:1024]
    FX1[q] = o_d1[:, quarter(q)]
    for copy, got in d1_pairs:
        copy.wait_send()
        settle(copy)
        got.wait_recv()
    for j in range(4):
        for t in range(8):
            o_d1[:, 128 * (4 * t + j) : 128 * (4 * t + j) + 128] = FX1[j, :, 128 * t : 128 * t + 128]

    rs_wait_z(U_BB)
    FB[:, 1024:2176] = rs_total(U_BB, (their32, 32))
    _, got_bb = exchange(FB.at[:, 1024:2176], FXB.at[:, 1024:2176], C)
    part = rs_total(U_BB, (mine32, 32))
    o_db[:, 1024:1152] = part[:, 0:128]
    got_bb.wait_recv()
    merge(o_db, 1152, part[:, 128:1152], FXB[:, 1152:2176])
    got_v.wait_recv()
    merge(o_dv, 0, part_v, FXV[...])

    for copy in open_sends:
        copy.wait_send()
    for w in (VALUE, BASE, PROJ):
        close_gather(w)

    def close_sums(u):
        def one(k, carry):
            rs_y(u, k).wait_send()
            if u < U_1:
                rs_x(u, k, 0).wait_send()
                rs_x(u, k, 1).wait_send()
            return carry

        lax.fori_loop(0, NZ, one, 0)

        def plane(k, carry):
            rs_z(u, k).wait_send()
            return carry

        lax.fori_loop(1, NZ, plane, 0)

    for u in (U_V, U_P, U_BA, U_BB, U_1, U_2):
        close_sums(u)


def hand_on_kernel(*refs):
    large, (ema, sums), outs = refs[:7], refs[7:9], refs[9:]
    for src, dst in zip(large, outs):
        dst[...] = src[...]
    for a in range(4):
        for g in range(8):
            outs[7 + a][:, 128 * g : 128 * g + 128] = ema[a, :, g, :]
    for out, (row, n) in zip(outs[11:], SMALL_ROWS):
        if out.shape[0] == 1:
            for g in range(n):
                out[:, 128 * g : 128 * g + 128] = sums[row + g : row + g + 1, :]
        else:
            out[...] = sums[row : row + n, :]


def fast_shards(
    tokens,
    out_grad,
    norm1_gain,
    norm1_bias,
    value_weight,
    value_bias,
    ema_delta,
    ema_alpha,
    ema_beta,
    ema_gamma,
    ema_omega,
    base_weight,
    base_bias,
    shared_gamma,
    query_offset,
    position_bias,
    proj_weight,
    proj_bias,
    norm2_gain,
    norm2_bias,
    ffn1_weight,
    ffn1_bias,
    ffn2_weight,
    ffn2_bias,
):
    NS = lax.axis_size("seq")
    NZ = NS // 4
    row = lambda v: v.reshape(1, -1)
    small = [
        tokens[0], out_grad[0], row(norm1_gain), row(norm1_bias), row(value_bias),
        ema_delta.T, ema_alpha.T, ema_beta.T, ema_gamma.T,
        row(ema_omega), row(base_bias), shared_gamma, row(query_offset),
        row(position_bias), row(proj_bias), row(norm2_gain), row(norm2_bias), row(ffn1_bias),
        row(ffn2_bias),
    ]
    large = [value_weight, base_weight, proj_weight, ffn1_weight, ffn2_weight]
    f = lambda *shape: jax.ShapeDtypeStruct(shape, F32)
    h = lambda *shape: jax.ShapeDtypeStruct(shape, BF)
    outs = [
        h(128, 1024), h(128, 1024), f(32, 2048), f(32, 4224), f(64, 1024), f(32, 4096), f(128, 1024),
        f(4, NDIM, 8, 128),
    ]
    outs.append(f(SM_ROWS, 128))
    vm = lambda *shape: pltpu.VMEM(shape, BF)
    vf = lambda *shape: pltpu.VMEM(shape, F32)
    dma = lambda *shape: pltpu.SemaphoreType.DMA(shape)
    scratch = [
        vf(SM_ROWS, 128), vf(4, NDIM, 8, 128), vf(8, 128),
        vm(1024, 1024), vm(1024, BASE_COLS), vm(1024, 1024), vm(1024, 1024), vm(1024, 1024),
        vm(1024, 1024), vm(1024, 1024), vm(1024, 1024), vm(1024, 1152), vm(512, 1152),
        vm(NZ, 64, 1024), vm(NZ, 64, 1024), vm(NZ, 64, 1024), vm(NZ, 64, 1152),
        vm(NZ, 128, 1024), vm(NZ, 128, 1024),
        vm(NZ - 1, 64, 1024), vm(NZ - 1, 64, 1024), vm(NZ - 1, 64, 1024), vm(NZ - 1, 64, 1152),
        vm(NZ - 1, 128, 1024), vm(NZ - 1, 128, 1024),
        vf(32, 1024), vf(32, BASE_COLS), vf(32, 1024), vf(32, BASE_COLS), vf(4, 32, 1024),
        vm(32, 1024), vm(32, BASE_COLS), vm(256, 1024), vm(256, 1024), vm(1024, 1024),
        vm(256, 1024), vm(256, 1024), vf(256, 1024), vf(128, 1024), vf(128, 1024), vf(256, 128),
        vm(256, 1024), vm(256, 1024), vm(256, 1024), vf(256, 128), vf(128, 1024), vf(128, 1024),
        vf(512, 1024), vm(1024, 1024),
        vm(512, 1024), vm(256, 1024), vm(128, 1024), vm(128, 1024), vm(128, 1024), vm(128, 1024), vf(128, 1024),
        vm(256, 1024), vm(128, 1024), vm(256, BASE_COLS), vm(256, 1024), vf(256, 128), vf(256, 128),
        vm(256, 1024), vf(256, 1024),
        vf(1024, 128), vf(1024, 128), vf(1024, 128), vf(1024, 128), vf(16, NDIM, 8, 128), vf(8, 8, 8, 128),
        vf(6, NDIM, 8, 128), vf(NDIM, 8, 128), vf(NDIM, 8, 128), vf(NZ - 1, NDIM, 8, 128),
        vf(NDIM, 8, 128), vf(NDIM, 8, 128), vf(NZ - 1, NDIM, 8, 128),
        vf(NDIM, 8, 128), vf(NDIM, 8, 128), vf(NDIM, 8, 128), vf(NDIM, 8, 128),
        vf(SM_ROWS // 2, 128), vf(2, SM_ROWS // 2, 128), vf(2, SM_ROWS // 2, 128),
        vf(NZ, SM_ROWS // 2, 128), vf(SM_ROWS // 2, 128),
        dma(5), dma(5, NZ, 2, 2), dma(5, NZ, 2), dma(5, NZ), dma(5, NZ), dma(3, 2, NZ), dma(3, 2, NZ),
        dma(4, NZ, 2), dma(4, NZ, 2), dma(6, NZ), dma(6, NZ), dma(6, NZ), dma(6, NZ), dma(64), dma(64),
    ]
    results = pl.pallas_call(
        functools.partial(layer_kernel, NS),
        out_shape=outs,
        in_specs=[pl.BlockSpec(memory_space=pltpu.VMEM)] * len(small)
        + [pl.BlockSpec(memory_space=pl.ANY)] * len(large),
        out_specs=[pl.BlockSpec(memory_space=pltpu.VMEM)] * len(outs),
        scratch_shapes=scratch,
        compiler_params=pltpu.CompilerParams(
            collective_id=0, has_side_effects=True, vmem_limit_bytes=VMEM_LIMIT
        ),
    )(*small, *large)
    final = list(outs[:7]) + [f(NDIM, D)] * 4
    final += [f(2, 128) if row == ROW_SG else f(1, 128 * n) for row, n in SMALL_ROWS]
    local = pl.BlockSpec(memory_space=pltpu.VMEM)
    (block_out, tokens_grad, dvalue, dbase, dproj, dffn1, dffn2, ddelta, dalpha, dbeta, dgamma, *sums) = (
        pl.pallas_call(
            hand_on_kernel,
            out_shape=final,
            in_specs=[local] * 9,
            out_specs=[local] * len(final),
        )(*results)
    )
    (dn1g, dn1b, dvb, dom, dbb, dsg, dqo, dpos, dpb, dn2g, dn2b, df1b, df2b) = [
        v if v.shape[0] == 2 else v.reshape(-1) for v in sums
    ]
    return (
        block_out[None],
        tokens_grad[None],
        dn1g,
        dn1b,
        dvalue,
        dvb,
        ddelta.T,
        dalpha.T,
        dbeta.T,
        dgamma.T,
        dom,
        dbase,
        dbb,
        dsg,
        dqo,
        dpos,
        dproj,
        dpb,
        dn2g,
        dn2b,
        dffn1,
        df1b,
        dffn2,
        df2b,
    )


def solution(mesh):
    in_specs = (
        P("batch", "seq", None),
        P("batch", "seq", None),
        P(),
        P(),
        P(("seq", "batch"), None),
        P(),
        P(),
        P(),
        P(),
        P(),
        P(),
        P(("seq", "batch"), None),
        P(),
        P(),
        P(),
        P(),
        P(("seq", "batch"), None),
        P(),
        P(),
        P(),
        P(("seq", "batch"), None),
        P(),
        P(("seq", "batch"), None),
        P(),
    )
    out_specs = (
        P("batch", "seq", None),
        P("batch", "seq", None),
        P(),
        P(),
        P(("seq", "batch"), None),
        P(),
        P(),
        P(),
        P(),
        P(),
        P(),
        P(("seq", "batch"), None),
        P(),
        P(),
        P(),
        P(),
        P(("seq", "batch"), None),
        P(),
        P(),
        P(),
        P(("seq", "batch"), None),
        P(),
        P(("seq", "batch"), None),
        P(),
    )
    one_device = fast_shards if mesh.shape['seq'] == 16 else shards
    return jax.shard_map(
        one_device, mesh=mesh, in_specs=in_specs, out_specs=out_specs, check_vma=False
    )
```
